32 devices in a mesh: blk: 8 (over z, x), uly: 4 (over y, core).
Axes of the slice: x: 2, y: 2, z: 4, core: 2. Of those that a mesh axis runs over, the one named last changes fastest.
Arguments:
- tokens: bfloat16 [2048, 2, 1536], P(('blk', 'uly')), may hold values from -6 to 6
- span_order: int32 [2, 16], replicated, may hold values from 0 to 15, as said below
- attn_gain: bfloat16 [1536], P(('blk', 'uly')), may hold values from 0.5 to 1.5
- qkv_weight: bfloat16 [1536, 2048], P(('blk', 'uly')), may hold values from -0.21875 to 0.21875
- qkv_bias: bfloat16 [2048], P(('blk', 'uly')), may hold values from -1.1953125 to 1.1953125
- out_weight: bfloat16 [1536, 1536], P(('blk', 'uly')), may hold values from -1 to 1
- ffn_gain: bfloat16 [1536], P('blk'), may hold values from 0.5 to 1.5
- gate_weight: bfloat16 [1536, 8960], P('blk', 'uly'), may hold values from -0.15625 to 0.15625
- up_weight: bfloat16 [1536, 8960], P('blk', 'uly'), may hold values from -0.15625 to 0.15625
- down_weight: bfloat16 [8960, 1536], P('uly', 'blk'), may hold values from -0.09375 to 0.09375
- cotangent: bfloat16 [2048, 2, 1536], P(('blk', 'uly')), may hold values from -6 to 6
Outputs:
- output: bfloat16 [2048, 2, 1536], P(('blk', 'uly'))
- grad_tokens: float32 [2048, 2, 1536], P(('blk', 'uly'))
- grad_attn_gain: float32 [1536], P(('blk', 'uly'))
- grad_qkv: float32 [1536, 2048], P(('blk', 'uly'))
- grad_bias: float32 [2048], P(('blk', 'uly'))
- grad_out_proj: float32 [1536, 1536], P(('blk', 'uly'))
- grad_ffn_gain: float32 [1536], P(('blk', 'uly'))
- grad_gate: float32 [1536, 8960], P('blk', 'uly')
- grad_up: float32 [1536, 8960], P('blk', 'uly')
- grad_down: float32 [8960, 1536], P('uly', 'blk')
The draws below stay inside these ranges and needn't reach their ends.
Inputs may be any that keep to these rules, and one draw needn't show every extreme that they name: Each row is a permutation: slot j of sequence s (its rows j * 128 to (j + 1) * 128 - 1) holds the tokens at positions span_order[s, j] * 128 onward, in order.
All inputs are finite; a program needn't handle non-finite values.
Results may differ from the reference program's by a relative error of at most 0.033.
Values may be sent and summed in bfloat16 or wider, within the bound.
No kernel may reach another device: no remote copies, remote signals or barrier semaphores. Data moves between devices by JAX's collectives and lax.ppermute only.
A program may use at most 512 MiB of HBM per device.

```python
import math
import jax
import jax.numpy as jnp
from jax import lax

D = 1536
HEADS = 12
KV_HEADS = 2
HEAD_DIM = 128
FF = 8960
SPAN = 128
SEQS = 2
SLOTS = 16
LEN = 2048
N_ULY = 4


def draw_span_order(key, part):
    key = jax.random.fold_in(key, 11)
    seq_keys = jax.random.split(key, SEQS)

    def shuffle(seq_key):
        return jax.random.permutation(seq_key, SLOTS)
    return jax.vmap(shuffle)(seq_keys).astype(jnp.int32)


def levels(rng, extent, shards, low, largest):
    def one(dim, blocks):
        steps = jax.random.uniform(jax.random.fold_in(jax.random.fold_in(rng, 6), dim), (blocks,), jnp.float32, low / len(shards), largest / len(shards))
        return jnp.repeat(jnp.exp(steps), extent[dim] // blocks).reshape((-1,) + (1,) * (len(extent) - dim - 1))

    loudness = one(*shards[0])
    for cut in shards[1:]:
        loudness = loudness * one(*cut)
    return loudness


def centred(stream_key, shape, scale, limit, cuts=(), kind=jnp.bfloat16):
    drawn = jax.random.normal(stream_key, shape, jnp.float32) * scale
    if len(cuts) > 0:
        drawn = levels(stream_key, shape, cuts, -0.22, 0.18) * drawn
    return jnp.clip(drawn, min=-limit, max=limit).astype(kind)


def setup_inputs(seed: int = 0) -> dict:
    streams_of = jax.random.split(jax.random.key(seed), 12)
    return {
        "tokens": centred(streams_of[0], (LEN, SEQS, D), 1.0, 6.0, ((0, 32),)),
        "span_order": draw_span_order(jax.random.fold_in(streams_of[11], 71), 0),
        "attn_gain": jnp.clip(1.0 + 0.1 * jax.random.normal(streams_of[2], (D,), jnp.float32), 0.5, 1.5).astype(jnp.bfloat16),
        "qkv_weight": centred(streams_of[3], (D, (HEADS + 2 * KV_HEADS) * HEAD_DIM), (D // 2) ** -0.5, 0.21875, ((0, 32),)),
        "qkv_bias": centred(streams_of[4], ((HEADS + 2 * KV_HEADS) * HEAD_DIM,), 0.2, 1.1953125, ((0, 32),)),
        "out_weight": centred(streams_of[5], (HEADS * HEAD_DIM, D), (D // 48) ** -0.5, 1.0, ((0, 32),)),
        "ffn_gain": jnp.clip(1.0 + 0.1 * jax.random.normal(streams_of[6], (D,), jnp.float32), 0.5, 1.5).astype(jnp.bfloat16),
        "gate_weight": centred(streams_of[7], (D, FF), D ** -0.5, 0.15625, ((0, 8), (1, 4))),
        "up_weight": centred(streams_of[8], (D, FF), D ** -0.5, 0.15625, ((0, 8), (1, 4))),
        "down_weight": centred(streams_of[9], (FF, D), (FF // 2) ** -0.5, 0.09375, ((0, 4), (1, 8))),
        "cotangent": centred(streams_of[10], (LEN, SEQS, D), 1.0, 6.0, ((0, 32),)),
    }


EPS = 1e-06
THETA = 1000000.0
FLOOR = -1e+30

@jax.custom_vjp
def low(v):
    return lax.optimization_barrier(v.astype(jnp.bfloat16)).astype(jnp.float32)

@jax.custom_vjp
def low_back(v):
    return v

def low_keep(v):
    return (low(v), None)

def low_pass(kept, grad):
    return (grad,)

def back_keep(v):
    return (v, None)

def back_low(kept, grad):
    return (low(grad),)
low.defvjp(low_keep, low_pass)
low_back.defvjp(back_keep, back_low)

def product(left, right):
    return jnp.dot(left, right, precision=lax.Precision.HIGHEST)

def norm_rows(rows, gain):
    factor = lax.rsqrt(lax.optimization_barrier(jnp.mean(rows * rows, axis=-1, keepdims=True)) + EPS)
    return rows * factor * gain

def rope_tables(places):
    index = jnp.arange(HEAD_DIM // 2).astype(jnp.float32)
    freq = THETA ** (-2.0 * index / HEAD_DIM)
    angle = places.astype(jnp.float32)[..., None] * freq
    angle = jnp.concatenate([angle, angle], axis=-1)
    return (jnp.cos(angle), jnp.sin(angle))

def rotate(field, cosine, sine):
    half = field.shape[-1] // 2
    turned = jnp.concatenate([-field[..., half:], field[..., :half]], axis=-1)
    return field * cosine + turned * sine

def token_positions(order):
    places = jnp.arange(LEN).astype(jnp.int32)
    picked = order[:, places // SPAN].astype(jnp.int32)
    return (picked * SPAN + places % SPAN).T.astype(jnp.int32)

def attend_sequence(query, keys, values, places):
    group = HEADS // N_ULY
    key_heads = jnp.repeat(keys, group, axis=1)
    value_heads = jnp.repeat(values, group, axis=1)
    block = math.gcd(LEN, 512)
    factor = 1.0 / math.sqrt(HEAD_DIM)

    def one_block(pieces):
        rows, row_places = pieces
        scores = jnp.einsum('qhd,khd->hqk', rows, key_heads, precision=lax.Precision.HIGHEST) * factor
        scores = jnp.where(places[None, None, :] <= row_places[None, :, None], scores, FLOOR)
        probs = jax.nn.softmax(low_back(scores), axis=-1)
        return jnp.einsum('hqk,khd->qhd', low(probs), value_heads, precision=lax.Precision.HIGHEST)
    result = lax.map(jax.checkpoint(one_block), (query.reshape(LEN // block, block, HEADS, HEAD_DIM), places.reshape(LEN // block, block)))
    return result.reshape(LEN, HEADS, HEAD_DIM)

def layer(order, tokens, attn_gain, qkv_weight, qkv_bias, out_weight, ffn_gain, gate_weight, up_weight, down_weight):
    rows = tokens.reshape(LEN * SEQS, D)
    normed = low(norm_rows(rows, attn_gain))
    mixed = low_back(product(normed, qkv_weight) + qkv_bias).reshape(LEN, SEQS, -1)
    width = HEADS * HEAD_DIM
    side = KV_HEADS * HEAD_DIM
    query = mixed[..., :width].reshape(LEN, SEQS, HEADS, HEAD_DIM)
    keys = mixed[..., width:width + side].reshape(LEN, SEQS, KV_HEADS, HEAD_DIM)
    values = mixed[..., width + side:].reshape(LEN, SEQS, KV_HEADS, HEAD_DIM)
    places = token_positions(order)
    cosine, sine = rope_tables(places)
    cosine = cosine[:, :, None, :]
    sine = sine[:, :, None, :]
    slot_heads = [u * (HEADS // N_ULY) // (HEADS // KV_HEADS) for u in range(N_ULY)]
    query = low(low_back(rotate(query, cosine, sine)))
    keys = low(low_back(rotate(keys, cosine, sine)[:, :, slot_heads]))
    values = low(low_back(values[:, :, slot_heads]))

    def per_sequence(pieces):
        return attend_sequence(pieces[0], pieces[1], pieces[2], pieces[3])
    attended = lax.map(per_sequence, (jnp.moveaxis(query, 1, 0), jnp.moveaxis(keys, 1, 0), jnp.moveaxis(values, 1, 0), places.T))
    attended = low(low_back(jnp.moveaxis(attended, 0, 1).reshape(LEN * SEQS, width)))
    hidden = rows + low_back(product(attended, out_weight))
    normed_mid = low(norm_rows(hidden, ffn_gain))
    gate = low_back(product(normed_mid, gate_weight))
    upper = low_back(product(normed_mid, up_weight))
    active = low(jax.nn.silu(gate) * upper)
    result = hidden + low_back(product(active, down_weight))
    return result.reshape(LEN, SEQS, D)

def reference(tokens, span_order, attn_gain, qkv_weight, qkv_bias, out_weight, ffn_gain, gate_weight, up_weight, down_weight, cotangent):
    floats = tuple((item.astype(jnp.float32) for item in (tokens, attn_gain, qkv_weight, qkv_bias, out_weight, ffn_gain, gate_weight, up_weight, down_weight)))

    def forward(*weights):
        return layer(span_order, *weights)
    result, pullback = jax.vjp(forward, *floats)
    grads = pullback(cotangent.astype(jnp.float32))
    return (result.astype(jnp.bfloat16), grads[0], grads[1], grads[2], grads[3], grads[4], grads[5], grads[6], grads[7], grads[8])
```

```python
import math

import jax
import jax.numpy as jnp
from jax import lax
from jax.sharding import PartitionSpec as P

HEADS = 12
KV_HEADS = 2
HEAD_DIM = 128
SPAN = 128
PAIR = 2


EPS = 1e-06
THETA = 1000000.0
FLOOR = -1e30
BF16 = jnp.bfloat16
F32 = jnp.float32


def norm_rows(rows):
    factor = lax.rsqrt(jnp.mean(rows * rows, axis=-1, keepdims=True) + EPS)
    return (rows * factor, factor)


def norm_back(scaled, unit, factor):
    return factor * (scaled - unit * jnp.mean(scaled * unit, axis=-1, keepdims=True))


def matmul(left, right):
    return jnp.dot(left, right, preferred_element_type=F32)


def contract_rows(left, right):
    return lax.dot_general(left, right, (((0,), (0,)), ((), ())), preferred_element_type=F32)


def contract_cols(left, right):
    return lax.dot_general(left, right, (((1,), (1,)), ((), ())), preferred_element_type=F32)


def positions(order, rows):
    table = jnp.arange(order.shape[1], dtype=jnp.int32)
    slots = rows // SPAN
    picked = jnp.where(slots[None, :, None] == table[None, None, :], order[:, None, :], 0)
    return jnp.sum(picked, axis=-1) * SPAN + (rows % SPAN)[None, :]


def rope_tables(places):
    index = jnp.arange(HEAD_DIM // 2).astype(F32)
    freq = THETA ** (-2.0 * index / HEAD_DIM)
    angle = places.astype(F32)[..., None] * freq
    angle = jnp.concatenate([angle, angle], axis=-1)
    return (jnp.cos(angle), jnp.sin(angle))


def rotate(field, cosine, sine):
    half = field.shape[-1] // 2
    turned = jnp.concatenate([-field[..., half:], field[..., :half]], axis=-1)
    return field * cosine + turned * sine


def unrotate(grad, cosine, sine):
    half = grad.shape[-1] // 2
    moved = grad * sine
    return grad * cosine + jnp.concatenate([moved[..., half:], -moved[..., :half]], axis=-1)


class Grid:
    def __init__(self):
        self.blocks = lax.axis_size("blk")
        self.ulys = lax.axis_size("uly")
        self.depth = self.blocks // PAIR
        self.b = lax.axis_index("blk")
        self.u = lax.axis_index("uly")
        self.z = self.b // PAIR
        self.x = self.b % PAIR
        self.y = self.u // 2
        self.c = self.u % 2

    def to_z(self, value, step):
        pairs = [
            (z * PAIR + x, ((z + step) % self.depth) * PAIR + x)
            for z in range(self.depth)
            for x in range(PAIR)
        ]
        return lax.ppermute(value, "blk", pairs)

    def swap_x(self, value):
        return lax.ppermute(value, "blk", [(i, i ^ 1) for i in range(self.blocks)])

    def swap_y(self, value):
        return lax.ppermute(value, "uly", [(i, i ^ 2) for i in range(self.ulys)])

    def swap_core(self, value):
        return lax.ppermute(value, "uly", [(i, i ^ 1) for i in range(self.ulys)])


def paired(bit, mine, other, axis):
    low = jnp.where(bit == 0, mine, other)
    high = jnp.where(bit == 0, other, mine)
    return jnp.stack([low, high], axis=axis)


def pick(bit, array, axis):
    low = lax.index_in_dim(array, 0, axis, keepdims=False)
    high = lax.index_in_dim(array, 1, axis, keepdims=False)
    return jnp.where(bit == 0, low, high), jnp.where(bit == 0, high, low)


def order_z(grid, pieces):
    stacked = jnp.stack(pieces[::-1] + pieces[::-1][:-1])
    start = (grid.depth - 1 - grid.z) % grid.depth
    return lax.dynamic_slice_in_dim(stacked, start, grid.depth, 0)


def gather_uly(grid, value):
    both = paired(grid.y, value, grid.swap_y(value), 0)
    every = paired(grid.c, both, grid.swap_core(both), 1)
    return every.reshape((grid.ulys,) + value.shape)


def scatter_uly(grid, parts, kind=BF16):
    parts = parts.reshape((2, 2) + parts.shape[1:])
    keep, send = pick(grid.c, parts, 1)
    both = keep.astype(F32) + grid.swap_core(send.astype(kind)).astype(F32)
    keep, send = pick(grid.y, both, 0)
    return keep + grid.swap_y(send.astype(kind)).astype(F32)


def gather_blk(grid, value):
    pieces = [value] + [grid.to_z(value, d) for d in range(1, grid.depth)]
    pairs = [paired(grid.x, piece, grid.swap_x(piece), 0) for piece in pieces]
    return order_z(grid, pairs)


def exchange_z(grid, parts):
    pieces = [lax.dynamic_index_in_dim(parts, grid.z, 0, keepdims=False)]
    for d in range(1, grid.depth):
        there = (grid.z + d) % grid.depth
        pieces.append(grid.to_z(lax.dynamic_index_in_dim(parts, there, 0, keepdims=False), d))
    return pieces


def scatter_blk(grid, parts):
    keep, send = pick(grid.x, parts, 1)
    both = keep.astype(F32) + grid.swap_x(send.astype(BF16)).astype(F32)
    pieces = exchange_z(grid, both.astype(BF16))
    return sum(piece.astype(F32) for piece in pieces)


def exchange_uly(parts):
    return lax.all_to_all(parts, "uly", split_axis=0, concat_axis=0, tiled=True)


def per_device(
    tokens,
    span_order,
    attn_gain,
    qkv_weight,
    qkv_bias,
    out_weight,
    ffn_gain,
    gate_weight,
    up_weight,
    down_weight,
    cotangent,
):
    grid = Grid()
    local_rows, seqs, model = tokens.shape
    count = local_rows * seqs
    ulys = grid.ulys
    depth = grid.depth
    cycle_rows = local_rows * ulys
    group = HEADS // ulys
    factor = 1.0 / math.sqrt(HEAD_DIM)
    width = group * HEAD_DIM
    columns = width + HEAD_DIM
    shard = qkv_weight.shape[0]
    cycle_start = grid.b * cycle_rows
    head_rows = cycle_start + jnp.arange(cycle_rows, dtype=jnp.int32)
    query_places = positions(span_order, head_rows)

    gain_one = attn_gain.astype(F32)[:, None]
    scaled = (qkv_weight.astype(F32) * gain_one).astype(BF16)
    side = HEADS * HEAD_DIM

    def by_uly(array):
        lead = array.shape[0]
        heads = array[:, :side].reshape(lead, ulys, width)
        kinds = array[:, side:].reshape(lead, 2, KV_HEADS, HEAD_DIM)
        kinds = jnp.transpose(kinds, (0, 2, 1, 3)).reshape(lead, ulys, HEAD_DIM)
        return jnp.transpose(jnp.concatenate([heads, kinds], axis=-1), (1, 0, 2))

    def from_uly(array):
        lead = array.shape[1]
        heads = jnp.transpose(array[..., :width], (1, 0, 2)).reshape(lead, side)
        kinds = array[..., width:].reshape(KV_HEADS, 2, lead, HEAD_DIM)
        kinds = jnp.transpose(kinds, (2, 1, 0, 3)).reshape(lead, 2 * KV_HEADS * HEAD_DIM)
        return jnp.concatenate([heads, kinds], axis=-1)

    block_rows = exchange_uly(by_uly(scaled)).reshape(ulys * shard, columns)
    qkv_part = gather_blk(grid, block_rows).reshape(model, columns)
    bias_full = lax.all_gather(qkv_bias, ("blk", "uly"), axis=0, tiled=True)
    bias = lax.dynamic_index_in_dim(by_uly(bias_full[None]), grid.u, 0, keepdims=False)

    rows = tokens.astype(F32).reshape(count, model)
    unit_one, factor_one = norm_rows(rows)
    units = gather_uly(grid, unit_one.astype(BF16)).reshape(ulys * count, model)
    mixed = (matmul(units, qkv_part) + bias.astype(F32)).reshape(cycle_rows, seqs, columns)

    cosine, sine = rope_tables(query_places.T)
    cosine = cosine[:, :, None, :]
    sine = sine[:, :, None, :]
    query = rotate(
        mixed[..., :width].reshape(cycle_rows, seqs, group, HEAD_DIM), cosine, sine
    ).astype(BF16)
    is_key = grid.c == 0
    kind_cosine = jnp.where(is_key, cosine, 1.0)
    kind_sine = jnp.where(is_key, sine, 0.0)
    kind = rotate(mixed[:, :, None, width:], kind_cosine, kind_sine)[:, :, 0].astype(BF16)
    kinds = gather_blk(grid, kind).reshape(grid.blocks * cycle_rows, seqs, HEAD_DIM)
    pairs_all = paired(grid.c, kinds, grid.swap_core(kinds), 2)
    query_t = jnp.transpose(query, (1, 2, 0, 3))
    total_rows = pairs_all.shape[0]
    size = math.gcd(total_rows, 4 * SPAN)

    out_rows = gather_blk(grid, out_weight).reshape(ulys, grid.blocks // ulys, shard, model)
    out_part = jnp.transpose(exchange_uly(out_rows), (1, 0, 2, 3)).reshape(width, model)

    gain_two = ffn_gain.astype(F32)[:, None]
    hidden_units = gate_weight.shape[1] // depth

    def by_z(array):
        return jnp.transpose(array.reshape(array.shape[0], depth, hidden_units), (1, 0, 2))

    tiles = jnp.stack(
        [
            by_z((gate_weight.astype(F32) * gain_two).astype(BF16)),
            by_z((up_weight.astype(F32) * gain_two).astype(BF16)),
            by_z(down_weight.T),
        ],
        axis=1,
    )
    tile_pieces = exchange_z(grid, tiles)
    tile_pairs = [paired(grid.x, piece, grid.swap_x(piece), 0) for piece in tile_pieces]
    ffn_weights = order_z(grid, tile_pairs)
    ffn_weights = jnp.transpose(ffn_weights, (2, 0, 1, 3, 4)).reshape(3, model, hidden_units)
    gate_used, upper_used, down_used = ffn_weights[0], ffn_weights[1], ffn_weights[2]

    def spread(value):
        chunks = []
        for d in range(depth):
            piece = value if d == 0 else grid.to_z(value, d)
            both = jnp.concatenate([piece, grid.swap_y(piece)], axis=0)
            chunks.append(jnp.concatenate([both, grid.swap_core(both)], axis=0))
        return chunks

    def collect(chunks):
        total = None
        for d, chunk in enumerate(chunks):
            chunk = chunk.reshape(2, 2, count, model)
            both = chunk[0].astype(F32) + grid.swap_core(chunk[1].astype(BF16)).astype(F32)
            part = both[0] + grid.swap_y(both[1].astype(BF16)).astype(F32)
            if d > 0:
                part = grid.to_z(part.astype(BF16), -d).astype(F32)
            total = part if total is None else total + part
        return total

    cot_flat = cotangent.reshape(count, model)
    cot_chunks = spread(cot_flat)

    def forward_step(state, index):
        summed, peak, weight_sum = state
        offset = index * size
        block = lax.dynamic_slice_in_dim(pairs_all, offset, size, 0)
        key_places = positions(span_order, offset + jnp.arange(size, dtype=jnp.int32))
        scores = (
            jnp.einsum("shrd,ksd->shrk", query_t, block[:, :, 0], preferred_element_type=F32)
            * factor
        )
        allowed = key_places[:, None, None, :] <= query_places[:, None, :, None]
        scores = jnp.where(allowed, scores, FLOOR)
        new_peak = jnp.maximum(peak, jnp.max(scores, axis=-1))
        weights = jnp.where(allowed, jnp.exp(scores - new_peak[..., None]), 0.0)
        fade = jnp.exp(peak - new_peak)
        weight_sum = weight_sum * fade + jnp.sum(weights, axis=-1)
        summed = summed * fade[..., None] + jnp.einsum(
            "shrk,ksd->shrd",
            weights.astype(BF16),
            block[:, :, 1],
            preferred_element_type=F32,
        )
        return ((summed, new_peak, weight_sum), None)

    initial = (
        jnp.zeros((seqs, group, cycle_rows, HEAD_DIM), F32),
        jnp.full((seqs, group, cycle_rows), FLOOR, F32),
        jnp.zeros((seqs, group, cycle_rows), F32),
    )
    (summed, peak, weight_sum), unused = lax.scan(
        forward_step, initial, jnp.arange(total_rows // size, dtype=jnp.int32)
    )
    log_total = peak + jnp.log(weight_sum)
    result_t = (summed / weight_sum[..., None]).astype(BF16)
    attended = jnp.transpose(result_t, (2, 0, 1, 3)).reshape(cycle_rows * seqs, width)
    projected = matmul(attended, out_part).reshape(ulys, count, model)
    hidden = rows + scatter_uly(grid, projected)

    unit_two, factor_two = norm_rows(hidden)
    grad_rows = cotangent.astype(F32).reshape(count, model)
    mid_chunks = spread(unit_two.astype(BF16))

    actives, gate_grads, upper_grads, back_chunks = [], [], [], []
    for mid, cot in zip(mid_chunks, cot_chunks):
        gate = matmul(mid, gate_used)
        upper = matmul(mid, upper_used)
        sigmoid = jax.nn.sigmoid(gate)
        active_grad = matmul(cot, down_used)
        actives.append((gate * sigmoid * upper).astype(BF16))
        gate_grad = (active_grad * upper * sigmoid * (1.0 + gate * (1.0 - sigmoid))).astype(BF16)
        upper_grad = (active_grad * gate * sigmoid).astype(BF16)
        gate_grads.append(gate_grad)
        upper_grads.append(upper_grad)
        back_chunks.append(contract_cols(gate_grad, gate_used) + contract_cols(upper_grad, upper_used))
    mid_grad = collect(back_chunks)
    out_chunks = [contract_cols(active, down_used) for active in actives]
    result = hidden + collect(out_chunks)
    output = result.astype(BF16).reshape(local_rows, seqs, model)

    mid_all = jnp.concatenate(mid_chunks)
    cot_all = jnp.concatenate(cot_chunks)
    shares = jnp.stack(
        [
            contract_rows(mid_all, jnp.concatenate(gate_grads)).astype(BF16),
            contract_rows(mid_all, jnp.concatenate(upper_grads)).astype(BF16),
            contract_rows(cot_all, jnp.concatenate(actives)).astype(BF16),
        ]
    ).reshape(3, depth, PAIR, model // grid.blocks, hidden_units)
    keep, send = pick(grid.x, shares, 2)
    both = keep.astype(F32) + grid.swap_x(send).astype(F32)
    both = jnp.transpose(both, (1, 0, 2, 3)).astype(BF16)
    owned = order_z(grid, exchange_z(grid, both)).astype(F32)
    owned = jnp.transpose(owned, (1, 2, 0, 3)).reshape(3, model // grid.blocks, -1)
    grad_gate = owned[0] * gain_two
    grad_upper = owned[1] * gain_two
    grad_down = owned[2].T
    gain_part = jnp.sum(
        owned[0] * gate_weight.astype(F32) + owned[1] * up_weight.astype(F32), axis=-1
    )
    grad_gain_two = scatter_uly(grid, gain_part.reshape(ulys, -1), F32)

    hidden_grad = grad_rows + norm_back(mid_grad, unit_two, factor_two)
    branch_one = gather_uly(grid, hidden_grad.astype(BF16)).reshape(ulys * count, model)
    grad_heads = (
        contract_cols(branch_one, out_part)
        .astype(BF16)
        .reshape(cycle_rows, seqs, group, HEAD_DIM)
    )
    out_share = contract_rows(attended, branch_one).astype(BF16)
    out_share = out_share.reshape(grid.blocks // ulys, ulys, shard, model)
    out_share = exchange_uly(jnp.transpose(out_share, (1, 0, 2, 3)))
    grad_out = scatter_blk(grid, out_share.reshape(depth, PAIR, shard, model))

    grad_t = jnp.transpose(grad_heads, (1, 2, 0, 3))
    delta = jnp.sum(grad_t.astype(F32) * result_t.astype(F32), axis=-1)

    def backward_step(query_grad, index):
        offset = index * size
        block = lax.dynamic_slice_in_dim(pairs_all, offset, size, 0)
        key_places = positions(span_order, offset + jnp.arange(size, dtype=jnp.int32))
        scores = (
            jnp.einsum("shrd,ksd->shrk", query_t, block[:, :, 0], preferred_element_type=F32)
            * factor
        )
        allowed = key_places[:, None, None, :] <= query_places[:, None, :, None]
        probs = jnp.where(allowed, jnp.exp(scores - log_total[..., None]), 0.0)
        prob_grad = jnp.einsum(
            "shrd,ksd->shrk", grad_t, block[:, :, 1], preferred_element_type=F32
        )
        score_grad = (probs * (prob_grad - delta[..., None])).astype(BF16)
        query_grad = (
            query_grad
            + jnp.einsum("shrk,ksd->shrd", score_grad, block[:, :, 0], preferred_element_type=F32)
            * factor
        )
        key_grad = (
            jnp.einsum("shrk,shrd->ksd", score_grad, query_t, preferred_element_type=F32) * factor
        )
        value_grad = jnp.einsum(
            "shrk,shrd->ksd", probs.astype(BF16), grad_t, preferred_element_type=F32
        )
        return (query_grad, jnp.stack([key_grad, value_grad], axis=0))

    query_grad_t, terms = lax.scan(
        backward_step,
        jnp.zeros((seqs, group, cycle_rows, HEAD_DIM), F32),
        jnp.arange(total_rows // size, dtype=jnp.int32),
    )
    terms = jnp.transpose(terms, (1, 0, 2, 3, 4)).reshape(2, total_rows, seqs, HEAD_DIM)
    keep, send = pick(grid.c, terms, 0)
    kind_terms = keep + grid.swap_core(send.astype(BF16)).astype(F32)
    kind_terms = kind_terms.astype(BF16).reshape(depth, PAIR, cycle_rows, seqs, HEAD_DIM)
    kind_grad = scatter_blk(grid, kind_terms)
    kind_grad = unrotate(kind_grad[:, :, None, :], kind_cosine, kind_sine)
    query_grad = jnp.transpose(query_grad_t, (2, 0, 1, 3)).astype(BF16).astype(F32)
    query_grad = unrotate(query_grad, cosine, sine)
    mixed_grad = jnp.concatenate([query_grad, kind_grad], axis=2)
    mixed_grad = mixed_grad.reshape(cycle_rows * seqs, columns).astype(BF16)
    bias_part = lax.psum(jnp.sum(mixed_grad.astype(F32), axis=0), "blk")
    bias_all = lax.all_gather(bias_part, "uly", axis=0)
    bias_all = from_uly(bias_all[:, None, :])[0]
    owned_columns = qkv_bias.shape[0]
    grad_bias = lax.dynamic_slice_in_dim(
        bias_all, (grid.b * ulys + grid.u) * owned_columns, owned_columns, 0
    )
    normed_grad = contract_cols(mixed_grad, qkv_part).reshape(ulys, count, model)
    rows_part = norm_back(scatter_uly(grid, normed_grad), unit_one, factor_one)
    grad_tokens = (hidden_grad + rows_part).reshape(local_rows, seqs, model)
    qkv_share = contract_rows(units, mixed_grad).astype(BF16)
    qkv_share = scatter_blk(grid, qkv_share.reshape(depth, PAIR, ulys * shard, columns))
    qkv_share = exchange_uly(qkv_share.astype(BF16).reshape(ulys, shard, columns))
    qkv_share = from_uly(qkv_share).astype(F32)
    grad_qkv = qkv_share * gain_one
    grad_gain_one = jnp.sum(qkv_share * qkv_weight.astype(F32), axis=-1)
    return (
        output,
        grad_tokens,
        grad_gain_one,
        grad_qkv,
        grad_bias,
        grad_out,
        grad_gain_two.reshape(-1),
        grad_gate,
        grad_upper,
        grad_down,
    )


def solution(mesh):
    in_specs = (
        P(("blk", "uly"), None, None),
        P(),
        P(("blk", "uly")),
        P(("blk", "uly"), None),
        P(("blk", "uly")),
        P(("blk", "uly"), None),
        P("blk"),
        P("blk", "uly"),
        P("blk", "uly"),
        P("uly", "blk"),
        P(("blk", "uly"), None, None),
    )
    out_specs = (
        P(("blk", "uly"), None, None),
        P(("blk", "uly"), None, None),
        P(("blk", "uly")),
        P(("blk", "uly"), None),
        P(("blk", "uly")),
        P(("blk", "uly"), None),
        P(("blk", "uly")),
        P("blk", "uly"),
        P("blk", "uly"),
        P("uly", "blk"),
    )
    return jax.shard_map(
        per_device, mesh=mesh, in_specs=in_specs, out_specs=out_specs, check_vma=False
    )
```

```python
import functools
import math

import jax
import jax.numpy as jnp
from jax import lax
from jax.experimental import pallas as pl
from jax.experimental.pallas import tpu as pltpu
from jax.sharding import PartitionSpec as P

HEADS = 12
KV_HEADS = 2
HEAD_DIM = 128
SPAN = 128
PAIR = 2


EPS = 1e-06
THETA = 1000000.0
FLOOR = -1e30
LOG2E = 1.4426950408889634
BF16 = jnp.bfloat16
F32 = jnp.float32
SMALL = pl.CostEstimate(flops=1, transcendentals=0, bytes_accessed=1)
VMEM_LIMIT = 48 * 1024 * 1024

def norm_rows(rows):
    factor = lax.rsqrt(jnp.mean(rows * rows, axis=-1, keepdims=True) + EPS)
    return (rows * factor, factor)


def norm_back(scaled, unit, factor):
    return factor * (scaled - unit * jnp.mean(scaled * unit, axis=-1, keepdims=True))


def matmul(left, right):
    return jnp.dot(left, right, preferred_element_type=F32)


def contract_rows(left, right):
    return lax.dot_general(left, right, (((0,), (0,)), ((), ())), preferred_element_type=F32)


def contract_cols(left, right):
    return lax.dot_general(left, right, (((1,), (1,)), ((), ())), preferred_element_type=F32)


def positions(order, rows):
    table = jnp.arange(order.shape[1], dtype=jnp.int32)
    slots = rows // SPAN
    picked = jnp.where(slots[None, :, None] == table[None, None, :], order[:, None, :], 0)
    return jnp.sum(picked, axis=-1) * SPAN + (rows % SPAN)[None, :]


def rope_tables(places):
    index = jnp.arange(HEAD_DIM // 2).astype(F32)
    freq = THETA ** (-2.0 * index / HEAD_DIM)
    angle = places.astype(F32)[..., None] * freq
    cosine, sine = jnp.cos(angle), jnp.sin(angle)
    cosine = jnp.concatenate([cosine, cosine], axis=-1)
    return (cosine, jnp.concatenate([-sine, sine], axis=-1))


def dot_nn(left, right):
    return lax.dot_general(left, right, (((1,), (0,)), ((), ())), preferred_element_type=F32)


def dot_nt(left, right):
    return lax.dot_general(left, right, (((1,), (1,)), ((), ())), preferred_element_type=F32)


def dot_tn(left, right):
    return lax.dot_general(left, right, (((0,), (0,)), ((), ())), preferred_element_type=F32)


def call(kernel, scalars, arrays, outs, **options):
    return pl.pallas_call(
        kernel,
        grid_spec=pltpu.PrefetchScalarGridSpec(
            num_scalar_prefetch=len(scalars),
            grid=(1,),
            in_specs=[
                pl.BlockSpec(memory_space=pltpu.HBM) if i in options.get("far", ()) else whole(array.shape)
                for i, array in enumerate(arrays)
            ],
            out_specs=[whole(out.shape) for out in outs],
            scratch_shapes=options.get("scratch", ()),
        ),
        out_shape=outs,
        compiler_params=pltpu.CompilerParams(vmem_limit_bytes=VMEM_LIMIT),
        cost_estimate=SMALL,
    )(*scalars, *arrays)


def whole(shape):
    return pl.BlockSpec(shape, lambda *unused: (0,) * len(shape))


def turn(field):
    return pltpu.roll(field, HEAD_DIM // 2, 1)


AT_Z, AT_X, AT_Y, AT_C, AT_B, AT_U = range(6)


def mix_kernel(depth, group, place, own, near, across, cosine, sine, *rest):
    pieces, far = rest[:depth], rest[depth : 2 * depth]
    units, weights, query, kind, bias_rows, flags = rest[2 * depth :]
    u = place[AT_U]
    rows = weights.shape[1]
    copies = []

    def bring(source, target):
        copies.append(pltpu.make_async_copy(source, target, flags.at[len(copies)]))
        copies[-1].start()

    for d in range(depth):
        from_z = lax.rem(place[AT_Z] - d + depth, depth)
        for k in range(PAIR):
            piece = far[d] if k else pieces[d]
            from_x = place[AT_X] if k == 0 else 1 - place[AT_X]
            bring(piece.at[pl.ds(0, rows)], weights.at[from_z * PAIR + from_x])
            bring(piece.at[pl.ds(rows, 16)], bias_rows.at[PAIR * d + k])
    bring(own, units.at[u])
    bring(near, units.at[u ^ 2])
    bring(across.at[0], units.at[u ^ 1])
    bring(across.at[1], units.at[u ^ 3])
    for copy in copies:
        copy.wait()
    bias = jnp.sum(bias_rows[...].astype(F32), axis=(0, 1))[None]
    model = units.shape[2]
    all_weights = weights[...].reshape(model, weights.shape[2])
    is_key = place[AT_C] == 0
    for i in range(units.shape[0]):
        mixed = dot_nn(units[i], all_weights) + bias
        cos, sin = cosine[i], sine[i]
        for h in range(group):
            field = mixed[:, h * HEAD_DIM : (h + 1) * HEAD_DIM]
            query[i, :, h * HEAD_DIM : (h + 1) * HEAD_DIM] = (field * cos + turn(field) * sin).astype(
                BF16
            )
        field = mixed[:, group * HEAD_DIM :]
        turned = field * cos + turn(field) * sin
        kind[i] = jnp.where(is_key, turned, field).astype(BF16)


def stack_heads(block, group):
    block = block.reshape(SPAN, group * HEAD_DIM)
    return jnp.concatenate(
        [block[:, h * HEAD_DIM : (h + 1) * HEAD_DIM] for h in range(group)], axis=0
    )


def key_mask(first_key, keys, place, group):
    key = first_key + lax.broadcasted_iota(jnp.int32, (keys, group * SPAN), 0)
    row = lax.broadcasted_iota(jnp.int32, (keys, group * SPAN), 1) % SPAN
    return key <= place * SPAN + row


def attend_kernel(
    depth, spans, chunk, group, scale, order, place, query, a_own, a_far, b_own, b_far, out, lse, kv
):
    seq = pl.program_id(0)
    core, x, z = place[AT_C], place[AT_X], place[AT_Z]
    step = query.shape[0] // spans
    slots = depth * PAIR * spans

    def settle(slot, unused):
        blk, span = slot // spans, lax.rem(slot, spans)
        d = lax.rem(z - blk // PAIR + depth, depth)
        there = pl.ds(pl.multiple_of(order[seq, slot] * SPAN, SPAN), SPAN)
        here = pl.ds(span * step, step)
        for mine, other, far in ((a_own, b_own, False), (a_far, b_far, True)):

            @pl.when((lax.rem(blk, PAIR) != x) == far)
            def unused_copy():
                kv[0, core, there] = mine[d, here, 0].reshape(SPAN, HEAD_DIM)
                kv[0, 1 - core, there] = other[d, here, 0].reshape(SPAN, HEAD_DIM)

        return 0

    lax.fori_loop(0, slots, settle, 0)
    for span in range(spans):
        spot = order[seq, place[AT_B] * spans + span]
        queries = stack_heads(query[span * step : (span + 1) * step, 0], group)

        def advance(index, state, masked):
            peak, total, summed = state
            keys = pl.ds(pl.multiple_of(index * chunk, chunk), chunk)
            scores = dot_nt(kv[0, 0, keys], queries)
            if masked:
                allowed = key_mask(index * chunk, chunk, spot, group)
                scores = jnp.where(allowed, scores, FLOOR)
            new_peak = jnp.maximum(peak, jnp.max(scores, axis=0, keepdims=True))
            weights = jnp.exp2((scores - new_peak) * scale)
            fade = jnp.exp2((peak - new_peak) * scale)
            total = total * fade + jnp.sum(weights, axis=0, keepdims=True)
            summed = summed * fade + dot_tn(kv[0, 1, keys], weights.astype(BF16))
            return new_peak, total, summed

        start = (
            jnp.full((1, group * SPAN), FLOOR, F32),
            jnp.zeros((1, group * SPAN), F32),
            jnp.zeros((HEAD_DIM, group * SPAN), F32),
        )
        last = spot * SPAN // chunk
        state = lax.fori_loop(0, last, lambda i, s: advance(i, s, False), start)
        peak, total, summed = advance(last, state, True)
        lse[0, span] = peak * scale + jnp.log2(total)
        result = (summed / total).T.astype(BF16)
        for h in range(group):
            out[span * step : (span + 1) * step, 0, :, h * HEAD_DIM : (h + 1) * HEAD_DIM] = result[
                h * SPAN : (h + 1) * SPAN
            ].reshape(step, SPAN // step, HEAD_DIM)


def attend_back_kernel(
    depth,
    spans,
    chunk,
    group,
    scale,
    factor,
    order,
    place,
    query,
    kv,
    grad,
    out,
    lse,
    cosine,
    sine,
    query_grad,
    keep_own,
    keep_far,
    send_both,
    sums,
):
    seq = pl.program_id(0)
    core, x, z = place[AT_C], place[AT_X], place[AT_Z]
    step = query.shape[0] // spans
    slots = depth * PAIR * spans
    sums[...] = jnp.zeros(sums.shape, F32)
    for span in range(spans):
        spot = order[seq, place[AT_B] * spans + span]
        at = slice(span * step, (span + 1) * step)
        queries = stack_heads(query[at, 0], group)
        grads = stack_heads(grad[at, 0], group)
        results = stack_heads(out[at, 0], group)
        delta = jnp.sum(
            (grads.astype(F32) * results.astype(F32)).T, axis=0, keepdims=True
        )
        level = lse[0, span]

        def advance(index, total, masked):
            keys = pl.ds(pl.multiple_of(index * chunk, chunk), chunk)
            key, value = kv[0, 0, keys], kv[0, 1, keys]
            probs = jnp.exp2(dot_nt(key, queries) * scale - level)
            if masked:
                probs = jnp.where(key_mask(index * chunk, chunk, spot, group), probs, 0.0)
            score_grad = (probs * (dot_nt(value, grads) - delta)).astype(BF16)
            sums[1, keys] += dot_nn(probs.astype(BF16), grads)
            sums[0, keys] += dot_nn(score_grad, queries)
            return total + dot_tn(key, score_grad)

        last = spot * SPAN // chunk
        total = jnp.zeros((HEAD_DIM, group * SPAN), F32)
        total = lax.fori_loop(0, last, lambda i, s: advance(i, s, False), total)
        total = (advance(last, total, True) * factor).T
        cos = cosine[at, 0].reshape(SPAN, HEAD_DIM)
        sin = sine[at, 0].reshape(SPAN, HEAD_DIM)
        for h in range(group):
            field = total[h * SPAN : (h + 1) * SPAN]
            field = (field * cos - turn(field) * sin).astype(BF16)
            query_grad[at, 0, :, h * HEAD_DIM : (h + 1) * HEAD_DIM] = field.reshape(
                step, SPAN // step, HEAD_DIM
            )

    keep_scale = jnp.where(core == 0, factor, 1.0)
    send_scale = jnp.where(core == 0, 1.0, factor)

    def settle(slot, unused):
        blk, span = slot // spans, lax.rem(slot, spans)
        d = lax.rem(z - blk // PAIR + depth, depth)
        there = pl.ds(pl.multiple_of(order[seq, slot] * SPAN, SPAN), SPAN)
        here = pl.ds(span * step, step)
        shape = (step, SPAN // step, HEAD_DIM)
        for keep, send, far in ((keep_own, 0, False), (keep_far, 1, True)):

            @pl.when((lax.rem(blk, PAIR) != x) == far)
            def unused_copy():
                keep[d, here, 0] = (sums[core, there] * keep_scale).astype(BF16).reshape(shape)
                send_both[send, d, here, 0] = (sums[1 - core, there] * send_scale).astype(BF16).reshape(shape)

        return 0

    lax.fori_loop(0, slots, settle, 0)


def project_kernel(transposed, place, *refs):
    count = (len(refs) - 2) // 2
    lefts, rights, (keep, send) = refs[:count], refs[count : 2 * count], refs[2 * count :]
    u = place[AT_U]
    dot = dot_nt if transposed else dot_nn
    for at, target, spot in ((1, send, 0), (3, send, 1), (0, keep, 0), (2, keep, 1)):
        total = None
        for left, right in zip(lefts, rights):
            part = dot(left[u ^ at], right[...])
            total = part if total is None else total + part
        target[spot] = total.astype(target.dtype)


def heads_grad_kernel(place, own, near, across, weights, out):
    u = place[AT_U]
    for at, piece in ((0, own[...]), (2, near[...]), (1, across[0]), (3, across[1])):
        out[u ^ at] = dot_nt(piece, weights[...]).astype(BF16)


def out_share_kernel(place, own, near, across, attended, out):
    u = place[AT_U]
    total = dot_tn(attended[u], own[...])
    total = total + dot_tn(attended[u ^ 2], near[...])
    total = total + dot_tn(attended[u ^ 1], across[0])
    total = total + dot_tn(attended[u ^ 3], across[1])
    out[...] = total.astype(BF16)


def split_tiles_kernel(depth, place, gate, upper, down, gain, *rest):
    pieces, parts = rest[:depth], rest[depth]
    units = parts.shape[3]
    for i, (tile, scaled) in enumerate(((gate, True), (upper, True), (down, False))):
        for k in range(depth):
            part = tile[:, k * units : (k + 1) * units]
            if scaled:
                part = (part.astype(F32) * gain[...]).astype(BF16)
            parts[k, i] = part
    for d in range(depth):
        pieces[d][...] = parts[lax.rem(place[AT_Z] + d, depth)]


def merge_tiles_kernel(depth, place, *refs):
    mine, far, outs = refs[:depth], refs[depth : 2 * depth], refs[2 * depth :]
    for d in range(depth):
        from_z = lax.rem(place[AT_Z] - d + depth, depth)
        for i, out in enumerate(outs):
            out[from_z * PAIR + place[AT_X]] = mine[d][i]
            out[from_z * PAIR + 1 - place[AT_X]] = far[d][i]


def by_source_kernel(place, source, target):
    depth, ulys = source.shape[:2]
    for d in range(depth):
        from_z = lax.rem(place[AT_Z] - d + depth, depth)
        for m, other in enumerate((0, 2, 1, 3)):
            target[place[AT_U] ^ other, from_z] = source[d, m]


def sort_rows_kernel(depth, place, *refs):
    mine, far, outs, rows = refs[:depth], refs[depth : 2 * depth], refs[2 * depth : -1], refs[-1]
    share = outs[0].shape[0]
    for d in range(depth):
        from_z = lax.rem(place[AT_Z] - d + depth, depth)
        rows[from_z * PAIR + place[AT_X]] = mine[d][...]
        rows[from_z * PAIR + 1 - place[AT_X]] = far[d][...]
    for m, out in enumerate(outs):
        out[...] = rows[pl.ds((place[AT_U] ^ m) * share, share)]


def place_rows_kernel(place, *refs):
    out = refs[-1]
    for m, part in enumerate(refs[:-1]):
        out[:, place[AT_U] ^ m] = part[...]


def choose_kernel(place, *refs):
    shares, (keep, send) = refs[:-2], refs[-2:]
    for i, share in enumerate(shares):
        keep[:, i] = share[:, place[AT_X]]
        send[:, i] = share[:, 1 - place[AT_X]]


def fold_kernel(depth, place, keep, got, *outs):
    for d in range(depth):
        at = lax.rem(place[AT_Z] + d, depth)
        outs[d][...] = (keep[at].astype(F32) + got[at].astype(F32)).astype(BF16)


def split_uly_kernel(place, pieces, own, near):
    total = None
    parts = []
    for m in range(4):
        total = None
        for z in range(pieces.shape[0]):
            part = pieces[z, 0, place[AT_U] ^ m].astype(F32)
            total = part if total is None else total + part
        parts.append(total.astype(BF16))
    own[0], own[1], near[0], near[1] = parts


def pick_uly_kernel(place, share, own, near):
    own[0], own[1] = share[:, place[AT_U]], share[:, place[AT_U] ^ 1]
    near[0], near[1] = share[:, place[AT_U] ^ 2], share[:, place[AT_U] ^ 3]


def group_rows_kernel(place, own, near, across, keep, send, rows):
    share = own.shape[1]
    for m, part in ((0, own[0]), (2, near[0]), (1, across[0]), (3, across[1])):
        rows[pl.ds((place[AT_U] ^ m) * share, share)] = part
    for z in range(keep.shape[0]):
        keep[z, 0] = rows[z * PAIR + place[AT_X]]
        send[z, 0] = rows[z * PAIR + 1 - place[AT_X]]


def finish_qkv_kernel(place, *refs):
    heads, kinds = refs[:3], refs[3:6]
    weight, gain, grad, grad_gain, bias, head_parts, kind_parts = refs[6:]
    width, side = heads[0].shape[2], heads[0].shape[2] * 4
    for parts, (own, near, across) in ((head_parts, heads), (kind_parts, kinds)):
        parts[place[AT_U]] = own[0]
        parts[place[AT_U] ^ 2] = near[0]
        parts[place[AT_U] ^ 1] = across[0]
        parts[place[AT_U] ^ 3] = across[1]
    total = jnp.zeros(grad_gain.shape, F32)
    for u in range(4):
        bias[u] = kind_parts[u, :16].astype(F32)
        start = side + (u % 2) * KV_HEADS * HEAD_DIM + (u // 2) * HEAD_DIM
        for at, part in (
            (slice(u * width, (u + 1) * width), head_parts[u]),
            (slice(start, start + HEAD_DIM), kind_parts[u, 16:]),
        ):
            part = part.astype(F32)
            grad[:, at] = part * gain[...]
            total = total + jnp.sum(part * weight[:, at].astype(F32), axis=1, keepdims=True)
    grad_gain[...] = total


def finish_kernel(depth, gates, uppers, downs, gate, upper, gain, grad_gate, grad_upper, grad_down, grad_gain):
    units = downs.shape[3]
    total = jnp.zeros(grad_gain.shape, F32)
    for k in range(depth):
        at = slice(k * units, (k + 1) * units)
        part = gates[k, 0].astype(F32)
        grad_gate[:, at] = part * gain[...]
        total = total + jnp.sum(part * gate[:, at].astype(F32), axis=1, keepdims=True)
        part = uppers[k, 0].astype(F32)
        grad_upper[:, at] = part * gain[...]
        total = total + jnp.sum(part * upper[:, at].astype(F32), axis=1, keepdims=True)
        grad_down[:, at] = downs[k, 0].astype(F32)
    grad_gain[...] = total


def like(shape, kind=BF16):
    return jax.ShapeDtypeStruct(shape, kind)


def together(*values):
    return lax.optimization_barrier(values)


def after(value, *others):
    return lax.optimization_barrier((value, others))[0]


class Grid:
    def __init__(self):
        self.blocks = lax.axis_size("blk")
        self.ulys = lax.axis_size("uly")
        self.depth = self.blocks // PAIR
        self.b = lax.axis_index("blk")
        self.u = lax.axis_index("uly")
        self.z = self.b // PAIR
        self.x = self.b % PAIR
        self.y = self.u // 2
        self.c = self.u % 2

    def to_z(self, value, step):
        pairs = [
            (z * PAIR + x, ((z + step) % self.depth) * PAIR + x)
            for z in range(self.depth)
            for x in range(PAIR)
        ]
        return lax.ppermute(value, "blk", pairs)

    def swap_x(self, value):
        return lax.ppermute(value, "blk", [(i, i ^ 1) for i in range(self.blocks)])

    def swap_y(self, value):
        return lax.ppermute(value, "uly", [(i, i ^ 2) for i in range(self.ulys)])

    def swap_both(self, value):
        return lax.ppermute(value, "uly", [(i, i ^ 3) for i in range(self.ulys)])

    def swap_core(self, value):
        return lax.ppermute(value, "uly", [(i, i ^ 1) for i in range(self.ulys)])


def paired(bit, mine, other, axis):
    low = jnp.where(bit == 0, mine, other)
    high = jnp.where(bit == 0, other, mine)
    return jnp.stack([low, high], axis=axis)


def pick(bit, array, axis):
    low = lax.index_in_dim(array, 0, axis, keepdims=False)
    high = lax.index_in_dim(array, 1, axis, keepdims=False)
    return jnp.where(bit == 0, low, high), jnp.where(bit == 0, high, low)


def order_z(grid, pieces):
    stacked = jnp.stack(pieces[::-1] + pieces[::-1][:-1])
    start = (grid.depth - 1 - grid.z) % grid.depth
    return lax.dynamic_slice_in_dim(stacked, start, grid.depth, 0)


def gather_uly(grid, value):
    both = paired(grid.y, value, grid.swap_y(value), 0)
    every = paired(grid.c, both, grid.swap_core(both), 1)
    return every.reshape((grid.ulys,) + value.shape)


def scatter_uly(grid, parts, kind=BF16):
    parts = parts.reshape((2, 2) + parts.shape[1:])
    keep, send = pick(grid.c, parts, 1)
    both = keep.astype(F32) + grid.swap_core(send.astype(kind)).astype(F32)
    keep, send = pick(grid.y, both, 0)
    return keep + grid.swap_y(send.astype(kind)).astype(F32)


def gather_blk(grid, value):
    pieces = [value] + [grid.to_z(value, d) for d in range(1, grid.depth)]
    pairs = [paired(grid.x, piece, grid.swap_x(piece), 0) for piece in pieces]
    return order_z(grid, pairs)


def exchange_z(grid, parts):
    pieces = [lax.dynamic_index_in_dim(parts, grid.z, 0, keepdims=False)]
    for d in range(1, grid.depth):
        there = (grid.z + d) % grid.depth
        pieces.append(grid.to_z(lax.dynamic_index_in_dim(parts, there, 0, keepdims=False), d))
    return pieces


def exchange_z_all(grid, parts):
    groups = [[z * PAIR + x for z in range(grid.depth)] for x in range(PAIR)]
    return lax.all_to_all(
        parts, "blk", split_axis=0, concat_axis=0, axis_index_groups=groups, tiled=True
    )


def scatter_blk(grid, parts):
    keep, send = pick(grid.x, parts, 1)
    both = keep.astype(F32) + grid.swap_x(send.astype(BF16)).astype(F32)
    return jnp.sum(exchange_z_all(grid, both.astype(BF16)).astype(F32), axis=0)


def exchange_uly(parts):
    return lax.all_to_all(parts, "uly", split_axis=0, concat_axis=0, tiled=True)


def per_device(
    tokens,
    span_order,
    attn_gain,
    qkv_weight,
    qkv_bias,
    out_weight,
    ffn_gain,
    gate_weight,
    up_weight,
    down_weight,
    cotangent,
):
    grid = Grid()
    local_rows, seqs, model = tokens.shape
    count = local_rows * seqs
    ulys = grid.ulys
    depth = grid.depth
    blocks = grid.blocks
    cycle_rows = local_rows * ulys
    spans = cycle_rows // SPAN
    slots = blocks * spans
    group = HEADS // ulys
    factor = 1.0 / math.sqrt(HEAD_DIM)
    width = group * HEAD_DIM
    columns = width + HEAD_DIM
    shard = qkv_weight.shape[0]
    block_model = shard * ulys
    chunk = math.gcd(slots, 4) * SPAN
    side = HEADS * HEAD_DIM
    place = jnp.stack([grid.z, grid.x, grid.y, grid.c, grid.b, grid.u]).astype(jnp.int32)

    def by_seq(array):
        return jnp.transpose(array, (1, 0, 2)).reshape(count, model)

    def by_row(array):
        return jnp.transpose(array.reshape(seqs, local_rows, model), (1, 0, 2))

    def by_uly(array):
        lead = array.shape[0]
        heads = array[:, :side].reshape(lead, ulys, width)
        kinds = array[:, side:].reshape(lead, 2, KV_HEADS, HEAD_DIM)
        kinds = jnp.transpose(kinds, (0, 2, 1, 3)).reshape(lead, ulys, HEAD_DIM)
        return jnp.transpose(jnp.concatenate([heads, kinds], axis=-1), (1, 0, 2))

    rows = by_seq(tokens).astype(F32)
    unit_one, factor_one = norm_rows(rows)
    unit_own = unit_one.astype(BF16)
    unit_near = grid.swap_y(unit_own)
    gain_one = attn_gain.astype(F32)[:, None]
    scaled = (qkv_weight.astype(F32) * gain_one).astype(BF16)
    heads_share = blocks // ulys
    owned_columns = qkv_bias.shape[0]
    column_start = (grid.b * ulys + grid.u) * owned_columns
    bias_row = lax.dynamic_update_slice(
        jnp.zeros((16, owned_columns * blocks * ulys), BF16),
        jnp.pad(qkv_bias[None], ((0, 15), (0, 0))),
        (0, column_start),
    )
    by_head = by_uly(jnp.concatenate([scaled, bias_row], axis=0))
    by_head = exchange_uly(by_head)
    block_rows = jnp.concatenate(
        [by_head[:, :shard].reshape(block_model, columns), jnp.sum(by_head[:, shard:], axis=0)],
        axis=0,
    )
    qkv_mine = [block_rows] + [grid.to_z(block_rows, d) for d in range(1, depth)]
    first_far = grid.swap_x(block_rows)
    cot_flat = by_seq(cotangent)
    *qkv_mine, first_far, unit_near = together(*qkv_mine, first_far, unit_near)

    gain_two = ffn_gain.astype(F32)[:, None]
    hidden_units = gate_weight.shape[1] // depth
    tile_pieces = call(
        functools.partial(split_tiles_kernel, depth),
        [place],
        [gate_weight, up_weight, down_weight.T, gain_two],
        [like((3, block_model, hidden_units))] * depth,
        scratch=[pltpu.VMEM((depth, 3, block_model, hidden_units), BF16)],
    )
    qkv_far = [first_far] + [grid.swap_x(piece) for piece in qkv_mine[1:]]
    unit_across = grid.swap_core(jnp.stack([unit_own, unit_near]))
    out_first, cot_first = after((out_weight, cot_flat), *qkv_mine[1:])
    out_mine = [out_first] + [grid.to_z(out_first, d) for d in range(1, depth)]
    cot_near = grid.swap_y(cot_first)
    *held, unit_across, cot_near = together(*qkv_far, *out_mine, unit_across, cot_near)
    qkv_far, out_mine = held[:depth], held[depth:]
    unit_parts = (unit_own, unit_near, unit_across)

    head_rows = grid.b * cycle_rows + jnp.arange(cycle_rows, dtype=jnp.int32)
    places = positions(span_order, head_rows).reshape(seqs, ulys, local_rows)
    places = jnp.transpose(places, (1, 0, 2)).reshape(ulys, count)
    cosine, sine = rope_tables(places)
    units, qkv_part, query, kind = call(
        functools.partial(mix_kernel, depth, group),
        [place],
        [*unit_parts, cosine, sine, *qkv_mine, *qkv_far],
        [
            like((ulys, count, model)),
            like((blocks, block_model, columns)),
            like((ulys, count, width)),
            like((ulys, count, HEAD_DIM)),
        ],
        scratch=[
            pltpu.VMEM((blocks, 16, columns), BF16),
            pltpu.SemaphoreType.DMA((2 * blocks + ulys,)),
        ],
        far=(0, 1, 2, *range(5, 2 * depth + 5)),
    )
    units = units.reshape(ulys * count, model)
    qkv_part = qkv_part.reshape(model, columns)
    order = sorted(range(1, depth), key=lambda d: (min(d, depth - d), d))
    kinds = [kind] + [grid.to_z(kind, d) for d in range(1, depth)]
    *held, kind = after((*out_mine, *tile_pieces, kind), kind)
    out_mine, tile_pieces = held[:depth], held[depth:]
    out_far = [grid.swap_x(piece) for piece in out_mine]
    tile_mine = {0: tile_pieces[0]}
    tile_mine[order[0]] = grid.to_z(tile_pieces[order[0]], order[0])
    *held, cot_near = together(*kinds, *out_far, cot_near)
    kinds, out_far = held[:depth], held[depth:]

    a_own = jnp.stack(kinds)
    a_far = grid.swap_x(a_own)
    b_own = grid.swap_core(a_own)
    out_sets = call(
        functools.partial(sort_rows_kernel, depth),
        [place],
        [*out_mine, *out_far],
        [like((blocks // ulys, shard, model))] * ulys,
        scratch=[pltpu.VMEM((blocks, shard, model), BF16)],
    )
    out_sets = [
        out_sets[0],
        grid.swap_core(out_sets[1]),
        grid.swap_y(out_sets[2]),
        grid.swap_both(out_sets[3]),
    ]
    middle, late = order[1:-1], order[-1]
    for d in middle:
        tile_mine[d] = grid.to_z(after(tile_pieces[d], *kinds), d)
    a_far, b_own, tile_mine[order[0]], *held = together(
        a_far, b_own, tile_mine[order[0]], *[tile_mine[d] for d in middle]
    )
    tile_mine.update(zip(middle, held))

    b_far = grid.swap_core(a_far)
    tile_far = {0: grid.swap_x(after(tile_mine[0], a_far))}
    tile_far[order[0]] = grid.swap_x(tile_mine[order[0]])
    tile_mine[late] = grid.to_z(after(tile_pieces[late], a_far), late)

    def over_uly(piece):
        both = jnp.concatenate([piece, grid.swap_y(piece)], axis=0)
        return jnp.concatenate([both, grid.swap_core(both)], axis=0)

    grad_rows = cot_flat.astype(F32)

    scale = factor * LOG2E
    kv_shape = (depth, ulys, seqs, local_rows, HEAD_DIM)
    kv_spec = pl.BlockSpec(
        (depth, ulys, 1, local_rows, HEAD_DIM), lambda s, *unused: (0, 0, s, 0, 0)
    )
    heads_shape = (ulys, seqs, local_rows, width)
    heads_spec = pl.BlockSpec((ulys, 1, local_rows, width), lambda s, *unused: (0, s, 0, 0))
    lse_spec = pl.BlockSpec((1, spans, 1, group * SPAN), lambda s, *unused: (s, 0, 0, 0))
    table_shape = (ulys, seqs, local_rows, HEAD_DIM)
    table_spec = pl.BlockSpec((ulys, 1, local_rows, HEAD_DIM), lambda s, *unused: (0, s, 0, 0))
    sorted_spec = pl.BlockSpec((1, 2, slots * SPAN, HEAD_DIM), lambda s, *unused: (s, 0, 0, 0))
    params = pltpu.CompilerParams(vmem_limit_bytes=VMEM_LIMIT)
    query = query.reshape(heads_shape)
    attended, lse, kv = pl.pallas_call(
        functools.partial(attend_kernel, depth, spans, chunk, group, scale),
        grid_spec=pltpu.PrefetchScalarGridSpec(
            num_scalar_prefetch=2,
            grid=(seqs,),
            in_specs=[heads_spec] + [kv_spec] * 4,
            out_specs=[heads_spec, lse_spec, sorted_spec],
        ),
        out_shape=[
            like(heads_shape),
            like((seqs, spans, 1, group * SPAN), F32),
            like((seqs, 2, slots * SPAN, HEAD_DIM)),
        ],
        compiler_params=params,
        cost_estimate=SMALL,
    )(span_order, place, query, *[part.reshape(kv_shape) for part in (a_own, a_far, b_own, b_far)])
    flat = attended.reshape(ulys, count, width)
    out_sets = after(tuple(out_sets), attended)
    (out_part,) = call(
        place_rows_kernel, [place], out_sets, [like((blocks // ulys, ulys, shard, model))]
    )
    out_part = out_part.reshape(width, model)
    keep, send = call(
        functools.partial(project_kernel, False),
        [place],
        [flat, out_part],
        [like((2, count, model), F32), like((2, count, model))],
    )
    got = grid.swap_core(send)
    got, tile_far[0] = together(got, tile_far[0])
    both = keep + got.astype(F32)
    for d in middle:
        tile_far[d] = grid.swap_x(after(tile_mine[d], got))
    got = grid.swap_y(both[1].astype(BF16))
    got, tile_far[order[0]], tile_mine[late], *held = together(
        got, tile_far[order[0]], tile_mine[late], *[tile_far[d] for d in middle]
    )
    tile_far.update(zip(middle, held))
    hidden = rows + both[0] + got.astype(F32)

    unit_two, factor_two = norm_rows(hidden)
    mid_own = unit_two.astype(BF16)
    mid_near = grid.swap_y(mid_own)
    mid_pieces = [mid_own, grid.to_z(mid_own, 1)]
    cot_pieces = [cot_first, grid.to_z(after(cot_first, got), 1)]
    tile_far[late] = grid.swap_x(after(tile_mine[late], got))
    mid_near, mid_pieces[1] = together(mid_near, mid_pieces[1])
    for d in range(2, depth):
        mid_pieces.append(grid.to_z(mid_pieces[-1], 1))
        cot_pieces.append(grid.to_z(cot_pieces[-1], 1))

    def chunk_of(own, near):
        both = jnp.concatenate([own, near], axis=0)
        return jnp.concatenate([both, grid.swap_core(both)], axis=0)

    mid_chunks = [chunk_of(mid_own, mid_near)] + [over_uly(piece) for piece in mid_pieces[1:]]
    cot_chunks = [chunk_of(cot_first, cot_near)] + [over_uly(piece) for piece in cot_pieces[1:]]
    gate_used, upper_used, down_used = [
        tile.reshape(model, hidden_units)
        for tile in call(
            functools.partial(merge_tiles_kernel, depth),
            [place],
            [tile_mine[d] for d in range(depth)] + [tile_far[d] for d in range(depth)],
            [like((blocks, block_model, hidden_units))] * 3,
        )
    ]
    actives, gate_grads, upper_grads, back_chunks = [], [], [], []
    for mid, cot in zip(mid_chunks, cot_chunks):
        gate = matmul(mid, gate_used)
        upper = matmul(mid, upper_used)
        sigmoid = jax.nn.sigmoid(gate)
        active_grad = matmul(cot, down_used)
        actives.append((gate * sigmoid * upper).astype(BF16))
        gate_grad = (active_grad * upper * sigmoid * (1.0 + gate * (1.0 - sigmoid))).astype(BF16)
        upper_grad = (active_grad * gate * sigmoid).astype(BF16)
        gate_grads.append(gate_grad)
        upper_grads.append(upper_grad)
        back_chunks.append(
            contract_cols(gate_grad, gate_used) + contract_cols(upper_grad, upper_used)
        )
    def over_core(chunk):
        chunk = chunk.reshape(2, 2, count, model)
        return chunk[0].astype(F32) + grid.swap_core(chunk[1].astype(BF16)).astype(F32)

    def over_y(both):
        return both[0] + grid.swap_y(both[1].astype(BF16)).astype(F32)

    def halve(shares, rows):
        shape = (depth, PAIR, *rows, shares[0].shape[-1])
        shares = [share.astype(BF16).reshape(shape) for share in shares]
        half = like((depth, len(shares), *rows, shape[-1]))
        return call(choose_kernel, [place], shares, [half] * 2)

    def fold(keep, got):
        return exchange_z_all(grid, (keep.astype(F32) + got.astype(F32)).astype(BF16))

    z_groups = [[z * PAIR + x for z in range(depth)] for x in range(PAIR)]
    tile_rows = (block_model,)
    mid_parts = [over_y(over_core(chunk)) for chunk in back_chunks]
    back_pieces = [grid.to_z(mid_parts[d].astype(BF16), -d) for d in range(1, depth)]
    mid_all = after(jnp.concatenate(mid_chunks), *back_chunks)
    cot_all = jnp.concatenate(cot_chunks)
    active_all = jnp.concatenate(actives)
    gate_keep, gate_send = halve([contract_rows(mid_all, jnp.concatenate(gate_grads))], tile_rows)
    upper_keep, upper_send = halve(
        [contract_rows(after(mid_all, gate_send), jnp.concatenate(upper_grads))], tile_rows
    )
    active_now = after(active_all, upper_send)
    down_keep, down_send = halve([contract_rows(cot_all, active_now)], tile_rows)
    gate_got = grid.swap_x(gate_send)
    upper_got = grid.swap_x(after(upper_send, gate_got))
    down_got = grid.swap_x(after(down_send, upper_got))
    first, gate_got, upper_got, down_send, *back_pieces = together(
        mid_parts[0], gate_got, upper_got, down_send, *back_pieces
    )
    mid_grad = first + sum(piece.astype(F32) for piece in back_pieces)

    hidden_grad = grad_rows + norm_back(mid_grad, unit_two, factor_two)
    branch_own = hidden_grad.astype(BF16)
    branch_near = grid.swap_y(branch_own)
    out_all = contract_cols(after(active_all, branch_own), down_used).astype(BF16)
    gate_owned = fold(*after((gate_keep, gate_got), branch_own))
    branch_near, out_all, down_got = together(branch_near, out_all, down_got)
    branch_across = grid.swap_core(jnp.stack([branch_own, branch_near]))
    branch_parts = (branch_own, branch_near, branch_across)
    (grad_heads,) = call(
        heads_grad_kernel, [place], [*branch_parts, out_part], [like((ulys, count, width))]
    )

    grad_heads = grad_heads.reshape(heads_shape)
    both_spec = pl.BlockSpec(
        (2, depth, ulys, 1, local_rows, HEAD_DIM), lambda s, *unused: (0, 0, 0, s, 0, 0)
    )
    query_grad, keep_own, keep_far, send_both = pl.pallas_call(
        functools.partial(attend_back_kernel, depth, spans, chunk, group, scale, factor),
        grid_spec=pltpu.PrefetchScalarGridSpec(
            num_scalar_prefetch=2,
            grid=(seqs,),
            in_specs=[heads_spec, sorted_spec]
            + [heads_spec] * 2
            + [lse_spec]
            + [table_spec] * 2,
            out_specs=[heads_spec] + [kv_spec] * 2 + [both_spec],
            scratch_shapes=[pltpu.VMEM((2, slots * SPAN, HEAD_DIM), F32)],
        ),
        out_shape=[like(heads_shape)] + [like(kv_shape)] * 2 + [like((2, *kv_shape))],
        compiler_params=params,
        cost_estimate=SMALL,
    )(
        span_order,
        place,
        query,
        kv,
        grad_heads,
        attended,
        lse,
        cosine.reshape(table_shape),
        sine.reshape(table_shape),
    )
    got_far, got_own = [
        jnp.concatenate([grid.swap_core(part) for part in jnp.split(send_both[k], 2, axis=0)])
        for k in (1, 0)
    ]
    query_grad = query_grad.reshape(ulys * count, width)
    got_far, got_own, query_grad, gate_owned = together(got_far, got_own, query_grad, gate_owned)
    upper_owned = fold(*after((upper_keep, upper_got), gate_owned))
    (out_all,) = call(
        by_source_kernel,
        [place],
        [after(out_all, got_far).reshape(depth, ulys, count, model)],
        [like((ulys, depth, count, model))],
    )
    from_x = grid.swap_x((keep_far.astype(F32) + got_far.astype(F32)).astype(BF16))
    share_parts = after(branch_parts, got_far)
    (out_share,) = call(out_share_kernel, [place], [*share_parts, flat], [like((width, model))])
    out_own, out_near = call(
        pick_uly_kernel,
        [place],
        [out_share.reshape(heads_share, ulys, shard, model)],
        [like((2, heads_share, shard, model))] * 2,
    )
    head_keep, head_send = halve([contract_rows(units, query_grad)], (ulys, shard))
    from_x, head_send, out_near, out_all = together(from_x, head_send, out_near, out_all)
    out_all = lax.psum_scatter(out_all, "uly", scatter_dimension=0, tiled=False)
    out_all = lax.psum_scatter(
        out_all, "blk", scatter_dimension=0, axis_index_groups=z_groups, tiled=False
    )
    kind_parts = keep_own.astype(F32) + got_own.astype(F32) + from_x.astype(F32)
    kind_parts = kind_parts.astype(BF16)
    kind_back = [grid.to_z(kind_parts[d], -d) for d in range(1, depth)]
    head_got = grid.swap_x(head_send)
    out_near = grid.swap_y(out_near)
    *kind_back, out_near, kind_parts, head_got, upper_owned = together(
        *kind_back, out_near, kind_parts, head_got, upper_owned
    )
    out_across = grid.swap_core(jnp.stack([out_own[1], out_near[1]]))
    head_pieces = fold(head_keep, head_got)
    kind_grad = kind_parts[0].astype(F32)
    for piece in kind_back:
        kind_grad = kind_grad + piece.astype(F32)
    kind_grad = kind_grad.reshape(ulys * count, HEAD_DIM)
    turned = jnp.roll(kind_grad, HEAD_DIM // 2, axis=1)
    is_key = grid.c == 0
    flat_cosine = cosine.reshape(ulys * count, HEAD_DIM)
    flat_sine = sine.reshape(ulys * count, HEAD_DIM)
    kind_grad = jnp.where(is_key, kind_grad * flat_cosine - turned * flat_sine, kind_grad)
    kind_grad = kind_grad.astype(BF16)

    bias = jnp.sum(query_grad.astype(F32), axis=0).reshape(group, HEAD_DIM)
    bias = jnp.concatenate([bias, jnp.sum(kind_grad.astype(F32), axis=0)[None]], axis=0)
    bias = jnp.pad(bias.astype(BF16), ((0, 16 - group - 1), (0, 0)))
    bias = jnp.broadcast_to(bias, (blocks, ulys, 16, HEAD_DIM))
    share = contract_rows(units, kind_grad).astype(BF16)
    share = share.reshape(blocks, ulys, shard, HEAD_DIM)
    share = jnp.concatenate([bias, share], axis=2)
    kind_keep, kind_send = halve([share], (ulys, shard + 16))
    kind_got = grid.swap_x(kind_send)
    keep, send = call(
        functools.partial(project_kernel, True),
        [place],
        [
            query_grad.reshape(ulys, count, width),
            kind_grad.reshape(ulys, count, HEAD_DIM),
            qkv_part[:, :width],
            qkv_part[:, width:],
        ],
        [like((2, count, model), F32), like((2, count, model))],
    )
    send, kind_got, out_across = after((send, kind_got, out_across), send)
    both = keep + grid.swap_core(send).astype(F32)
    out_keep, out_send = call(
        group_rows_kernel,
        [place],
        [out_own, out_near, out_across],
        [like((depth, 1, shard, model))] * 2,
        scratch=[pltpu.VMEM((blocks, shard, model), BF16)],
    )
    out_got = grid.swap_x(out_send)
    down_owned = fold(*after((down_keep, down_got), head_pieces))
    out_pieces = fold(*after((out_keep, out_got), down_owned))
    kind_pieces = call(
        functools.partial(fold_kernel, depth),
        [place],
        [kind_keep, kind_got],
        [like(kind_keep.shape[1:])] * depth,
    )
    kind_pieces = [kind_pieces[0]] + [grid.to_z(kind_pieces[d], d) for d in range(1, depth)]
    kind_pieces = jnp.stack(kind_pieces)

    def to_owners(pieces):
        own, near = call(
            split_uly_kernel, [place], [pieces], [like((2, *pieces.shape[3:]))] * 2
        )
        near = grid.swap_y(near)
        return own, near, grid.swap_core(jnp.stack([own[1], near[1]]))

    head_owned = to_owners(head_pieces)
    kind_owned = to_owners(kind_pieces)
    grad_qkv, grad_gain_one, bias = call(
        finish_qkv_kernel,
        [place],
        [*head_owned, *kind_owned, qkv_weight, gain_one],
        [
            like(qkv_weight.shape, F32),
            like((shard, 1), F32),
            like((ulys, 16, HEAD_DIM), F32),
        ],
        scratch=[
            pltpu.VMEM((ulys, shard, width), BF16),
            pltpu.VMEM((ulys, shard + 16, HEAD_DIM), BF16),
        ],
    )
    grad_gain_one = grad_gain_one[:, 0]
    kind_bias = bias[:, group].reshape(KV_HEADS, 2, HEAD_DIM)
    bias = jnp.concatenate(
        [bias[:, :group].reshape(-1), jnp.transpose(kind_bias, (1, 0, 2)).reshape(-1)]
    )
    grad_bias = lax.dynamic_slice_in_dim(bias, column_start, owned_columns, 0)
    grad_out = jnp.sum(out_pieces[:, 0].astype(F32), axis=0)
    result = hidden + after(out_all, grad_qkv).astype(F32)
    output = by_row(result.astype(BF16))
    normed_grad = both[0] + grid.swap_y(both[1].astype(BF16)).astype(F32)
    grad_tokens = by_row(hidden_grad + norm_back(normed_grad, unit_one, factor_one))
    tile_shape = gate_weight.shape
    grad_gate, grad_upper, grad_down, gain_part = call(
        functools.partial(finish_kernel, depth),
        [],
        [*after((gate_owned, upper_owned, down_owned), head_pieces), gate_weight, up_weight, gain_two],
        [like(tile_shape, F32)] * 3 + [like((block_model, 1), F32)],
    )
    grad_down = grad_down.T
    grad_gain_two = scatter_uly(grid, gain_part.reshape(ulys, -1), F32)
    return (
        output,
        grad_tokens,
        grad_gain_one,
        grad_qkv,
        grad_bias,
        grad_out,
        grad_gain_two.reshape(-1),
        grad_gate,
        grad_upper,
        grad_down,
    )


def solution(mesh):
    in_specs = (
        P(("blk", "uly"), None, None),
        P(),
        P(("blk", "uly")),
        P(("blk", "uly"), None),
        P(("blk", "uly")),
        P(("blk", "uly"), None),
        P("blk"),
        P("blk", "uly"),
        P("blk", "uly"),
        P("uly", "blk"),
        P(("blk", "uly"), None, None),
    )
    out_specs = (
        P(("blk", "uly"), None, None),
        P(("blk", "uly"), None, None),
        P(("blk", "uly")),
        P(("blk", "uly"), None),
        P(("blk", "uly")),
        P(("blk", "uly"), None),
        P(("blk", "uly")),
        P("blk", "uly"),
        P("blk", "uly"),
        P("uly", "blk"),
    )
    return jax.shard_map(
        per_device, mesh=mesh, in_specs=in_specs, out_specs=out_specs, check_vma=False
    )
```

```python
import functools
import math

import jax
import jax.numpy as jnp
from jax import lax
from jax.experimental import pallas as pl
from jax.experimental.pallas import tpu as pltpu
from jax.sharding import PartitionSpec as P

HEADS = 12
KV_HEADS = 2
HEAD_DIM = 128
SPAN = 128
PAIR = 2


EPS = 1e-06
THETA = 1000000.0
FLOOR = -1e30
LOG2E = 1.4426950408889634
BF16 = jnp.bfloat16
F32 = jnp.float32
SMALL = pl.CostEstimate(flops=1, transcendentals=0, bytes_accessed=1)
VMEM_LIMIT = 48 * 1024 * 1024

def norm_rows(rows):
    factor = lax.rsqrt(jnp.mean(rows * rows, axis=-1, keepdims=True) + EPS)
    return (rows * factor, factor)


def norm_back(scaled, unit, factor):
    return factor * (scaled - unit * jnp.mean(scaled * unit, axis=-1, keepdims=True))


def matmul(left, right):
    return jnp.dot(left, right, preferred_element_type=F32)


def contract_rows(left, right):
    return lax.dot_general(left, right, (((0,), (0,)), ((), ())), preferred_element_type=F32)


def contract_cols(left, right):
    return lax.dot_general(left, right, (((1,), (1,)), ((), ())), preferred_element_type=F32)


def positions(order, rows):
    table = jnp.arange(order.shape[1], dtype=jnp.int32)
    slots = rows // SPAN
    picked = jnp.where(slots[None, :, None] == table[None, None, :], order[:, None, :], 0)
    return jnp.sum(picked, axis=-1) * SPAN + (rows % SPAN)[None, :]


def rope_tables(places):
    index = jnp.arange(HEAD_DIM // 2).astype(F32)
    freq = THETA ** (-2.0 * index / HEAD_DIM)
    angle = places.astype(F32)[..., None] * freq
    cosine, sine = jnp.cos(angle), jnp.sin(angle)
    cosine = jnp.concatenate([cosine, cosine], axis=-1)
    return (cosine, jnp.concatenate([-sine, sine], axis=-1))


def dot_nn(left, right):
    return lax.dot_general(left, right, (((1,), (0,)), ((), ())), preferred_element_type=F32)


def dot_nt(left, right):
    return lax.dot_general(left, right, (((1,), (1,)), ((), ())), preferred_element_type=F32)


def dot_tn(left, right):
    return lax.dot_general(left, right, (((0,), (0,)), ((), ())), preferred_element_type=F32)


def call(kernel, scalars, arrays, outs, **options):
    return pl.pallas_call(
        kernel,
        grid_spec=pltpu.PrefetchScalarGridSpec(
            num_scalar_prefetch=len(scalars),
            grid=(1,),
            in_specs=[
                pl.BlockSpec(memory_space=pltpu.HBM) if i in options.get("far", ()) else whole(array.shape)
                for i, array in enumerate(arrays)
            ],
            out_specs=[whole(out.shape) for out in outs],
            scratch_shapes=options.get("scratch", ()),
        ),
        out_shape=outs,
        compiler_params=pltpu.CompilerParams(vmem_limit_bytes=VMEM_LIMIT),
        cost_estimate=SMALL,
    )(*scalars, *arrays)


def whole(shape):
    return pl.BlockSpec(shape, lambda *unused: (0,) * len(shape))


def turn(field):
    return pltpu.roll(field, HEAD_DIM // 2, 1)


AT_Z, AT_X, AT_Y, AT_C, AT_B, AT_U = range(6)


def mix_kernel(depth, group, place, own, near, across, cosine, sine, *rest):
    pieces, far = rest[:depth], rest[depth : 2 * depth]
    units, weights, query, kind, bias_rows, flags = rest[2 * depth :]
    u = place[AT_U]
    rows = weights.shape[1]
    copies = []

    def bring(source, target):
        copies.append(pltpu.make_async_copy(source, target, flags.at[len(copies)]))
        copies[-1].start()

    for d in range(depth):
        from_z = lax.rem(place[AT_Z] - d + depth, depth)
        for k in range(PAIR):
            piece = far[d] if k else pieces[d]
            from_x = place[AT_X] if k == 0 else 1 - place[AT_X]
            bring(piece.at[pl.ds(0, rows)], weights.at[from_z * PAIR + from_x])
            bring(piece.at[pl.ds(rows, 16)], bias_rows.at[PAIR * d + k])
    bring(own, units.at[u])
    bring(near, units.at[u ^ 2])
    bring(across.at[0], units.at[u ^ 1])
    bring(across.at[1], units.at[u ^ 3])
    for copy in copies:
        copy.wait()
    bias = jnp.sum(bias_rows[...].astype(F32), axis=(0, 1))[None]
    model = units.shape[2]
    all_weights = weights[...].reshape(model, weights.shape[2])
    is_key = place[AT_C] == 0
    for i in range(units.shape[0]):
        mixed = dot_nn(units[i], all_weights) + bias
        cos, sin = cosine[i], sine[i]
        for h in range(group):
            field = mixed[:, h * HEAD_DIM : (h + 1) * HEAD_DIM]
            query[i, :, h * HEAD_DIM : (h + 1) * HEAD_DIM] = (field * cos + turn(field) * sin).astype(
                BF16
            )
        field = mixed[:, group * HEAD_DIM :]
        turned = field * cos + turn(field) * sin
        kind[i] = jnp.where(is_key, turned, field).astype(BF16)


def stack_heads(block, group):
    block = block.reshape(SPAN, group * HEAD_DIM)
    return jnp.concatenate(
        [block[:, h * HEAD_DIM : (h + 1) * HEAD_DIM] for h in range(group)], axis=0
    )


def key_mask(first_key, keys, place, group):
    key = first_key + lax.broadcasted_iota(jnp.int32, (keys, group * SPAN), 0)
    row = lax.broadcasted_iota(jnp.int32, (keys, group * SPAN), 1) % SPAN
    return key <= place * SPAN + row


def attend_kernel(
    depth, spans, chunk, group, scale, order, place, query, a_own, a_far, b_own, b_far, out, lse, kv
):
    seq = pl.program_id(0)
    core, x, z = place[AT_C], place[AT_X], place[AT_Z]
    step = query.shape[0] // spans
    slots = depth * PAIR * spans

    def settle(slot, unused):
        blk, span = slot // spans, lax.rem(slot, spans)
        d = lax.rem(z - blk // PAIR + depth, depth)
        there = pl.ds(pl.multiple_of(order[seq, slot] * SPAN, SPAN), SPAN)
        here = pl.ds(span * step, step)
        for mine, other, far in ((a_own, b_own, False), (a_far, b_far, True)):

            @pl.when((lax.rem(blk, PAIR) != x) == far)
            def unused_copy():
                kv[0, core, there] = mine[d, here, 0].reshape(SPAN, HEAD_DIM)
                kv[0, 1 - core, there] = other[d, here, 0].reshape(SPAN, HEAD_DIM)

        return 0

    lax.fori_loop(0, slots, settle, 0)
    for span in range(spans):
        spot = order[seq, place[AT_B] * spans + span]
        queries = stack_heads(query[span * step : (span + 1) * step, 0], group)

        def advance(index, state, masked):
            peak, total, summed = state
            keys = pl.ds(pl.multiple_of(index * chunk, chunk), chunk)
            scores = dot_nt(kv[0, 0, keys], queries)
            if masked:
                allowed = key_mask(index * chunk, chunk, spot, group)
                scores = jnp.where(allowed, scores, FLOOR)
            new_peak = jnp.maximum(peak, jnp.max(scores, axis=0, keepdims=True))
            weights = jnp.exp2((scores - new_peak) * scale)
            fade = jnp.exp2((peak - new_peak) * scale)
            total = total * fade + jnp.sum(weights, axis=0, keepdims=True)
            summed = summed * fade + dot_tn(kv[0, 1, keys], weights.astype(BF16))
            return new_peak, total, summed

        start = (
            jnp.full((1, group * SPAN), FLOOR, F32),
            jnp.zeros((1, group * SPAN), F32),
            jnp.zeros((HEAD_DIM, group * SPAN), F32),
        )
        last = spot * SPAN // chunk
        state = lax.fori_loop(0, last, lambda i, s: advance(i, s, False), start)
        peak, total, summed = advance(last, state, True)
        lse[0, span] = peak * scale + jnp.log2(total)
        result = (summed / total).T.astype(BF16)
        for h in range(group):
            out[span * step : (span + 1) * step, 0, :, h * HEAD_DIM : (h + 1) * HEAD_DIM] = result[
                h * SPAN : (h + 1) * SPAN
            ].reshape(step, SPAN // step, HEAD_DIM)


def attend_back_kernel(
    depth,
    spans,
    chunk,
    group,
    scale,
    factor,
    order,
    place,
    query,
    kv,
    grad,
    out,
    lse,
    cosine,
    sine,
    query_grad,
    keep_own,
    keep_far,
    send_both,
    sums,
):
    seq = pl.program_id(0)
    core, x, z = place[AT_C], place[AT_X], place[AT_Z]
    step = query.shape[0] // spans
    slots = depth * PAIR * spans
    sums[...] = jnp.zeros(sums.shape, F32)
    for span in range(spans):
        spot = order[seq, place[AT_B] * spans + span]
        at = slice(span * step, (span + 1) * step)
        queries = stack_heads(query[at, 0], group)
        grads = stack_heads(grad[at, 0], group)
        results = stack_heads(out[at, 0], group)
        delta = jnp.sum(
            (grads.astype(F32) * results.astype(F32)).T, axis=0, keepdims=True
        )
        level = lse[0, span]

        def advance(index, total, masked):
            keys = pl.ds(pl.multiple_of(index * chunk, chunk), chunk)
            key, value = kv[0, 0, keys], kv[0, 1, keys]
            probs = jnp.exp2(dot_nt(key, queries) * scale - level)
            if masked:
                probs = jnp.where(key_mask(index * chunk, chunk, spot, group), probs, 0.0)
            score_grad = (probs * (dot_nt(value, grads) - delta)).astype(BF16)
            sums[1, keys] += dot_nn(probs.astype(BF16), grads)
            sums[0, keys] += dot_nn(score_grad, queries)
            return total + dot_tn(key, score_grad)

        last = spot * SPAN // chunk
        total = jnp.zeros((HEAD_DIM, group * SPAN), F32)
        total = lax.fori_loop(0, last, lambda i, s: advance(i, s, False), total)
        total = (advance(last, total, True) * factor).T
        cos = cosine[at, 0].reshape(SPAN, HEAD_DIM)
        sin = sine[at, 0].reshape(SPAN, HEAD_DIM)
        for h in range(group):
            field = total[h * SPAN : (h + 1) * SPAN]
            field = (field * cos - turn(field) * sin).astype(BF16)
            query_grad[at, 0, :, h * HEAD_DIM : (h + 1) * HEAD_DIM] = field.reshape(
                step, SPAN // step, HEAD_DIM
            )

    keep_scale = jnp.where(core == 0, factor, 1.0)
    send_scale = jnp.where(core == 0, 1.0, factor)

    def settle(slot, unused):
        blk, span = slot // spans, lax.rem(slot, spans)
        d = lax.rem(z - blk // PAIR + depth, depth)
        there = pl.ds(pl.multiple_of(order[seq, slot] * SPAN, SPAN), SPAN)
        here = pl.ds(span * step, step)
        shape = (step, SPAN // step, HEAD_DIM)
        for keep, send, far in ((keep_own, 0, False), (keep_far, 1, True)):

            @pl.when((lax.rem(blk, PAIR) != x) == far)
            def unused_copy():
                keep[d, here, 0] = (sums[core, there] * keep_scale).astype(BF16).reshape(shape)
                send_both[send, d, here, 0] = (sums[1 - core, there] * send_scale).astype(BF16).reshape(shape)

        return 0

    lax.fori_loop(0, slots, settle, 0)


def project_kernel(transposed, place, *refs):
    count = (len(refs) - 2) // 2
    lefts, rights, (keep, send) = refs[:count], refs[count : 2 * count], refs[2 * count :]
    u = place[AT_U]
    dot = dot_nt if transposed else dot_nn
    for at, target, spot in ((1, send, 0), (3, send, 1), (0, keep, 0), (2, keep, 1)):
        total = None
        for left, right in zip(lefts, rights):
            part = dot(left[u ^ at], right[...])
            total = part if total is None else total + part
        target[spot] = total.astype(target.dtype)


def heads_grad_kernel(place, own, near, across, weights, out):
    u = place[AT_U]
    for at, piece in ((0, own[...]), (2, near[...]), (1, across[0]), (3, across[1])):
        out[u ^ at] = dot_nt(piece, weights[...]).astype(BF16)


def out_share_kernel(place, own, near, across, attended, out):
    u = place[AT_U]
    total = dot_tn(attended[u], own[...])
    total = total + dot_tn(attended[u ^ 2], near[...])
    total = total + dot_tn(attended[u ^ 1], across[0])
    total = total + dot_tn(attended[u ^ 3], across[1])
    out[...] = total.astype(BF16)


def split_tiles_kernel(depth, place, gate, upper, down, gain, *rest):
    pieces, parts = rest[:depth], rest[depth]
    units = parts.shape[3]
    for i, (tile, scaled) in enumerate(((gate, True), (upper, True), (down, False))):
        for k in range(depth):
            part = tile[:, k * units : (k + 1) * units]
            if scaled:
                part = (part.astype(F32) * gain[...]).astype(BF16)
            parts[k, i] = part
    for d in range(depth):
        pieces[d][...] = parts[lax.rem(place[AT_Z] + d, depth)]


def merge_tiles_kernel(depth, place, *refs):
    mine, far, outs = refs[:depth], refs[depth : 2 * depth], refs[2 * depth :]
    for d in range(depth):
        from_z = lax.rem(place[AT_Z] - d + depth, depth)
        for i, out in enumerate(outs):
            out[from_z * PAIR + place[AT_X]] = mine[d][i]
            out[from_z * PAIR + 1 - place[AT_X]] = far[d][i]


def down_kernel(depth, place, *refs):
    actives, (weight, out) = refs[:depth], refs[depth:]
    count = out.shape[2]
    for d, active in enumerate(actives):
        from_z = lax.rem(place[AT_Z] - d + depth, depth)
        rows = dot_nt(active[...], weight[...])
        for i, other in enumerate((0, 2, 1, 3)):
            out[place[AT_U] ^ other, from_z] = rows[i * count : (i + 1) * count].astype(BF16)


def sort_rows_kernel(place, mine, far, own, near, rows):
    share = own.shape[1]
    for z in range(mine.shape[0]):
        rows[z * PAIR + place[AT_X]] = mine[z]
        rows[z * PAIR + 1 - place[AT_X]] = far[z]

    def part(m):
        return rows[pl.ds((place[AT_U] ^ m) * share, share)]

    own[0], own[1] = part(0), part(1)
    near[0], near[1] = part(2), part(3)


def place_rows_kernel(place, own, near, across, out):
    out[:, place[AT_U]] = own[0]
    out[:, place[AT_U] ^ 2] = near[0]
    out[:, place[AT_U] ^ 1] = across[0]
    out[:, place[AT_U] ^ 3] = across[1]


def choose_kernel(place, *refs):
    shares, (keep, send) = refs[:-2], refs[-2:]
    for i, share in enumerate(shares):
        keep[:, i] = share[:, place[AT_X]]
        send[:, i] = share[:, 1 - place[AT_X]]


def fold_kernel(depth, place, keep, got, *outs):
    for d in range(depth):
        at = lax.rem(place[AT_Z] + d, depth)
        outs[d][...] = (keep[at].astype(F32) + got[at].astype(F32)).astype(BF16)


def split_uly_kernel(place, pieces, own, near):
    total = None
    parts = []
    for m in range(4):
        total = None
        for z in range(pieces.shape[0]):
            part = pieces[z, 0, place[AT_U] ^ m].astype(F32)
            total = part if total is None else total + part
        parts.append(total.astype(BF16))
    own[0], own[1], near[0], near[1] = parts


def pick_uly_kernel(place, share, own, near):
    own[0], own[1] = share[:, place[AT_U]], share[:, place[AT_U] ^ 1]
    near[0], near[1] = share[:, place[AT_U] ^ 2], share[:, place[AT_U] ^ 3]


def group_rows_kernel(place, own, near, across, keep, send, rows):
    share = own.shape[1]
    for m, part in ((0, own[0]), (2, near[0]), (1, across[0]), (3, across[1])):
        rows[pl.ds((place[AT_U] ^ m) * share, share)] = part
    for z in range(keep.shape[0]):
        keep[z, 0] = rows[z * PAIR + place[AT_X]]
        send[z, 0] = rows[z * PAIR + 1 - place[AT_X]]


def finish_qkv_kernel(place, *refs):
    heads, kinds = refs[:3], refs[3:6]
    weight, gain, grad, grad_gain, bias, head_parts, kind_parts = refs[6:]
    width, side = heads[0].shape[2], heads[0].shape[2] * 4
    for parts, (own, near, across) in ((head_parts, heads), (kind_parts, kinds)):
        parts[place[AT_U]] = own[0]
        parts[place[AT_U] ^ 2] = near[0]
        parts[place[AT_U] ^ 1] = across[0]
        parts[place[AT_U] ^ 3] = across[1]
    total = jnp.zeros(grad_gain.shape, F32)
    for u in range(4):
        bias[u] = kind_parts[u, :16].astype(F32)
        start = side + (u % 2) * KV_HEADS * HEAD_DIM + (u // 2) * HEAD_DIM
        for at, part in (
            (slice(u * width, (u + 1) * width), head_parts[u]),
            (slice(start, start + HEAD_DIM), kind_parts[u, 16:]),
        ):
            part = part.astype(F32)
            grad[:, at] = part * gain[...]
            total = total + jnp.sum(part * weight[:, at].astype(F32), axis=1, keepdims=True)
    grad_gain[...] = total


def finish_kernel(depth, gates, uppers, downs, gate, upper, gain, grad_gate, grad_upper, grad_down, grad_gain):
    units = downs.shape[3]
    total = jnp.zeros(grad_gain.shape, F32)
    for k in range(depth):
        at = slice(k * units, (k + 1) * units)
        part = gates[k, 0].astype(F32)
        grad_gate[:, at] = part * gain[...]
        total = total + jnp.sum(part * gate[:, at].astype(F32), axis=1, keepdims=True)
        part = uppers[k, 0].astype(F32)
        grad_upper[:, at] = part * gain[...]
        total = total + jnp.sum(part * upper[:, at].astype(F32), axis=1, keepdims=True)
        grad_down[:, at] = downs[k, 0].astype(F32)
    grad_gain[...] = total


def like(shape, kind=BF16):
    return jax.ShapeDtypeStruct(shape, kind)


def together(*values):
    return lax.optimization_barrier(values)


def after(value, *others):
    return lax.optimization_barrier((value, others))[0]


class Grid:
    def __init__(self):
        self.blocks = lax.axis_size("blk")
        self.ulys = lax.axis_size("uly")
        self.depth = self.blocks // PAIR
        self.b = lax.axis_index("blk")
        self.u = lax.axis_index("uly")
        self.z = self.b // PAIR
        self.x = self.b % PAIR
        self.y = self.u // 2
        self.c = self.u % 2

    def to_z(self, value, step):
        pairs = [
            (z * PAIR + x, ((z + step) % self.depth) * PAIR + x)
            for z in range(self.depth)
            for x in range(PAIR)
        ]
        return lax.ppermute(value, "blk", pairs)

    def swap_x(self, value):
        return lax.ppermute(value, "blk", [(i, i ^ 1) for i in range(self.blocks)])

    def swap_y(self, value):
        return lax.ppermute(value, "uly", [(i, i ^ 2) for i in range(self.ulys)])

    def swap_both(self, value):
        return lax.ppermute(value, "uly", [(i, i ^ 3) for i in range(self.ulys)])

    def swap_core(self, value):
        return lax.ppermute(value, "uly", [(i, i ^ 1) for i in range(self.ulys)])


def paired(bit, mine, other, axis):
    low = jnp.where(bit == 0, mine, other)
    high = jnp.where(bit == 0, other, mine)
    return jnp.stack([low, high], axis=axis)


def pick(bit, array, axis):
    low = lax.index_in_dim(array, 0, axis, keepdims=False)
    high = lax.index_in_dim(array, 1, axis, keepdims=False)
    return jnp.where(bit == 0, low, high), jnp.where(bit == 0, high, low)


def order_z(grid, pieces):
    stacked = jnp.stack(pieces[::-1] + pieces[::-1][:-1])
    start = (grid.depth - 1 - grid.z) % grid.depth
    return lax.dynamic_slice_in_dim(stacked, start, grid.depth, 0)


def gather_uly(grid, value):
    both = paired(grid.y, value, grid.swap_y(value), 0)
    every = paired(grid.c, both, grid.swap_core(both), 1)
    return every.reshape((grid.ulys,) + value.shape)


def scatter_uly(grid, parts, kind=BF16):
    parts = parts.reshape((2, 2) + parts.shape[1:])
    keep, send = pick(grid.c, parts, 1)
    both = keep.astype(F32) + grid.swap_core(send.astype(kind)).astype(F32)
    keep, send = pick(grid.y, both, 0)
    return keep + grid.swap_y(send.astype(kind)).astype(F32)


def gather_blk(grid, value):
    pieces = [value] + [grid.to_z(value, d) for d in range(1, grid.depth)]
    pairs = [paired(grid.x, piece, grid.swap_x(piece), 0) for piece in pieces]
    return order_z(grid, pairs)


def exchange_z(grid, parts):
    pieces = [lax.dynamic_index_in_dim(parts, grid.z, 0, keepdims=False)]
    for d in range(1, grid.depth):
        there = (grid.z + d) % grid.depth
        pieces.append(grid.to_z(lax.dynamic_index_in_dim(parts, there, 0, keepdims=False), d))
    return pieces


def exchange_z_all(grid, parts):
    groups = [[z * PAIR + x for z in range(grid.depth)] for x in range(PAIR)]
    return lax.all_to_all(
        parts, "blk", split_axis=0, concat_axis=0, axis_index_groups=groups, tiled=True
    )


def spread_z(grid, value):
    return exchange_z_all(grid, jnp.broadcast_to(value, (grid.depth, *value.shape)))


def exchange_uly(parts):
    return lax.all_to_all(parts, "uly", split_axis=0, concat_axis=0, tiled=True)


def per_device(
    tokens,
    span_order,
    attn_gain,
    qkv_weight,
    qkv_bias,
    out_weight,
    ffn_gain,
    gate_weight,
    up_weight,
    down_weight,
    cotangent,
):
    grid = Grid()
    local_rows, seqs, model = tokens.shape
    count = local_rows * seqs
    ulys = grid.ulys
    depth = grid.depth
    blocks = grid.blocks
    cycle_rows = local_rows * ulys
    spans = cycle_rows // SPAN
    slots = blocks * spans
    group = HEADS // ulys
    factor = 1.0 / math.sqrt(HEAD_DIM)
    width = group * HEAD_DIM
    columns = width + HEAD_DIM
    shard = qkv_weight.shape[0]
    block_model = shard * ulys
    chunk = math.gcd(slots, 4) * SPAN
    side = HEADS * HEAD_DIM
    place = jnp.stack([grid.z, grid.x, grid.y, grid.c, grid.b, grid.u]).astype(jnp.int32)

    def by_seq(array):
        return jnp.transpose(array, (1, 0, 2)).reshape(count, model)

    def by_row(array):
        return jnp.transpose(array.reshape(seqs, local_rows, model), (1, 0, 2))

    def by_uly(array):
        lead = array.shape[0]
        heads = array[:, :side].reshape(lead, ulys, width)
        kinds = array[:, side:].reshape(lead, 2, KV_HEADS, HEAD_DIM)
        kinds = jnp.transpose(kinds, (0, 2, 1, 3)).reshape(lead, ulys, HEAD_DIM)
        return jnp.transpose(jnp.concatenate([heads, kinds], axis=-1), (1, 0, 2))

    rows = by_seq(tokens).astype(F32)
    unit_one, factor_one = norm_rows(rows)
    unit_own = unit_one.astype(BF16)
    unit_near = grid.swap_y(unit_own)
    gain_one = attn_gain.astype(F32)[:, None]
    scaled = (qkv_weight.astype(F32) * gain_one).astype(BF16)
    heads_share = blocks // ulys
    owned_columns = qkv_bias.shape[0]
    column_start = (grid.b * ulys + grid.u) * owned_columns
    bias_row = lax.dynamic_update_slice(
        jnp.zeros((16, owned_columns * blocks * ulys), BF16),
        jnp.pad(qkv_bias[None], ((0, 15), (0, 0))),
        (0, column_start),
    )
    by_head = by_uly(jnp.concatenate([scaled, bias_row], axis=0))
    by_head = exchange_uly(by_head)
    block_rows = jnp.concatenate(
        [by_head[:, :shard].reshape(block_model, columns), jnp.sum(by_head[:, shard:], axis=0)],
        axis=0,
    )
    qkv_mine = [block_rows] + [grid.to_z(block_rows, d) for d in range(1, depth)]
    first_far = grid.swap_x(block_rows)
    first_arrived = qkv_mine[1]
    *qkv_mine, first_far, unit_near = together(*qkv_mine, first_far, unit_near)

    gain_two = ffn_gain.astype(F32)[:, None]
    hidden_units = gate_weight.shape[1] // depth
    order = sorted(range(1, depth), key=lambda d: (min(d, depth - d), d))
    early, middle, late = order[0], order[1:-1], order[-1]
    split_in = after((gate_weight, up_weight, down_weight), first_arrived)
    split_in = (*split_in[:2], split_in[2].T)
    tile_pieces = call(
        functools.partial(split_tiles_kernel, depth),
        [place],
        [*split_in, gain_two],
        [like((3, block_model, hidden_units))] * depth,
        scratch=[pltpu.VMEM((depth, 3, block_model, hidden_units), BF16)],
    )
    qkv_far = [first_far] + [grid.swap_x(piece) for piece in qkv_mine[1:]]
    unit_across = grid.swap_core(jnp.stack([unit_own, unit_near]))
    out_first, early_piece = after((out_weight, tile_pieces[early]), *qkv_mine[1:])
    tile_mine = {0: tile_pieces[0], early: grid.to_z(early_piece, early)}
    out_mine = spread_z(grid, out_first)
    tile_far = {0: grid.swap_x(after(tile_pieces[0], qkv_far[1]))}
    *qkv_far, unit_across = together(*qkv_far, unit_across)
    unit_parts = (unit_own, unit_near, unit_across)

    head_rows = grid.b * cycle_rows + jnp.arange(cycle_rows, dtype=jnp.int32)
    places = positions(span_order, head_rows).reshape(seqs, ulys, local_rows)
    places = jnp.transpose(places, (1, 0, 2)).reshape(ulys, count)
    cosine, sine = rope_tables(places)
    units, qkv_part, query, kind = call(
        functools.partial(mix_kernel, depth, group),
        [place],
        [*unit_parts, cosine, sine, *qkv_mine, *qkv_far],
        [
            like((ulys, count, model)),
            like((blocks, block_model, columns)),
            like((ulys, count, width)),
            like((ulys, count, HEAD_DIM)),
        ],
        scratch=[
            pltpu.VMEM((blocks, 16, columns), BF16),
            pltpu.SemaphoreType.DMA((2 * blocks + ulys,)),
        ],
        far=(0, 1, 2, *range(5, 2 * depth + 5)),
    )
    units = units.reshape(ulys * count, model)
    qkv_part = qkv_part.reshape(model, columns)
    kinds = [kind] + [grid.to_z(kind, d) for d in range(1, depth)]
    out_mine, cot_flat = after((out_mine, by_seq(cotangent)), kind)
    out_far = grid.swap_x(out_mine)
    cot_first = cot_flat
    cot_near = grid.swap_y(cot_first)
    *held, late_pair, late_down = after(
        (*[tile_pieces[d] for d in middle], tile_pieces[late][:2], tile_pieces[late][2:]), kinds[1]
    )
    for d, piece in zip(middle, held):
        tile_mine[d] = grid.to_z(piece, d)
    out_far, cot_near, tile_mine[early], tile_far[0], *kinds = together(
        out_far, cot_near, tile_mine[early], tile_far[0], *kinds
    )
    late_pair = grid.to_z(after(late_pair, kinds[-1]), late)

    a_own = jnp.stack(kinds)
    a_far = grid.swap_x(a_own)
    b_own = grid.swap_core(a_own)
    out_own, out_near = call(
        sort_rows_kernel,
        [place],
        [out_mine, out_far],
        [like((2, heads_share, shard, model))] * 2,
        scratch=[pltpu.VMEM((blocks, shard, model), BF16)],
    )
    out_near = grid.swap_y(out_near)
    a_far, b_own, out_near, *held = together(
        a_far, b_own, out_near, *[tile_mine[d] for d in middle]
    )
    tile_mine.update(zip(middle, held))

    b_far = grid.swap_core(a_far)
    out_across = grid.swap_core(jnp.stack([out_own[1], out_near[1]]))
    tile_far[early] = grid.swap_x(after(tile_mine[early], a_far))
    b_far, out_across = together(b_far, out_across)

    def over_uly(piece):
        both = jnp.concatenate([piece, grid.swap_y(piece)], axis=0)
        return jnp.concatenate([both, grid.swap_core(both)], axis=0)

    grad_rows = cot_flat.astype(F32)

    scale = factor * LOG2E
    kv_shape = (depth, ulys, seqs, local_rows, HEAD_DIM)
    kv_spec = pl.BlockSpec(
        (depth, ulys, 1, local_rows, HEAD_DIM), lambda s, *unused: (0, 0, s, 0, 0)
    )
    heads_shape = (ulys, seqs, local_rows, width)
    heads_spec = pl.BlockSpec((ulys, 1, local_rows, width), lambda s, *unused: (0, s, 0, 0))
    lse_spec = pl.BlockSpec((1, spans, 1, group * SPAN), lambda s, *unused: (s, 0, 0, 0))
    table_shape = (ulys, seqs, local_rows, HEAD_DIM)
    table_spec = pl.BlockSpec((ulys, 1, local_rows, HEAD_DIM), lambda s, *unused: (0, s, 0, 0))
    sorted_spec = pl.BlockSpec((1, 2, slots * SPAN, HEAD_DIM), lambda s, *unused: (s, 0, 0, 0))
    params = pltpu.CompilerParams(vmem_limit_bytes=VMEM_LIMIT)
    query = query.reshape(heads_shape)
    attended, lse, kv = pl.pallas_call(
        functools.partial(attend_kernel, depth, spans, chunk, group, scale),
        grid_spec=pltpu.PrefetchScalarGridSpec(
            num_scalar_prefetch=2,
            grid=(seqs,),
            in_specs=[heads_spec] + [kv_spec] * 4,
            out_specs=[heads_spec, lse_spec, sorted_spec],
        ),
        out_shape=[
            like(heads_shape),
            like((seqs, spans, 1, group * SPAN), F32),
            like((seqs, 2, slots * SPAN, HEAD_DIM)),
        ],
        compiler_params=params,
        cost_estimate=SMALL,
    )(span_order, place, query, *[part.reshape(kv_shape) for part in (a_own, a_far, b_own, b_far)])
    flat = attended.reshape(ulys, count, width)
    out_own, tile_far[early], late_pair, attended = together(
        out_own, tile_far[early], late_pair, attended
    )
    late_down = grid.to_z(after(late_down, attended), late)
    flat = attended.reshape(ulys, count, width)
    for d in middle:
        tile_far[d] = grid.swap_x(after(tile_mine[d], attended))
    (out_part,) = call(
        place_rows_kernel, [place], [out_own, out_near, out_across], [like((heads_share, ulys, shard, model))]
    )
    out_part = out_part.reshape(width, model)
    keep, send = call(
        functools.partial(project_kernel, False),
        [place],
        [flat, out_part],
        [like((2, count, model), F32), like((2, count, model))],
    )
    got = grid.swap_core(send)
    both = keep + got.astype(F32)
    got = grid.swap_y(both[1].astype(BF16))
    got, late_down, *held = together(got, late_down, *[tile_far[d] for d in middle])
    tile_mine[late] = jnp.concatenate([late_pair, late_down])
    tile_far.update(zip(middle, held))
    tile_far[late] = grid.swap_x(after(tile_mine[late], got))
    hidden = rows + both[0] + got.astype(F32)

    unit_two, factor_two = norm_rows(hidden)
    mid_own = unit_two.astype(BF16)
    mid_near = grid.swap_y(mid_own)
    mid_pieces = [mid_own, grid.to_z(mid_own, 1)]
    cot_pieces = [cot_first, grid.to_z(after(cot_first, got), 1)]
    mid_near, tile_far[late] = together(mid_near, tile_far[late])
    for d in range(2, depth):
        mid_pieces.append(grid.to_z(mid_pieces[-1], 1))
        cot_pieces.append(grid.to_z(cot_pieces[-1], 1))

    def chunk_of(own, near):
        both = jnp.concatenate([own, near], axis=0)
        return jnp.concatenate([both, grid.swap_core(both)], axis=0)

    mid_chunks = [chunk_of(mid_own, mid_near)] + [over_uly(piece) for piece in mid_pieces[1:]]
    cot_chunks = [chunk_of(cot_first, cot_near)] + [over_uly(piece) for piece in cot_pieces[1:]]
    gate_used, upper_used, down_used = [
        tile.reshape(model, hidden_units)
        for tile in call(
            functools.partial(merge_tiles_kernel, depth),
            [place],
            [tile_mine[d] for d in range(depth)] + [tile_far[d] for d in range(depth)],
            [like((blocks, block_model, hidden_units))] * 3,
        )
    ]
    actives, gate_grads, upper_grads, back_chunks = [], [], [], []
    for mid, cot in zip(mid_chunks, cot_chunks):
        gate = matmul(mid, gate_used)
        upper = matmul(mid, upper_used)
        sigmoid = jax.nn.sigmoid(gate)
        active_grad = matmul(cot, down_used)
        actives.append((gate * sigmoid * upper).astype(BF16))
        gate_grad = (active_grad * upper * sigmoid * (1.0 + gate * (1.0 - sigmoid))).astype(BF16)
        upper_grad = (active_grad * gate * sigmoid).astype(BF16)
        gate_grads.append(gate_grad)
        upper_grads.append(upper_grad)
        back_chunks.append(
            contract_cols(gate_grad, gate_used) + contract_cols(upper_grad, upper_used)
        )
    def over_core(chunk):
        chunk = chunk.reshape(2, 2, count, model)
        return chunk[0].astype(F32) + grid.swap_core(chunk[1].astype(BF16)).astype(F32)

    def over_y(both):
        return both[0] + grid.swap_y(both[1].astype(BF16)).astype(F32)

    def halve(shares, rows):
        shape = (depth, PAIR, *rows, shares[0].shape[-1])
        shares = [share.astype(BF16).reshape(shape) for share in shares]
        half = like((depth, len(shares), *rows, shape[-1]))
        return call(choose_kernel, [place], shares, [half] * 2)

    def fold(keep, got):
        return exchange_z_all(grid, (keep.astype(F32) + got.astype(F32)).astype(BF16))

    z_groups = [[z * PAIR + x for z in range(depth)] for x in range(PAIR)]
    tile_rows = (block_model,)
    boths = [over_core(chunk) for chunk in back_chunks]
    mid_parts = [over_y(both) for both in boths]
    back_pieces = [grid.to_z(mid_parts[d].astype(BF16), -d) for d in range(1, depth)]
    mid_all = jnp.concatenate(mid_chunks)
    mid_now = after(mid_all, back_chunks[-1], *boths[:-1], *mid_parts[:-1])
    gate_keep, gate_send = halve([contract_rows(mid_now, jnp.concatenate(gate_grads))], tile_rows)
    mid_now = after(mid_all, gate_send, *mid_parts, back_pieces[0])
    upper_keep, upper_send = halve([contract_rows(mid_now, jnp.concatenate(upper_grads))], tile_rows)
    gate_got = grid.swap_x(gate_send)
    first, gate_got, upper_send, *back_pieces = together(
        mid_parts[0], gate_got, upper_send, *back_pieces
    )
    mid_grad = first + sum(piece.astype(F32) for piece in back_pieces)

    hidden_grad = grad_rows + norm_back(mid_grad, unit_two, factor_two)
    branch_own = hidden_grad.astype(BF16)
    branch_near = grid.swap_y(branch_own)
    upper_got = grid.swap_x(after(upper_send, gate_got))
    gate_owned = fold(*after((gate_keep, gate_got), branch_own))
    held = after((*cot_chunks, *actives), branch_own)
    cot_all, active_all = [jnp.concatenate(part) for part in (held[:depth], held[depth:])]
    down_keep, down_send = halve([contract_rows(cot_all, active_all)], tile_rows)
    down_send, branch_near, upper_got = together(down_send, branch_near, upper_got)
    down_got = grid.swap_x(down_send)
    branch_across = grid.swap_core(jnp.stack([branch_own, branch_near]))
    branch_parts = (branch_own, branch_near, branch_across)
    (grad_heads,) = call(
        heads_grad_kernel, [place], [*branch_parts, out_part], [like((ulys, count, width))]
    )

    grad_heads, gate_owned = together(grad_heads.reshape(heads_shape), gate_owned)
    upper_owned = fold(*after((upper_keep, upper_got), gate_owned))
    both_spec = pl.BlockSpec(
        (2, depth, ulys, 1, local_rows, HEAD_DIM), lambda s, *unused: (0, 0, 0, s, 0, 0)
    )
    query_grad, keep_own, keep_far, send_both = pl.pallas_call(
        functools.partial(attend_back_kernel, depth, spans, chunk, group, scale, factor),
        grid_spec=pltpu.PrefetchScalarGridSpec(
            num_scalar_prefetch=2,
            grid=(seqs,),
            in_specs=[heads_spec, sorted_spec]
            + [heads_spec] * 2
            + [lse_spec]
            + [table_spec] * 2,
            out_specs=[heads_spec] + [kv_spec] * 2 + [both_spec],
            scratch_shapes=[pltpu.VMEM((2, slots * SPAN, HEAD_DIM), F32)],
        ),
        out_shape=[like(heads_shape)] + [like(kv_shape)] * 2 + [like((2, *kv_shape))],
        compiler_params=params,
        cost_estimate=SMALL,
    )(
        span_order,
        place,
        query,
        kv,
        grad_heads,
        attended,
        lse,
        cosine.reshape(table_shape),
        sine.reshape(table_shape),
    )
    got_far, got_own = [
        jnp.concatenate([grid.swap_core(part) for part in jnp.split(send_both[k], 2, axis=0)])
        for k in (1, 0)
    ]
    query_grad = query_grad.reshape(ulys * count, width)
    got_far, got_own, query_grad, upper_owned = together(
        got_far, got_own, query_grad, upper_owned
    )
    (out_all,) = call(
        functools.partial(down_kernel, depth),
        [place],
        [*after(tuple(actives), got_far), down_used],
        [like((ulys, depth, count, model))],
    )
    from_x = grid.swap_x((keep_far.astype(F32) + got_far.astype(F32)).astype(BF16))
    share_parts = after(branch_parts, got_far)
    (out_share,) = call(out_share_kernel, [place], [*share_parts, flat], [like((width, model))])
    out_own, out_near = call(
        pick_uly_kernel,
        [place],
        [out_share.reshape(heads_share, ulys, shard, model)],
        [like((2, heads_share, shard, model))] * 2,
    )
    head_keep, head_send = halve([contract_rows(units, query_grad)], (ulys, shard))
    from_x, head_send, out_near, out_all, down_got = together(
        from_x, head_send, out_near, out_all, down_got
    )
    out_all = lax.psum_scatter(out_all, "uly", scatter_dimension=0, tiled=False)
    kind_parts = keep_own.astype(F32) + got_own.astype(F32) + from_x.astype(F32)
    kind_parts = kind_parts.astype(BF16)
    kind_back = [grid.to_z(kind_parts[d], -d) for d in range(1, depth)]
    head_got = grid.swap_x(head_send)
    out_near = grid.swap_y(out_near)
    *kind_back, out_near, kind_parts, head_got = together(
        *kind_back, out_near, kind_parts, head_got
    )
    out_across = grid.swap_core(jnp.stack([out_own[1], out_near[1]]))
    kind_grad = kind_parts[0].astype(F32)
    for piece in kind_back:
        kind_grad = kind_grad + piece.astype(F32)
    kind_grad = kind_grad.reshape(ulys * count, HEAD_DIM)
    turned = jnp.roll(kind_grad, HEAD_DIM // 2, axis=1)
    is_key = grid.c == 0
    flat_cosine = cosine.reshape(ulys * count, HEAD_DIM)
    flat_sine = sine.reshape(ulys * count, HEAD_DIM)
    kind_grad = jnp.where(is_key, kind_grad * flat_cosine - turned * flat_sine, kind_grad)
    kind_grad = kind_grad.astype(BF16)

    bias = jnp.sum(query_grad.astype(F32), axis=0).reshape(group, HEAD_DIM)
    bias = jnp.concatenate([bias, jnp.sum(kind_grad.astype(F32), axis=0)[None]], axis=0)
    bias = jnp.pad(bias.astype(BF16), ((0, 16 - group - 1), (0, 0)))
    bias = jnp.broadcast_to(bias, (blocks, ulys, 16, HEAD_DIM))
    share = contract_rows(units, kind_grad).astype(BF16)
    share = share.reshape(blocks, ulys, shard, HEAD_DIM)
    share = jnp.concatenate([bias, share], axis=2)
    kind_keep, kind_send = halve([share], (ulys, shard + 16))
    kind_got = grid.swap_x(kind_send)
    out_all = lax.psum_scatter(
        after(out_all, kind_send), "blk", scatter_dimension=0, axis_index_groups=z_groups, tiled=False
    )
    head_pieces = fold(*after((head_keep, head_got), kind_send))
    out_across = after(out_across, kind_send)
    out_keep, out_send = call(
        group_rows_kernel,
        [place],
        [out_own, out_near, out_across],
        [like((depth, 1, shard, model))] * 2,
        scratch=[pltpu.VMEM((blocks, shard, model), BF16)],
    )
    out_got = grid.swap_x(after(out_send, kind_got))
    kind_pieces = call(
        functools.partial(fold_kernel, depth),
        [place],
        [kind_keep, kind_got],
        [like(kind_keep.shape[1:])] * depth,
    )
    kind_pieces = [kind_pieces[0]] + [grid.to_z(kind_pieces[d], d) for d in range(1, depth)]
    kind_pieces = jnp.stack(kind_pieces)
    kind_pieces, out_got = together(kind_pieces, out_got)
    kind_now = after(kind_grad, kind_pieces)
    keep, send = call(
        functools.partial(project_kernel, True),
        [place],
        [
            query_grad.reshape(ulys, count, width),
            kind_now.reshape(ulys, count, HEAD_DIM),
            qkv_part[:, :width],
            qkv_part[:, width:],
        ],
        [like((2, count, model), F32), like((2, count, model))],
    )
    both = keep + grid.swap_core(send).astype(F32)
    down_owned = fold(*after((down_keep, down_got), head_pieces))
    out_pieces = call(
        functools.partial(fold_kernel, depth),
        [place],
        [out_keep, out_got],
        [like(out_keep.shape[1:])] * depth,
    )
    out_pieces = [out_pieces[0]] + [grid.to_z(out_pieces[d], d) for d in range(1, depth)]

    def to_owners(pieces):
        own, near = call(
            split_uly_kernel, [place], [pieces], [like((2, *pieces.shape[3:]))] * 2
        )
        near = grid.swap_y(near)
        return own, near, grid.swap_core(jnp.stack([own[1], near[1]]))

    head_owned = to_owners(head_pieces)
    kind_owned = to_owners(kind_pieces)
    grad_qkv, grad_gain_one, bias = call(
        finish_qkv_kernel,
        [place],
        [*head_owned, *kind_owned, qkv_weight, gain_one],
        [
            like(qkv_weight.shape, F32),
            like((shard, 1), F32),
            like((ulys, 16, HEAD_DIM), F32),
        ],
        scratch=[
            pltpu.VMEM((ulys, shard, width), BF16),
            pltpu.VMEM((ulys, shard + 16, HEAD_DIM), BF16),
        ],
    )
    grad_gain_one = grad_gain_one[:, 0]
    kind_bias = bias[:, group].reshape(KV_HEADS, 2, HEAD_DIM)
    bias = jnp.concatenate(
        [bias[:, :group].reshape(-1), jnp.transpose(kind_bias, (1, 0, 2)).reshape(-1)]
    )
    grad_bias = lax.dynamic_slice_in_dim(bias, column_start, owned_columns, 0)
    grad_out = sum(piece[0].astype(F32) for piece in out_pieces)
    result = hidden + after(out_all, grad_qkv).astype(F32)
    output = by_row(result.astype(BF16))
    normed_grad = both[0] + grid.swap_y(both[1].astype(BF16)).astype(F32)
    grad_tokens = by_row(hidden_grad + norm_back(normed_grad, unit_one, factor_one))
    tile_shape = gate_weight.shape
    grad_gate, grad_upper, grad_down, gain_part = call(
        functools.partial(finish_kernel, depth),
        [],
        [gate_owned, upper_owned, after(down_owned, grad_qkv), gate_weight, up_weight, gain_two],
        [like(tile_shape, F32)] * 3 + [like((block_model, 1), F32)],
    )
    grad_down = grad_down.T
    grad_gain_two = scatter_uly(grid, gain_part.reshape(ulys, -1), F32)
    return (
        output,
        grad_tokens,
        grad_gain_one,
        grad_qkv,
        grad_bias,
        grad_out,
        grad_gain_two.reshape(-1),
        grad_gate,
        grad_upper,
        grad_down,
    )


def solution(mesh):
    in_specs = (
        P(("blk", "uly"), None, None),
        P(),
        P(("blk", "uly")),
        P(("blk", "uly"), None),
        P(("blk", "uly")),
        P(("blk", "uly"), None),
        P("blk"),
        P("blk", "uly"),
        P("blk", "uly"),
        P("uly", "blk"),
        P(("blk", "uly"), None, None),
    )
    out_specs = (
        P(("blk", "uly"), None, None),
        P(("blk", "uly"), None, None),
        P(("blk", "uly")),
        P(("blk", "uly"), None),
        P(("blk", "uly")),
        P(("blk", "uly"), None),
        P(("blk", "uly")),
        P("blk", "uly"),
        P("blk", "uly"),
        P("uly", "blk"),
    )
    return jax.shard_map(
        per_device, mesh=mesh, in_specs=in_specs, out_specs=out_specs, check_vma=False
    )
```

```python
import functools
import math

import jax
import jax.numpy as jnp
from jax import lax
from jax.experimental import pallas as pl
from jax.experimental.pallas import tpu as pltpu
from jax.sharding import PartitionSpec as P

HEADS = 12
KV_HEADS = 2
HEAD_DIM = 128
SPAN = 128
PAIR = 2


EPS = 1e-06
THETA = 1000000.0
FLOOR = -1e30
LOG2E = 1.4426950408889634
BF16 = jnp.bfloat16
F32 = jnp.float32
SMALL = pl.CostEstimate(flops=1, transcendentals=0, bytes_accessed=1)
VMEM_LIMIT = 48 * 1024 * 1024

def norm_rows(rows):
    factor = lax.rsqrt(jnp.mean(rows * rows, axis=-1, keepdims=True) + EPS)
    return (rows * factor, factor)


def norm_back(scaled, unit, factor):
    return factor * (scaled - unit * jnp.mean(scaled * unit, axis=-1, keepdims=True))


def matmul(left, right):
    return jnp.dot(left, right, preferred_element_type=F32)


def contract_rows(left, right):
    return lax.dot_general(left, right, (((0,), (0,)), ((), ())), preferred_element_type=F32)


def contract_cols(left, right):
    return lax.dot_general(left, right, (((1,), (1,)), ((), ())), preferred_element_type=F32)


def positions(order, rows):
    table = jnp.arange(order.shape[1], dtype=jnp.int32)
    slots = rows // SPAN
    picked = jnp.where(slots[None, :, None] == table[None, None, :], order[:, None, :], 0)
    return jnp.sum(picked, axis=-1) * SPAN + (rows % SPAN)[None, :]


def rope_tables(places):
    index = jnp.arange(HEAD_DIM // 2).astype(F32)
    freq = THETA ** (-2.0 * index / HEAD_DIM)
    angle = places.astype(F32)[..., None] * freq
    cosine, sine = jnp.cos(angle), jnp.sin(angle)
    cosine = jnp.concatenate([cosine, cosine], axis=-1)
    return (cosine, jnp.concatenate([-sine, sine], axis=-1))


def dot_nn(left, right):
    return lax.dot_general(left, right, (((1,), (0,)), ((), ())), preferred_element_type=F32)


def dot_nt(left, right):
    return lax.dot_general(left, right, (((1,), (1,)), ((), ())), preferred_element_type=F32)


def dot_tn(left, right):
    return lax.dot_general(left, right, (((0,), (0,)), ((), ())), preferred_element_type=F32)


def call(kernel, scalars, arrays, outs, **options):
    return pl.pallas_call(
        kernel,
        grid_spec=pltpu.PrefetchScalarGridSpec(
            num_scalar_prefetch=len(scalars),
            grid=(1,),
            in_specs=[
                pl.BlockSpec(memory_space=pltpu.HBM) if i in options.get("far", ()) else whole(array.shape)
                for i, array in enumerate(arrays)
            ],
            out_specs=[whole(out.shape) for out in outs],
            scratch_shapes=options.get("scratch", ()),
        ),
        out_shape=outs,
        compiler_params=pltpu.CompilerParams(vmem_limit_bytes=VMEM_LIMIT),
        cost_estimate=SMALL,
    )(*scalars, *arrays)


def whole(shape):
    return pl.BlockSpec(shape, lambda *unused: (0,) * len(shape))


def turn(field):
    return pltpu.roll(field, HEAD_DIM // 2, 1)


AT_Z, AT_X, AT_Y, AT_C, AT_B, AT_U = range(6)


def mix_kernel(depth, group, place, own, near, across, cosine, sine, *rest):
    pieces, far = rest[:depth], rest[depth : 2 * depth]
    units, weights, query, kind, bias_rows, flags = rest[2 * depth :]
    u = place[AT_U]
    rows = weights.shape[1]
    copies = []

    def bring(source, target):
        copies.append(pltpu.make_async_copy(source, target, flags.at[len(copies)]))
        copies[-1].start()

    for d in range(depth):
        from_z = lax.rem(place[AT_Z] - d + depth, depth)
        for k in range(PAIR):
            piece = far[d] if k else pieces[d]
            from_x = place[AT_X] if k == 0 else 1 - place[AT_X]
            bring(piece.at[pl.ds(0, rows)], weights.at[from_z * PAIR + from_x])
            bring(piece.at[pl.ds(rows, 16)], bias_rows.at[PAIR * d + k])
    bring(own, units.at[u])
    bring(near, units.at[u ^ 2])
    bring(across.at[0], units.at[u ^ 1])
    bring(across.at[1], units.at[u ^ 3])
    for copy in copies:
        copy.wait()
    bias = jnp.sum(bias_rows[...].astype(F32), axis=(0, 1))[None]
    model = units.shape[2]
    all_weights = weights[...].reshape(model, weights.shape[2])
    is_key = place[AT_C] == 0
    for i in range(units.shape[0]):
        mixed = dot_nn(units[i], all_weights) + bias
        cos, sin = cosine[i], sine[i]
        for h in range(group):
            field = mixed[:, h * HEAD_DIM : (h + 1) * HEAD_DIM]
            query[i, :, h * HEAD_DIM : (h + 1) * HEAD_DIM] = (field * cos + turn(field) * sin).astype(
                BF16
            )
        field = mixed[:, group * HEAD_DIM :]
        turned = field * cos + turn(field) * sin
        kind[i] = jnp.where(is_key, turned, field).astype(BF16)


def stack_heads(block, group):
    block = block.reshape(SPAN, group * HEAD_DIM)
    return jnp.concatenate(
        [block[:, h * HEAD_DIM : (h + 1) * HEAD_DIM] for h in range(group)], axis=0
    )


def key_mask(first_key, keys, place, group):
    key = first_key + lax.broadcasted_iota(jnp.int32, (keys, group * SPAN), 0)
    row = lax.broadcasted_iota(jnp.int32, (keys, group * SPAN), 1) % SPAN
    return key <= place * SPAN + row


def attend_kernel(
    depth, spans, chunk, group, scale, order, place, query, a_own, a_far, b_own, b_far, out, lse, kv
):
    seq = pl.program_id(0)
    core, x, z = place[AT_C], place[AT_X], place[AT_Z]
    step = query.shape[0] // spans
    slots = depth * PAIR * spans

    def settle(slot, unused):
        blk, span = slot // spans, lax.rem(slot, spans)
        d = lax.rem(z - blk // PAIR + depth, depth)
        there = pl.ds(pl.multiple_of(order[seq, slot] * SPAN, SPAN), SPAN)
        here = pl.ds(span * step, step)
        for mine, other, far in ((a_own, b_own, False), (a_far, b_far, True)):

            @pl.when((lax.rem(blk, PAIR) != x) == far)
            def unused_copy():
                kv[0, core, there] = mine[d, here, 0].reshape(SPAN, HEAD_DIM)
                kv[0, 1 - core, there] = other[d, here, 0].reshape(SPAN, HEAD_DIM)

        return 0

    lax.fori_loop(0, slots, settle, 0)
    for span in range(spans):
        spot = order[seq, place[AT_B] * spans + span]
        queries = stack_heads(query[span * step : (span + 1) * step, 0], group)

        def advance(index, state, masked):
            peak, total, summed = state
            keys = pl.ds(pl.multiple_of(index * chunk, chunk), chunk)
            scores = dot_nt(kv[0, 0, keys], queries)
            if masked:
                allowed = key_mask(index * chunk, chunk, spot, group)
                scores = jnp.where(allowed, scores, FLOOR)
            new_peak = jnp.maximum(peak, jnp.max(scores, axis=0, keepdims=True))
            weights = jnp.exp2((scores - new_peak) * scale)
            fade = jnp.exp2((peak - new_peak) * scale)
            total = total * fade + jnp.sum(weights, axis=0, keepdims=True)
            summed = summed * fade + dot_tn(kv[0, 1, keys], weights.astype(BF16))
            return new_peak, total, summed

        start = (
            jnp.full((1, group * SPAN), FLOOR, F32),
            jnp.zeros((1, group * SPAN), F32),
            jnp.zeros((HEAD_DIM, group * SPAN), F32),
        )
        last = spot * SPAN // chunk
        state = lax.fori_loop(0, last, lambda i, s: advance(i, s, False), start)
        peak, total, summed = advance(last, state, True)
        lse[0, span] = peak * scale + jnp.log2(total)
        result = (summed / total).T.astype(BF16)
        for h in range(group):
            out[span * step : (span + 1) * step, 0, :, h * HEAD_DIM : (h + 1) * HEAD_DIM] = result[
                h * SPAN : (h + 1) * SPAN
            ].reshape(step, SPAN // step, HEAD_DIM)


def attend_back_kernel(
    depth,
    spans,
    chunk,
    group,
    scale,
    factor,
    order,
    place,
    query,
    kv,
    grad,
    out,
    lse,
    cosine,
    sine,
    query_grad,
    keep_own,
    keep_far,
    send_both,
    sums,
):
    seq = pl.program_id(0)
    core, x, z = place[AT_C], place[AT_X], place[AT_Z]
    step = query.shape[0] // spans
    slots = depth * PAIR * spans
    sums[...] = jnp.zeros(sums.shape, F32)
    for span in range(spans):
        spot = order[seq, place[AT_B] * spans + span]
        at = slice(span * step, (span + 1) * step)
        queries = stack_heads(query[at, 0], group)
        grads = stack_heads(grad[at, 0], group)
        results = stack_heads(out[at, 0], group)
        delta = jnp.sum(
            (grads.astype(F32) * results.astype(F32)).T, axis=0, keepdims=True
        )
        level = lse[0, span]

        def advance(index, total, masked):
            keys = pl.ds(pl.multiple_of(index * chunk, chunk), chunk)
            key, value = kv[0, 0, keys], kv[0, 1, keys]
            probs = jnp.exp2(dot_nt(key, queries) * scale - level)
            if masked:
                probs = jnp.where(key_mask(index * chunk, chunk, spot, group), probs, 0.0)
            score_grad = (probs * (dot_nt(value, grads) - delta)).astype(BF16)
            sums[1, keys] += dot_nn(probs.astype(BF16), grads)
            sums[0, keys] += dot_nn(score_grad, queries)
            return total + dot_tn(key, score_grad)

        last = spot * SPAN // chunk
        total = jnp.zeros((HEAD_DIM, group * SPAN), F32)
        total = lax.fori_loop(0, last, lambda i, s: advance(i, s, False), total)
        total = (advance(last, total, True) * factor).T
        cos = cosine[at, 0].reshape(SPAN, HEAD_DIM)
        sin = sine[at, 0].reshape(SPAN, HEAD_DIM)
        for h in range(group):
            field = total[h * SPAN : (h + 1) * SPAN]
            field = (field * cos - turn(field) * sin).astype(BF16)
            query_grad[at, 0, :, h * HEAD_DIM : (h + 1) * HEAD_DIM] = field.reshape(
                step, SPAN // step, HEAD_DIM
            )

    keep_scale = jnp.where(core == 0, factor, 1.0)
    send_scale = jnp.where(core == 0, 1.0, factor)

    def settle(slot, unused):
        blk, span = slot // spans, lax.rem(slot, spans)
        d = lax.rem(z - blk // PAIR + depth, depth)
        there = pl.ds(pl.multiple_of(order[seq, slot] * SPAN, SPAN), SPAN)
        here = pl.ds(span * step, step)
        shape = (step, SPAN // step, HEAD_DIM)
        for keep, send, far in ((keep_own, 0, False), (keep_far, 1, True)):

            @pl.when((lax.rem(blk, PAIR) != x) == far)
            def unused_copy():
                keep[d, here, 0] = (sums[core, there] * keep_scale).astype(BF16).reshape(shape)
                send_both[send, d, here, 0] = (sums[1 - core, there] * send_scale).astype(BF16).reshape(shape)

        return 0

    lax.fori_loop(0, slots, settle, 0)


def project_kernel(transposed, place, *refs):
    count = (len(refs) - 2) // 2
    lefts, rights, (keep, send) = refs[:count], refs[count : 2 * count], refs[2 * count :]
    u = place[AT_U]
    dot = dot_nt if transposed else dot_nn
    for at, target, spot in ((1, send, 0), (3, send, 1), (0, keep, 0), (2, keep, 1)):
        total = None
        for left, right in zip(lefts, rights):
            part = dot(left[u ^ at], right[...])
            total = part if total is None else total + part
        target[spot] = total.astype(target.dtype)


def heads_grad_kernel(place, own, near, across, weights, out):
    u = place[AT_U]
    for at, piece in ((0, own[...]), (2, near[...]), (1, across[0]), (3, across[1])):
        out[u ^ at] = dot_nt(piece, weights[...]).astype(BF16)


def out_share_kernel(place, own, near, across, attended, out):
    u = place[AT_U]
    total = dot_tn(attended[u], own[...])
    total = total + dot_tn(attended[u ^ 2], near[...])
    total = total + dot_tn(attended[u ^ 1], across[0])
    total = total + dot_tn(attended[u ^ 3], across[1])
    out[...] = total.astype(BF16)


def pack_of(rows):
    return 2 if rows % 32 == 0 else 1


def packed(rows, units):
    pack = pack_of(rows)
    return (rows // pack, units * pack)


def put_packed(target, index, part):
    rows, units = part.shape
    size = rows // pack_of(rows)
    for j in range(pack_of(rows)):
        target[(*index, slice(None), slice(j * units, (j + 1) * units))] = part[
            j * size : (j + 1) * size
        ]


def get_packed(source, index, rows):
    pack = pack_of(rows)
    units = source.shape[-1] // pack
    return jnp.concatenate(
        [source[(*index, slice(None), slice(j * units, (j + 1) * units))] for j in range(pack)],
        axis=0,
    )


def split_tiles_kernel(depth, place, gate, upper, down, gain, *rest):
    pieces, parts = rest[:depth], rest[depth]
    units = gate.shape[1] // depth
    for i, (tile, scaled) in enumerate(((gate, True), (upper, True), (down, False))):
        for k in range(depth):
            part = tile[:, k * units : (k + 1) * units]
            if scaled:
                part = (part.astype(F32) * gain[...]).astype(BF16)
            put_packed(parts, (k, i), part)
    for d in range(depth):
        pieces[d][...] = parts[lax.rem(place[AT_Z] + d, depth)]


def merge_tiles_kernel(depth, place, *refs):
    mine, far, outs = refs[:depth], refs[depth : 2 * depth], refs[2 * depth :]
    for d in range(depth):
        from_z = lax.rem(place[AT_Z] - d + depth, depth)
        for i, out in enumerate(outs):
            rows = out.shape[1]
            out[from_z * PAIR + place[AT_X]] = get_packed(mine[d], (i,), rows)
            out[from_z * PAIR + 1 - place[AT_X]] = get_packed(far[d], (i,), rows)


def down_kernel(depth, place, *refs):
    actives, (weight, out) = refs[:depth], refs[depth:]
    count = out.shape[2]
    for d, active in enumerate(actives):
        from_z = lax.rem(place[AT_Z] - d + depth, depth)
        rows = dot_nt(active[...], weight[...])
        for i, other in enumerate((0, 2, 1, 3)):
            out[place[AT_U] ^ other, from_z] = rows[i * count : (i + 1) * count].astype(BF16)


def sort_rows_kernel(place, mine, far, own, near, rows):
    share = own.shape[1]
    for z in range(mine.shape[0]):
        rows[z * PAIR + place[AT_X]] = mine[z]
        rows[z * PAIR + 1 - place[AT_X]] = far[z]

    def part(m):
        return rows[pl.ds((place[AT_U] ^ m) * share, share)]

    own[0], own[1] = part(0), part(1)
    near[0], near[1] = part(2), part(3)


def place_rows_kernel(place, own, near, across, out):
    out[:, place[AT_U]] = own[0]
    out[:, place[AT_U] ^ 2] = near[0]
    out[:, place[AT_U] ^ 1] = across[0]
    out[:, place[AT_U] ^ 3] = across[1]


def choose_tile_kernel(place, share, keep, send):
    for z in range(share.shape[0]):
        put_packed(keep, (z, 0), share[z, place[AT_X]])
        put_packed(send, (z, 0), share[z, 1 - place[AT_X]])


def choose_kernel(place, *refs):
    shares, (keep, send) = refs[:-2], refs[-2:]
    for i, share in enumerate(shares):
        keep[:, i] = share[:, place[AT_X]]
        send[:, i] = share[:, 1 - place[AT_X]]


def fold_kernel(depth, place, keep, got, *outs):
    for d in range(depth):
        at = lax.rem(place[AT_Z] + d, depth)
        outs[d][...] = (keep[at].astype(F32) + got[at].astype(F32)).astype(BF16)


def split_uly_kernel(place, pieces, own, near):
    total = None
    parts = []
    for m in range(4):
        total = None
        for z in range(pieces.shape[0]):
            part = pieces[z, 0, place[AT_U] ^ m].astype(F32)
            total = part if total is None else total + part
        parts.append(total.astype(BF16))
    own[0], own[1], near[0], near[1] = parts


def pick_uly_kernel(place, share, own, near):
    own[0], own[1] = share[:, place[AT_U]], share[:, place[AT_U] ^ 1]
    near[0], near[1] = share[:, place[AT_U] ^ 2], share[:, place[AT_U] ^ 3]


def group_rows_kernel(place, own, near, across, keep, send, rows):
    share = own.shape[1]
    for m, part in ((0, own[0]), (2, near[0]), (1, across[0]), (3, across[1])):
        rows[pl.ds((place[AT_U] ^ m) * share, share)] = part
    for z in range(keep.shape[0]):
        keep[z, 0] = rows[z * PAIR + place[AT_X]]
        send[z, 0] = rows[z * PAIR + 1 - place[AT_X]]


def finish_qkv_kernel(place, *refs):
    heads, kinds = refs[:3], refs[3:6]
    weight, gain, grad, grad_gain, bias, head_parts, kind_parts = refs[6:]
    width, side = heads[0].shape[2], heads[0].shape[2] * 4
    for parts, (own, near, across) in ((head_parts, heads), (kind_parts, kinds)):
        parts[place[AT_U]] = own[0]
        parts[place[AT_U] ^ 2] = near[0]
        parts[place[AT_U] ^ 1] = across[0]
        parts[place[AT_U] ^ 3] = across[1]
    total = jnp.zeros(grad_gain.shape, F32)
    for u in range(4):
        bias[u] = kind_parts[u, :16].astype(F32)
        start = side + (u % 2) * KV_HEADS * HEAD_DIM + (u // 2) * HEAD_DIM
        for at, part in (
            (slice(u * width, (u + 1) * width), head_parts[u]),
            (slice(start, start + HEAD_DIM), kind_parts[u, 16:]),
        ):
            part = part.astype(F32)
            grad[:, at] = part * gain[...]
            total = total + jnp.sum(part * weight[:, at].astype(F32), axis=1, keepdims=True)
    grad_gain[...] = total


def finish_kernel(depth, gates, uppers, downs, gate, upper, gain, grad_gate, grad_upper, grad_down, grad_gain):
    rows, units = gate.shape[0], gate.shape[1] // depth
    total = jnp.zeros(grad_gain.shape, F32)
    for k in range(depth):
        at = slice(k * units, (k + 1) * units)
        part = get_packed(gates, (k, 0), rows).astype(F32)
        grad_gate[:, at] = part * gain[...]
        total = total + jnp.sum(part * gate[:, at].astype(F32), axis=1, keepdims=True)
        part = get_packed(uppers, (k, 0), rows).astype(F32)
        grad_upper[:, at] = part * gain[...]
        total = total + jnp.sum(part * upper[:, at].astype(F32), axis=1, keepdims=True)
        grad_down[:, at] = get_packed(downs, (k, 0), rows).astype(F32)
    grad_gain[...] = total


def like(shape, kind=BF16):
    return jax.ShapeDtypeStruct(shape, kind)


def together(*values):
    return lax.optimization_barrier(values)


def after(value, *others):
    return lax.optimization_barrier((value, others))[0]


class Grid:
    def __init__(self):
        self.blocks = lax.axis_size("blk")
        self.ulys = lax.axis_size("uly")
        self.depth = self.blocks // PAIR
        self.b = lax.axis_index("blk")
        self.u = lax.axis_index("uly")
        self.z = self.b // PAIR
        self.x = self.b % PAIR
        self.y = self.u // 2
        self.c = self.u % 2

    def to_z(self, value, step):
        pairs = [
            (z * PAIR + x, ((z + step) % self.depth) * PAIR + x)
            for z in range(self.depth)
            for x in range(PAIR)
        ]
        return lax.ppermute(value, "blk", pairs)

    def swap_x(self, value):
        return lax.ppermute(value, "blk", [(i, i ^ 1) for i in range(self.blocks)])

    def swap_y(self, value):
        return lax.ppermute(value, "uly", [(i, i ^ 2) for i in range(self.ulys)])

    def swap_both(self, value):
        return lax.ppermute(value, "uly", [(i, i ^ 3) for i in range(self.ulys)])

    def swap_core(self, value):
        return lax.ppermute(value, "uly", [(i, i ^ 1) for i in range(self.ulys)])


def paired(bit, mine, other, axis):
    low = jnp.where(bit == 0, mine, other)
    high = jnp.where(bit == 0, other, mine)
    return jnp.stack([low, high], axis=axis)


def pick(bit, array, axis):
    low = lax.index_in_dim(array, 0, axis, keepdims=False)
    high = lax.index_in_dim(array, 1, axis, keepdims=False)
    return jnp.where(bit == 0, low, high), jnp.where(bit == 0, high, low)


def order_z(grid, pieces):
    stacked = jnp.stack(pieces[::-1] + pieces[::-1][:-1])
    start = (grid.depth - 1 - grid.z) % grid.depth
    return lax.dynamic_slice_in_dim(stacked, start, grid.depth, 0)


def gather_uly(grid, value):
    both = paired(grid.y, value, grid.swap_y(value), 0)
    every = paired(grid.c, both, grid.swap_core(both), 1)
    return every.reshape((grid.ulys,) + value.shape)


def scatter_uly(grid, parts, kind=BF16):
    parts = parts.reshape((2, 2) + parts.shape[1:])
    keep, send = pick(grid.c, parts, 1)
    both = keep.astype(F32) + grid.swap_core(send.astype(kind)).astype(F32)
    keep, send = pick(grid.y, both, 0)
    return keep + grid.swap_y(send.astype(kind)).astype(F32)


def gather_blk(grid, value):
    pieces = [value] + [grid.to_z(value, d) for d in range(1, grid.depth)]
    pairs = [paired(grid.x, piece, grid.swap_x(piece), 0) for piece in pieces]
    return order_z(grid, pairs)


def exchange_z(grid, parts):
    pieces = [lax.dynamic_index_in_dim(parts, grid.z, 0, keepdims=False)]
    for d in range(1, grid.depth):
        there = (grid.z + d) % grid.depth
        pieces.append(grid.to_z(lax.dynamic_index_in_dim(parts, there, 0, keepdims=False), d))
    return pieces


def exchange_z_all(grid, parts):
    groups = [[z * PAIR + x for z in range(grid.depth)] for x in range(PAIR)]
    return lax.all_to_all(
        parts, "blk", split_axis=0, concat_axis=0, axis_index_groups=groups, tiled=True
    )


def spread_z(grid, value):
    return exchange_z_all(grid, jnp.broadcast_to(value, (grid.depth, *value.shape)))


def exchange_uly(parts):
    return lax.all_to_all(parts, "uly", split_axis=0, concat_axis=0, tiled=True)


def per_device(
    tokens,
    span_order,
    attn_gain,
    qkv_weight,
    qkv_bias,
    out_weight,
    ffn_gain,
    gate_weight,
    up_weight,
    down_weight,
    cotangent,
):
    grid = Grid()
    local_rows, seqs, model = tokens.shape
    count = local_rows * seqs
    ulys = grid.ulys
    depth = grid.depth
    blocks = grid.blocks
    cycle_rows = local_rows * ulys
    spans = cycle_rows // SPAN
    slots = blocks * spans
    group = HEADS // ulys
    factor = 1.0 / math.sqrt(HEAD_DIM)
    width = group * HEAD_DIM
    columns = width + HEAD_DIM
    shard = qkv_weight.shape[0]
    block_model = shard * ulys
    chunk = math.gcd(slots, 4) * SPAN
    side = HEADS * HEAD_DIM
    place = jnp.stack([grid.z, grid.x, grid.y, grid.c, grid.b, grid.u]).astype(jnp.int32)

    def by_seq(array):
        return jnp.transpose(array, (1, 0, 2)).reshape(count, model)

    def by_row(array):
        return jnp.transpose(array.reshape(seqs, local_rows, model), (1, 0, 2))

    def by_uly(array):
        lead = array.shape[0]
        heads = array[:, :side].reshape(lead, ulys, width)
        kinds = array[:, side:].reshape(lead, 2, KV_HEADS, HEAD_DIM)
        kinds = jnp.transpose(kinds, (0, 2, 1, 3)).reshape(lead, ulys, HEAD_DIM)
        return jnp.transpose(jnp.concatenate([heads, kinds], axis=-1), (1, 0, 2))

    rows = by_seq(tokens).astype(F32)
    unit_one, factor_one = norm_rows(rows)
    unit_own = unit_one.astype(BF16)
    unit_near = grid.swap_y(unit_own)
    gain_one = attn_gain.astype(F32)[:, None]
    scaled = (qkv_weight.astype(F32) * gain_one).astype(BF16)
    heads_share = blocks // ulys
    owned_columns = qkv_bias.shape[0]
    column_start = (grid.b * ulys + grid.u) * owned_columns
    bias_row = lax.dynamic_update_slice(
        jnp.zeros((16, owned_columns * blocks * ulys), BF16),
        jnp.pad(qkv_bias[None], ((0, 15), (0, 0))),
        (0, column_start),
    )
    by_head = by_uly(jnp.concatenate([scaled, bias_row], axis=0))
    by_head = exchange_uly(by_head)
    block_rows = jnp.concatenate(
        [by_head[:, :shard].reshape(block_model, columns), jnp.sum(by_head[:, shard:], axis=0)],
        axis=0,
    )
    qkv_mine = [block_rows] + [grid.to_z(block_rows, d) for d in range(1, depth)]
    first_far = grid.swap_x(block_rows)
    first_arrived = qkv_mine[1]
    *qkv_mine, first_far, unit_near = together(*qkv_mine, first_far, unit_near)

    gain_two = ffn_gain.astype(F32)[:, None]
    hidden_units = gate_weight.shape[1] // depth
    order = sorted(range(1, depth), key=lambda d: (min(d, depth - d), d))
    early, middle, late = order[0], order[1:-1], order[-1]
    split_in = after((gate_weight, up_weight, down_weight), first_arrived)
    split_in = (*split_in[:2], split_in[2].T)
    tile_pieces = call(
        functools.partial(split_tiles_kernel, depth),
        [place],
        [*split_in, gain_two],
        [like((3, *packed(block_model, hidden_units)))] * depth,
        scratch=[pltpu.VMEM((depth, 3, *packed(block_model, hidden_units)), BF16)],
    )
    qkv_far = [first_far] + [grid.swap_x(piece) for piece in qkv_mine[1:]]
    unit_across = grid.swap_core(jnp.stack([unit_own, unit_near]))
    out_first, early_piece = after((out_weight, tile_pieces[early]), *qkv_mine[1:])
    tile_mine = {0: tile_pieces[0], early: grid.to_z(early_piece, early)}
    out_mine = spread_z(grid, out_first)
    tile_far = {0: grid.swap_x(after(tile_pieces[0], qkv_far[1]))}
    *qkv_far, unit_across = together(*qkv_far, unit_across)
    unit_parts = (unit_own, unit_near, unit_across)

    head_rows = grid.b * cycle_rows + jnp.arange(cycle_rows, dtype=jnp.int32)
    places = positions(span_order, head_rows).reshape(seqs, ulys, local_rows)
    places = jnp.transpose(places, (1, 0, 2)).reshape(ulys, count)
    cosine, sine = rope_tables(places)
    units, qkv_part, query, kind = call(
        functools.partial(mix_kernel, depth, group),
        [place],
        [*unit_parts, cosine, sine, *qkv_mine, *qkv_far],
        [
            like((ulys, count, model)),
            like((blocks, block_model, columns)),
            like((ulys, count, width)),
            like((ulys, count, HEAD_DIM)),
        ],
        scratch=[
            pltpu.VMEM((blocks, 16, columns), BF16),
            pltpu.SemaphoreType.DMA((2 * blocks + ulys,)),
        ],
        far=(0, 1, 2, *range(5, 2 * depth + 5)),
    )
    units = units.reshape(ulys * count, model)
    qkv_part = qkv_part.reshape(model, columns)
    kinds = [kind] + [grid.to_z(kind, d) for d in range(1, depth)]
    out_mine, cot_flat = after((out_mine, by_seq(cotangent)), kind)
    out_far = grid.swap_x(out_mine)
    cot_first = cot_flat
    cot_near = grid.swap_y(cot_first)
    *held, late_pair, late_down = after(
        (*[tile_pieces[d] for d in middle], tile_pieces[late][:2], tile_pieces[late][2:]), kinds[1]
    )
    for d, piece in zip(middle, held):
        tile_mine[d] = grid.to_z(piece, d)
    out_far, cot_near, tile_mine[early], tile_far[0], *kinds = together(
        out_far, cot_near, tile_mine[early], tile_far[0], *kinds
    )
    late_pair = grid.to_z(after(late_pair, kinds[-1]), late)

    a_own = jnp.stack(kinds)
    a_far = grid.swap_x(a_own)
    b_own = grid.swap_core(a_own)
    out_own, out_near = call(
        sort_rows_kernel,
        [place],
        [out_mine, out_far],
        [like((2, heads_share, shard, model))] * 2,
        scratch=[pltpu.VMEM((blocks, shard, model), BF16)],
    )
    out_near = grid.swap_y(out_near)
    a_far, b_own, out_near, *held = together(
        a_far, b_own, out_near, *[tile_mine[d] for d in middle]
    )
    tile_mine.update(zip(middle, held))

    b_far = grid.swap_core(a_far)
    out_across = grid.swap_core(jnp.stack([out_own[1], out_near[1]]))
    tile_far[early] = grid.swap_x(after(tile_mine[early], a_far))
    b_far, out_across = together(b_far, out_across)

    def over_uly(piece):
        both = jnp.concatenate([piece, grid.swap_y(piece)], axis=0)
        return jnp.concatenate([both, grid.swap_core(both)], axis=0)

    grad_rows = cot_flat.astype(F32)

    scale = factor * LOG2E
    kv_shape = (depth, ulys, seqs, local_rows, HEAD_DIM)
    kv_spec = pl.BlockSpec(
        (depth, ulys, 1, local_rows, HEAD_DIM), lambda s, *unused: (0, 0, s, 0, 0)
    )
    heads_shape = (ulys, seqs, local_rows, width)
    heads_spec = pl.BlockSpec((ulys, 1, local_rows, width), lambda s, *unused: (0, s, 0, 0))
    lse_spec = pl.BlockSpec((1, spans, 1, group * SPAN), lambda s, *unused: (s, 0, 0, 0))
    table_shape = (ulys, seqs, local_rows, HEAD_DIM)
    table_spec = pl.BlockSpec((ulys, 1, local_rows, HEAD_DIM), lambda s, *unused: (0, s, 0, 0))
    sorted_spec = pl.BlockSpec((1, 2, slots * SPAN, HEAD_DIM), lambda s, *unused: (s, 0, 0, 0))
    params = pltpu.CompilerParams(vmem_limit_bytes=VMEM_LIMIT)
    query = query.reshape(heads_shape)
    attended, lse, kv = pl.pallas_call(
        functools.partial(attend_kernel, depth, spans, chunk, group, scale),
        grid_spec=pltpu.PrefetchScalarGridSpec(
            num_scalar_prefetch=2,
            grid=(seqs,),
            in_specs=[heads_spec] + [kv_spec] * 4,
            out_specs=[heads_spec, lse_spec, sorted_spec],
        ),
        out_shape=[
            like(heads_shape),
            like((seqs, spans, 1, group * SPAN), F32),
            like((seqs, 2, slots * SPAN, HEAD_DIM)),
        ],
        compiler_params=params,
        cost_estimate=SMALL,
    )(span_order, place, query, *[part.reshape(kv_shape) for part in (a_own, a_far, b_own, b_far)])
    flat = attended.reshape(ulys, count, width)
    out_own, tile_far[early], late_pair, attended = together(
        out_own, tile_far[early], late_pair, attended
    )
    late_down = grid.to_z(after(late_down, attended), late)
    flat = attended.reshape(ulys, count, width)
    for d in middle:
        tile_far[d] = grid.swap_x(after(tile_mine[d], attended))
    (out_part,) = call(
        place_rows_kernel, [place], [out_own, out_near, out_across], [like((heads_share, ulys, shard, model))]
    )
    out_part = out_part.reshape(width, model)
    keep, send = call(
        functools.partial(project_kernel, False),
        [place],
        [flat, out_part],
        [like((2, count, model), F32), like((2, count, model))],
    )
    got = grid.swap_core(send)
    both = keep + got.astype(F32)
    got = grid.swap_y(both[1].astype(BF16))
    got, late_down, *held = together(got, late_down, *[tile_far[d] for d in middle])
    tile_mine[late] = jnp.concatenate([late_pair, late_down])
    tile_far.update(zip(middle, held))
    tile_far[late] = grid.swap_x(after(tile_mine[late], got))
    hidden = rows + both[0] + got.astype(F32)

    unit_two, factor_two = norm_rows(hidden)
    mid_own = unit_two.astype(BF16)
    mid_near = grid.swap_y(mid_own)
    mid_pieces = [mid_own, grid.to_z(mid_own, 1)]
    cot_pieces = [cot_first, grid.to_z(after(cot_first, got), 1)]
    mid_near, tile_far[late] = together(mid_near, tile_far[late])
    for d in range(2, depth):
        mid_pieces.append(grid.to_z(mid_pieces[-1], 1))
        cot_pieces.append(grid.to_z(cot_pieces[-1], 1))

    def chunk_of(own, near):
        both = jnp.concatenate([own, near], axis=0)
        return jnp.concatenate([both, grid.swap_core(both)], axis=0)

    mid_chunks = [chunk_of(mid_own, mid_near)] + [over_uly(piece) for piece in mid_pieces[1:]]
    cot_chunks = [chunk_of(cot_first, cot_near)] + [over_uly(piece) for piece in cot_pieces[1:]]
    gate_used, upper_used, down_used = [
        tile.reshape(model, hidden_units)
        for tile in call(
            functools.partial(merge_tiles_kernel, depth),
            [place],
            [tile_mine[d] for d in range(depth)] + [tile_far[d] for d in range(depth)],
            [like((blocks, block_model, hidden_units))] * 3,
        )
    ]
    actives, gate_grads, upper_grads, back_chunks = [], [], [], []
    for mid, cot in zip(mid_chunks, cot_chunks):
        gate = matmul(mid, gate_used)
        upper = matmul(mid, upper_used)
        sigmoid = jax.nn.sigmoid(gate)
        active_grad = matmul(cot, down_used)
        actives.append((gate * sigmoid * upper).astype(BF16))
        gate_grad = (active_grad * upper * sigmoid * (1.0 + gate * (1.0 - sigmoid))).astype(BF16)
        upper_grad = (active_grad * gate * sigmoid).astype(BF16)
        gate_grads.append(gate_grad)
        upper_grads.append(upper_grad)
        back_chunks.append(
            contract_cols(gate_grad, gate_used) + contract_cols(upper_grad, upper_used)
        )
    def over_core(chunk):
        chunk = chunk.reshape(2, 2, count, model)
        return chunk[0].astype(F32) + grid.swap_core(chunk[1].astype(BF16)).astype(F32)

    def over_y(both):
        return both[0] + grid.swap_y(both[1].astype(BF16)).astype(F32)

    def halve(shares, rows):
        shape = (depth, PAIR, *rows, shares[0].shape[-1])
        shares = [share.astype(BF16).reshape(shape) for share in shares]
        half = like((depth, len(shares), *rows, shape[-1]))
        return call(choose_kernel, [place], shares, [half] * 2)

    def halve_tile(share):
        share = share.astype(BF16).reshape(depth, PAIR, block_model, hidden_units)
        half = like((depth, 1, *packed(block_model, hidden_units)))
        return call(choose_tile_kernel, [place], [share], [half] * 2)

    def fold(keep, got):
        return exchange_z_all(grid, (keep.astype(F32) + got.astype(F32)).astype(BF16))

    z_groups = [[z * PAIR + x for z in range(depth)] for x in range(PAIR)]
    boths = [over_core(chunk) for chunk in back_chunks]
    mid_parts = [over_y(both) for both in boths]
    back_pieces = [grid.to_z(mid_parts[d].astype(BF16), -d) for d in range(1, depth)]
    mid_all = jnp.concatenate(mid_chunks)
    mid_now = after(mid_all, back_chunks[-1], *boths[:-1], *mid_parts[:-1])
    gate_keep, gate_send = halve_tile(contract_rows(mid_now, jnp.concatenate(gate_grads)))
    mid_now = after(mid_all, gate_send, *mid_parts, back_pieces[0])
    upper_keep, upper_send = halve_tile(contract_rows(mid_now, jnp.concatenate(upper_grads)))
    gate_got = grid.swap_x(gate_send)
    first, gate_got, upper_send, *back_pieces = together(
        mid_parts[0], gate_got, upper_send, *back_pieces
    )
    mid_grad = first + sum(piece.astype(F32) for piece in back_pieces)

    hidden_grad = grad_rows + norm_back(mid_grad, unit_two, factor_two)
    branch_own = hidden_grad.astype(BF16)
    branch_near = grid.swap_y(branch_own)
    upper_got = grid.swap_x(after(upper_send, gate_got))
    gate_owned = fold(*after((gate_keep, gate_got), branch_own))
    held = after((*cot_chunks, *actives), branch_own)
    cot_all, active_all = [jnp.concatenate(part) for part in (held[:depth], held[depth:])]
    down_keep, down_send = halve_tile(contract_rows(cot_all, active_all))
    down_send, branch_near, upper_got = together(down_send, branch_near, upper_got)
    down_got = grid.swap_x(down_send)
    branch_across = grid.swap_core(jnp.stack([branch_own, branch_near]))
    branch_parts = (branch_own, branch_near, branch_across)
    (grad_heads,) = call(
        heads_grad_kernel, [place], [*branch_parts, out_part], [like((ulys, count, width))]
    )

    grad_heads, gate_owned = together(grad_heads.reshape(heads_shape), gate_owned)
    upper_owned = fold(*after((upper_keep, upper_got), gate_owned))
    both_spec = pl.BlockSpec(
        (2, depth, ulys, 1, local_rows, HEAD_DIM), lambda s, *unused: (0, 0, 0, s, 0, 0)
    )
    query_grad, keep_own, keep_far, send_both = pl.pallas_call(
        functools.partial(attend_back_kernel, depth, spans, chunk, group, scale, factor),
        grid_spec=pltpu.PrefetchScalarGridSpec(
            num_scalar_prefetch=2,
            grid=(seqs,),
            in_specs=[heads_spec, sorted_spec]
            + [heads_spec] * 2
            + [lse_spec]
            + [table_spec] * 2,
            out_specs=[heads_spec] + [kv_spec] * 2 + [both_spec],
            scratch_shapes=[pltpu.VMEM((2, slots * SPAN, HEAD_DIM), F32)],
        ),
        out_shape=[like(heads_shape)] + [like(kv_shape)] * 2 + [like((2, *kv_shape))],
        compiler_params=params,
        cost_estimate=SMALL,
    )(
        span_order,
        place,
        query,
        kv,
        grad_heads,
        attended,
        lse,
        cosine.reshape(table_shape),
        sine.reshape(table_shape),
    )
    got_far, got_own = [
        jnp.concatenate([grid.swap_core(part) for part in jnp.split(send_both[k], 2, axis=0)])
        for k in (1, 0)
    ]
    query_grad = query_grad.reshape(ulys * count, width)
    got_far, got_own, query_grad, upper_owned = together(
        got_far, got_own, query_grad, upper_owned
    )
    (out_all,) = call(
        functools.partial(down_kernel, depth),
        [place],
        [*after(tuple(actives), got_far), down_used],
        [like((ulys, depth, count, model))],
    )
    from_x = grid.swap_x((keep_far.astype(F32) + got_far.astype(F32)).astype(BF16))
    share_parts = after(branch_parts, got_far)
    (out_share,) = call(out_share_kernel, [place], [*share_parts, flat], [like((width, model))])
    out_own, out_near = call(
        pick_uly_kernel,
        [place],
        [out_share.reshape(heads_share, ulys, shard, model)],
        [like((2, heads_share, shard, model))] * 2,
    )
    head_keep, head_send = halve([contract_rows(units, query_grad)], (ulys, shard))
    from_x, head_send, out_near, out_all, down_got = together(
        from_x, head_send, out_near, out_all, down_got
    )
    out_all = lax.psum_scatter(out_all, "uly", scatter_dimension=0, tiled=False)
    kind_parts = keep_own.astype(F32) + got_own.astype(F32) + from_x.astype(F32)
    kind_parts = kind_parts.astype(BF16)
    kind_back = [grid.to_z(kind_parts[d], -d) for d in range(1, depth)]
    head_got = grid.swap_x(head_send)
    out_near = grid.swap_y(out_near)
    *kind_back, out_near, kind_parts, head_got = together(
        *kind_back, out_near, kind_parts, head_got
    )
    out_across = grid.swap_core(jnp.stack([out_own[1], out_near[1]]))
    kind_grad = kind_parts[0].astype(F32)
    for piece in kind_back:
        kind_grad = kind_grad + piece.astype(F32)
    kind_grad = kind_grad.reshape(ulys * count, HEAD_DIM)
    turned = jnp.roll(kind_grad, HEAD_DIM // 2, axis=1)
    is_key = grid.c == 0
    flat_cosine = cosine.reshape(ulys * count, HEAD_DIM)
    flat_sine = sine.reshape(ulys * count, HEAD_DIM)
    kind_grad = jnp.where(is_key, kind_grad * flat_cosine - turned * flat_sine, kind_grad)
    kind_grad = kind_grad.astype(BF16)

    bias = jnp.sum(query_grad.astype(F32), axis=0).reshape(group, HEAD_DIM)
    bias = jnp.concatenate([bias, jnp.sum(kind_grad.astype(F32), axis=0)[None]], axis=0)
    bias = jnp.pad(bias.astype(BF16), ((0, 16 - group - 1), (0, 0)))
    bias = jnp.broadcast_to(bias, (blocks, ulys, 16, HEAD_DIM))
    share = contract_rows(units, kind_grad).astype(BF16)
    share = share.reshape(blocks, ulys, shard, HEAD_DIM)
    share = jnp.concatenate([bias, share], axis=2)
    kind_keep, kind_send = halve([share], (ulys, shard + 16))
    kind_got = grid.swap_x(kind_send)
    out_all = lax.psum_scatter(
        after(out_all, kind_send), "blk", scatter_dimension=0, axis_index_groups=z_groups, tiled=False
    )
    head_pieces = fold(*after((head_keep, head_got), kind_send))
    out_across = after(out_across, kind_send)
    out_keep, out_send = call(
        group_rows_kernel,
        [place],
        [out_own, out_near, out_across],
        [like((depth, 1, shard, model))] * 2,
        scratch=[pltpu.VMEM((blocks, shard, model), BF16)],
    )
    out_got = grid.swap_x(after(out_send, kind_got))
    kind_pieces = call(
        functools.partial(fold_kernel, depth),
        [place],
        [kind_keep, kind_got],
        [like(kind_keep.shape[1:])] * depth,
    )
    kind_pieces = [kind_pieces[0]] + [grid.to_z(kind_pieces[d], d) for d in range(1, depth)]
    kind_pieces = jnp.stack(kind_pieces)
    kind_pieces, out_got = together(kind_pieces, out_got)
    kind_now = after(kind_grad, kind_pieces)
    keep, send = call(
        functools.partial(project_kernel, True),
        [place],
        [
            query_grad.reshape(ulys, count, width),
            kind_now.reshape(ulys, count, HEAD_DIM),
            qkv_part[:, :width],
            qkv_part[:, width:],
        ],
        [like((2, count, model), F32), like((2, count, model))],
    )
    both = keep + grid.swap_core(send).astype(F32)
    down_owned = fold(*after((down_keep, down_got), head_pieces))
    out_pieces = call(
        functools.partial(fold_kernel, depth),
        [place],
        [out_keep, out_got],
        [like(out_keep.shape[1:])] * depth,
    )
    out_pieces = [out_pieces[0]] + [grid.to_z(out_pieces[d], d) for d in range(1, depth)]

    def to_owners(pieces):
        own, near = call(
            split_uly_kernel, [place], [pieces], [like((2, *pieces.shape[3:]))] * 2
        )
        near = grid.swap_y(near)
        return own, near, grid.swap_core(jnp.stack([own[1], near[1]]))

    head_owned = to_owners(head_pieces)
    kind_owned = to_owners(kind_pieces)
    grad_qkv, grad_gain_one, bias = call(
        finish_qkv_kernel,
        [place],
        [*head_owned, *kind_owned, qkv_weight, gain_one],
        [
            like(qkv_weight.shape, F32),
            like((shard, 1), F32),
            like((ulys, 16, HEAD_DIM), F32),
        ],
        scratch=[
            pltpu.VMEM((ulys, shard, width), BF16),
            pltpu.VMEM((ulys, shard + 16, HEAD_DIM), BF16),
        ],
    )
    grad_gain_one = grad_gain_one[:, 0]
    kind_bias = bias[:, group].reshape(KV_HEADS, 2, HEAD_DIM)
    bias = jnp.concatenate(
        [bias[:, :group].reshape(-1), jnp.transpose(kind_bias, (1, 0, 2)).reshape(-1)]
    )
    grad_bias = lax.dynamic_slice_in_dim(bias, column_start, owned_columns, 0)
    grad_out = sum(piece[0].astype(F32) for piece in out_pieces)
    result = hidden + after(out_all, grad_qkv).astype(F32)
    output = by_row(result.astype(BF16))
    normed_grad = both[0] + grid.swap_y(both[1].astype(BF16)).astype(F32)
    grad_tokens = by_row(hidden_grad + norm_back(normed_grad, unit_one, factor_one))
    tile_shape = gate_weight.shape
    grad_gate, grad_upper, grad_down, gain_part = call(
        functools.partial(finish_kernel, depth),
        [],
        [gate_owned, upper_owned, after(down_owned, grad_qkv), gate_weight, up_weight, gain_two],
        [like(tile_shape, F32)] * 3 + [like((block_model, 1), F32)],
    )
    grad_down = grad_down.T
    grad_gain_two = scatter_uly(grid, gain_part.reshape(ulys, -1), F32)
    return (
        output,
        grad_tokens,
        grad_gain_one,
        grad_qkv,
        grad_bias,
        grad_out,
        grad_gain_two.reshape(-1),
        grad_gate,
        grad_upper,
        grad_down,
    )


def solution(mesh):
    in_specs = (
        P(("blk", "uly"), None, None),
        P(),
        P(("blk", "uly")),
        P(("blk", "uly"), None),
        P(("blk", "uly")),
        P(("blk", "uly"), None),
        P("blk"),
        P("blk", "uly"),
        P("blk", "uly"),
        P("uly", "blk"),
        P(("blk", "uly"), None, None),
    )
    out_specs = (
        P(("blk", "uly"), None, None),
        P(("blk", "uly"), None, None),
        P(("blk", "uly")),
        P(("blk", "uly"), None),
        P(("blk", "uly")),
        P(("blk", "uly"), None),
        P(("blk", "uly")),
        P("blk", "uly"),
        P("blk", "uly"),
        P("uly", "blk"),
    )
    return jax.shard_map(
        per_device, mesh=mesh, in_specs=in_specs, out_specs=out_specs, check_vma=False
    )
```

```python
import functools
import math

import jax
import jax.numpy as jnp
from jax import lax
from jax.experimental import pallas as pl
from jax.experimental.pallas import tpu as pltpu
from jax.sharding import PartitionSpec as P

HEADS = 12
KV_HEADS = 2
HEAD_DIM = 128
SPAN = 128
PAIR = 2


EPS = 1e-06
THETA = 1000000.0
FLOOR = -1e30
LOG2E = 1.4426950408889634
BF16 = jnp.bfloat16
F32 = jnp.float32
SMALL = pl.CostEstimate(flops=1, transcendentals=0, bytes_accessed=1)
VMEM_LIMIT = 48 * 1024 * 1024

def norm_rows(rows):
    factor = lax.rsqrt(jnp.mean(rows * rows, axis=-1, keepdims=True) + EPS)
    return (rows * factor, factor)


def norm_back(scaled, unit, factor):
    return factor * (scaled - unit * jnp.mean(scaled * unit, axis=-1, keepdims=True))


def matmul(left, right):
    return jnp.dot(left, right, preferred_element_type=F32)


def contract_rows(left, right):
    return lax.dot_general(left, right, (((0,), (0,)), ((), ())), preferred_element_type=F32)


def contract_cols(left, right):
    return lax.dot_general(left, right, (((1,), (1,)), ((), ())), preferred_element_type=F32)


def positions(order, rows):
    table = jnp.arange(order.shape[1], dtype=jnp.int32)
    slots = rows // SPAN
    picked = jnp.where(slots[None, :, None] == table[None, None, :], order[:, None, :], 0)
    return jnp.sum(picked, axis=-1) * SPAN + (rows % SPAN)[None, :]


def rope_tables(places):
    index = jnp.arange(HEAD_DIM // 2).astype(F32)
    freq = THETA ** (-2.0 * index / HEAD_DIM)
    angle = places.astype(F32)[..., None] * freq
    cosine, sine = jnp.cos(angle), jnp.sin(angle)
    cosine = jnp.concatenate([cosine, cosine], axis=-1)
    return (cosine, jnp.concatenate([-sine, sine], axis=-1))


def dot_nn(left, right):
    return lax.dot_general(left, right, (((1,), (0,)), ((), ())), preferred_element_type=F32)


def dot_nt(left, right):
    return lax.dot_general(left, right, (((1,), (1,)), ((), ())), preferred_element_type=F32)


def dot_tn(left, right):
    return lax.dot_general(left, right, (((0,), (0,)), ((), ())), preferred_element_type=F32)


def call(kernel, scalars, arrays, outs, **options):
    return pl.pallas_call(
        kernel,
        grid_spec=pltpu.PrefetchScalarGridSpec(
            num_scalar_prefetch=len(scalars),
            grid=(1,),
            in_specs=[
                pl.BlockSpec(memory_space=pltpu.HBM) if i in options.get("far", ()) else whole(array.shape, options.get("single", False))
                for i, array in enumerate(arrays)
            ],
            out_specs=[whole(out.shape, options.get("single", False)) for out in outs],
            scratch_shapes=options.get("scratch", ()),
        ),
        out_shape=outs,
        compiler_params=pltpu.CompilerParams(vmem_limit_bytes=VMEM_LIMIT),
        cost_estimate=SMALL,
    )(*scalars, *arrays)


def whole(shape, single=False):
    mode = pl.Buffered(buffer_count=1) if single else None
    return pl.BlockSpec(shape, lambda *unused: (0,) * len(shape), pipeline_mode=mode)


def turn(field):
    return pltpu.roll(field, HEAD_DIM // 2, 1)


AT_Z, AT_X, AT_Y, AT_C, AT_B, AT_U = range(6)


def mix_kernel(depth, group, place, own, near, across, cosine, sine, *rest):
    pieces, far = rest[:depth], rest[depth : 2 * depth]
    units, weights, query, kind, bias_rows, flags = rest[2 * depth :]
    u = place[AT_U]
    rows = weights.shape[1]
    copies = []

    def bring(source, target):
        copies.append(pltpu.make_async_copy(source, target, flags.at[len(copies)]))
        copies[-1].start()

    for d in range(depth):
        from_z = lax.rem(place[AT_Z] - d + depth, depth)
        for k in range(PAIR):
            piece = far[d] if k else pieces[d]
            from_x = place[AT_X] if k == 0 else 1 - place[AT_X]
            bring(piece.at[pl.ds(0, rows)], weights.at[from_z * PAIR + from_x])
            bring(piece.at[pl.ds(rows, 16)], bias_rows.at[PAIR * d + k])
    bring(own, units.at[u])
    bring(near, units.at[u ^ 2])
    bring(across.at[0], units.at[u ^ 1])
    bring(across.at[1], units.at[u ^ 3])
    for copy in copies:
        copy.wait()
    bias = jnp.sum(bias_rows[...].astype(F32), axis=(0, 1))[None]
    model = units.shape[2]
    all_weights = weights[...].reshape(model, weights.shape[2])
    is_key = place[AT_C] == 0
    for i in range(units.shape[0]):
        mixed = dot_nn(units[i], all_weights) + bias
        cos, sin = cosine[i], sine[i]
        for h in range(group):
            field = mixed[:, h * HEAD_DIM : (h + 1) * HEAD_DIM]
            query[i, :, h * HEAD_DIM : (h + 1) * HEAD_DIM] = (field * cos + turn(field) * sin).astype(
                BF16
            )
        field = mixed[:, group * HEAD_DIM :]
        turned = field * cos + turn(field) * sin
        kind[i] = jnp.where(is_key, turned, field).astype(BF16)


def stack_heads(block, group):
    block = block.reshape(SPAN, group * HEAD_DIM)
    return jnp.concatenate(
        [block[:, h * HEAD_DIM : (h + 1) * HEAD_DIM] for h in range(group)], axis=0
    )


def key_mask(first_key, keys, place, group):
    key = first_key + lax.broadcasted_iota(jnp.int32, (keys, group * SPAN), 0)
    row = lax.broadcasted_iota(jnp.int32, (keys, group * SPAN), 1) % SPAN
    return key <= place * SPAN + row


def attend_kernel(
    depth, spans, chunk, group, scale, order, place, query, a_own, a_far, b_own, b_far, out, lse, kv
):
    seq = pl.program_id(0)
    core, x, z = place[AT_C], place[AT_X], place[AT_Z]
    step = query.shape[0] // spans
    slots = depth * PAIR * spans

    def settle(slot, unused):
        blk, span = slot // spans, lax.rem(slot, spans)
        d = lax.rem(z - blk // PAIR + depth, depth)
        there = pl.ds(pl.multiple_of(order[seq, slot] * SPAN, SPAN), SPAN)
        here = pl.ds(span * step, step)
        for mine, other, far in ((a_own, b_own, False), (a_far, b_far, True)):

            @pl.when((lax.rem(blk, PAIR) != x) == far)
            def unused_copy():
                kv[0, core, there] = mine[d, here, 0].reshape(SPAN, HEAD_DIM)
                kv[0, 1 - core, there] = other[d, here, 0].reshape(SPAN, HEAD_DIM)

        return 0

    lax.fori_loop(0, slots, settle, 0)
    for span in range(spans):
        spot = order[seq, place[AT_B] * spans + span]
        queries = stack_heads(query[span * step : (span + 1) * step, 0], group)

        def advance(index, state, masked):
            peak, total, summed = state
            keys = pl.ds(pl.multiple_of(index * chunk, chunk), chunk)
            scores = dot_nt(kv[0, 0, keys], queries)
            if masked:
                allowed = key_mask(index * chunk, chunk, spot, group)
                scores = jnp.where(allowed, scores, FLOOR)
            new_peak = jnp.maximum(peak, jnp.max(scores, axis=0, keepdims=True))
            weights = jnp.exp2((scores - new_peak) * scale)
            fade = jnp.exp2((peak - new_peak) * scale)
            total = total * fade + jnp.sum(weights, axis=0, keepdims=True)
            summed = summed * fade + dot_tn(kv[0, 1, keys], weights.astype(BF16))
            return new_peak, total, summed

        start = (
            jnp.full((1, group * SPAN), FLOOR, F32),
            jnp.zeros((1, group * SPAN), F32),
            jnp.zeros((HEAD_DIM, group * SPAN), F32),
        )
        last = spot * SPAN // chunk
        state = lax.fori_loop(0, last, lambda i, s: advance(i, s, False), start)
        peak, total, summed = advance(last, state, True)
        lse[0, span] = peak * scale + jnp.log2(total)
        result = (summed / total).T.astype(BF16)
        for h in range(group):
            out[span * step : (span + 1) * step, 0, :, h * HEAD_DIM : (h + 1) * HEAD_DIM] = result[
                h * SPAN : (h + 1) * SPAN
            ].reshape(step, SPAN // step, HEAD_DIM)


def attend_back_kernel(
    depth,
    spans,
    chunk,
    group,
    scale,
    factor,
    order,
    place,
    query,
    kv,
    grad,
    out,
    lse,
    cosine,
    sine,
    query_grad,
    keep_own,
    keep_far,
    send_both,
    sums,
):
    seq = pl.program_id(0)
    core, x, z = place[AT_C], place[AT_X], place[AT_Z]
    step = query.shape[0] // spans
    slots = depth * PAIR * spans
    sums[...] = jnp.zeros(sums.shape, F32)
    for span in range(spans):
        spot = order[seq, place[AT_B] * spans + span]
        at = slice(span * step, (span + 1) * step)
        queries = stack_heads(query[at, 0], group)
        grads = stack_heads(grad[at, 0], group)
        results = stack_heads(out[at, 0], group)
        delta = jnp.sum(
            (grads.astype(F32) * results.astype(F32)).T, axis=0, keepdims=True
        )
        level = lse[0, span]

        def advance(index, total, masked):
            keys = pl.ds(pl.multiple_of(index * chunk, chunk), chunk)
            key, value = kv[0, 0, keys], kv[0, 1, keys]
            probs = jnp.exp2(dot_nt(key, queries) * scale - level)
            if masked:
                probs = jnp.where(key_mask(index * chunk, chunk, spot, group), probs, 0.0)
            score_grad = (probs * (dot_nt(value, grads) - delta)).astype(BF16)
            sums[1, keys] += dot_nn(probs.astype(BF16), grads)
            sums[0, keys] += dot_nn(score_grad, queries)
            return total + dot_tn(key, score_grad)

        last = spot * SPAN // chunk
        total = jnp.zeros((HEAD_DIM, group * SPAN), F32)
        total = lax.fori_loop(0, last, lambda i, s: advance(i, s, False), total)
        total = (advance(last, total, True) * factor).T
        cos = cosine[at, 0].reshape(SPAN, HEAD_DIM)
        sin = sine[at, 0].reshape(SPAN, HEAD_DIM)
        for h in range(group):
            field = total[h * SPAN : (h + 1) * SPAN]
            field = (field * cos - turn(field) * sin).astype(BF16)
            query_grad[at, 0, :, h * HEAD_DIM : (h + 1) * HEAD_DIM] = field.reshape(
                step, SPAN // step, HEAD_DIM
            )

    keep_scale = jnp.where(core == 0, factor, 1.0)
    send_scale = jnp.where(core == 0, 1.0, factor)

    def settle(slot, unused):
        blk, span = slot // spans, lax.rem(slot, spans)
        d = lax.rem(z - blk // PAIR + depth, depth)
        there = pl.ds(pl.multiple_of(order[seq, slot] * SPAN, SPAN), SPAN)
        here = pl.ds(span * step, step)
        shape = (step, SPAN // step, HEAD_DIM)
        for keep, send, far in ((keep_own, 0, False), (keep_far, 1, True)):

            @pl.when((lax.rem(blk, PAIR) != x) == far)
            def unused_copy():
                keep[d, here, 0] = (sums[core, there] * keep_scale).astype(BF16).reshape(shape)
                send_both[send, d, here, 0] = (sums[1 - core, there] * send_scale).astype(BF16).reshape(shape)

        return 0

    lax.fori_loop(0, slots, settle, 0)


def project_kernel(transposed, place, *refs):
    count = (len(refs) - 2) // 2
    lefts, rights, (keep, send) = refs[:count], refs[count : 2 * count], refs[2 * count :]
    u = place[AT_U]
    dot = dot_nt if transposed else dot_nn
    for at, target, spot in ((1, send, 0), (3, send, 1), (0, keep, 0), (2, keep, 1)):
        total = None
        for left, right in zip(lefts, rights):
            part = dot(left[u ^ at], right[...])
            total = part if total is None else total + part
        target[spot] = total.astype(target.dtype)


def heads_grad_kernel(place, own, near, across, weights, out):
    u = place[AT_U]
    for at, piece in ((0, own[...]), (2, near[...]), (1, across[0]), (3, across[1])):
        out[u ^ at] = dot_nt(piece, weights[...]).astype(BF16)


def out_share_kernel(place, own, near, across, attended, out):
    u = place[AT_U]
    total = dot_tn(attended[u], own[...])
    total = total + dot_tn(attended[u ^ 2], near[...])
    total = total + dot_tn(attended[u ^ 1], across[0])
    total = total + dot_tn(attended[u ^ 3], across[1])
    out[...] = total.astype(BF16)


def pack_of(rows):
    return 2 if rows % 32 == 0 else 1


def packed(rows, units):
    pack = pack_of(rows)
    return (rows // pack, units * pack)


def put_packed(target, index, part):
    rows, units = part.shape
    size = rows // pack_of(rows)
    for j in range(pack_of(rows)):
        target[(*index, slice(None), slice(j * units, (j + 1) * units))] = part[
            j * size : (j + 1) * size
        ]


def get_packed(source, index, rows):
    pack = pack_of(rows)
    units = source.shape[-1] // pack
    return jnp.concatenate(
        [source[(*index, slice(None), slice(j * units, (j + 1) * units))] for j in range(pack)],
        axis=0,
    )


def split_tiles_kernel(depth, place, gate, upper, down, gain, *rest):
    pieces, parts = rest[:depth], rest[depth]
    units = gate.shape[1] // depth
    for i, (tile, scaled) in enumerate(((gate, True), (upper, True), (down, False))):
        for k in range(depth):
            part = tile[:, k * units : (k + 1) * units]
            if scaled:
                part = (part.astype(F32) * gain[...]).astype(BF16)
            put_packed(parts, (k, i), part)
    for d in range(depth):
        pieces[d][...] = parts[lax.rem(place[AT_Z] + d, depth)]


def merge_tiles_kernel(depth, place, *refs):
    mine, far, outs = refs[:depth], refs[depth : 2 * depth], refs[2 * depth :]
    for d in range(depth):
        from_z = lax.rem(place[AT_Z] - d + depth, depth)
        for i, out in enumerate(outs):
            rows = out.shape[1]
            out[from_z * PAIR + place[AT_X]] = get_packed(mine[d], (i,), rows)
            out[from_z * PAIR + 1 - place[AT_X]] = get_packed(far[d], (i,), rows)


def down_kernel(depth, place, *refs):
    actives, (weight, out) = refs[:depth], refs[depth:]
    count = out.shape[2]
    for d, active in enumerate(actives):
        from_z = lax.rem(place[AT_Z] - d + depth, depth)
        rows = dot_nt(active[...], weight[...])
        for i, other in enumerate((0, 2, 1, 3)):
            out[place[AT_U] ^ other, from_z] = rows[i * count : (i + 1) * count].astype(BF16)


def sort_rows_kernel(place, mine, far, own, near, rows):
    share = own.shape[1]
    for z in range(mine.shape[0]):
        rows[z * PAIR + place[AT_X]] = mine[z]
        rows[z * PAIR + 1 - place[AT_X]] = far[z]

    def part(m):
        return rows[pl.ds((place[AT_U] ^ m) * share, share)]

    own[0], own[1] = part(0), part(1)
    near[0], near[1] = part(2), part(3)


def place_rows_kernel(place, own, near, across, out):
    out[:, place[AT_U]] = own[0]
    out[:, place[AT_U] ^ 2] = near[0]
    out[:, place[AT_U] ^ 1] = across[0]
    out[:, place[AT_U] ^ 3] = across[1]


def weight_grad_kernel(depth, place, *refs):
    rows, grads, (keep, send, total) = refs[:depth], refs[depth : 2 * depth], refs[2 * depth :]
    step = total.shape[0] // 4
    for k in range(4):
        at = slice(k * step, (k + 1) * step)
        part = None
        for row, grad in zip(rows, grads):
            new = dot_tn(row[:, at], grad[...])
            part = new if part is None else part + new
        total[at] = part
    size = total.shape[0] // (depth * PAIR)
    for z in range(depth):
        for out, x in ((keep, place[AT_X]), (send, 1 - place[AT_X])):
            start = pl.multiple_of((z * PAIR + x) * size, 16)
            put_packed(out, (z, 0), total[pl.ds(start, size)].astype(BF16))


def choose_kernel(place, *refs):
    shares, (keep, send) = refs[:-2], refs[-2:]
    for i, share in enumerate(shares):
        keep[:, i] = share[:, place[AT_X]]
        send[:, i] = share[:, 1 - place[AT_X]]


def fold_kernel(depth, place, keep, got, *outs):
    for d in range(depth):
        at = lax.rem(place[AT_Z] + d, depth)
        outs[d][...] = (keep[at].astype(F32) + got[at].astype(F32)).astype(BF16)


def split_uly_kernel(place, pieces, own, near):
    total = None
    parts = []
    for m in range(4):
        total = None
        for z in range(pieces.shape[0]):
            part = pieces[z, 0, place[AT_U] ^ m].astype(F32)
            total = part if total is None else total + part
        parts.append(total.astype(BF16))
    own[0], own[1], near[0], near[1] = parts


def pick_uly_kernel(place, share, own, near):
    own[0], own[1] = share[:, place[AT_U]], share[:, place[AT_U] ^ 1]
    near[0], near[1] = share[:, place[AT_U] ^ 2], share[:, place[AT_U] ^ 3]


def group_rows_kernel(place, own, near, across, keep, send, rows):
    share = own.shape[1]
    for m, part in ((0, own[0]), (2, near[0]), (1, across[0]), (3, across[1])):
        rows[pl.ds((place[AT_U] ^ m) * share, share)] = part
    for z in range(keep.shape[0]):
        keep[z, 0] = rows[z * PAIR + place[AT_X]]
        send[z, 0] = rows[z * PAIR + 1 - place[AT_X]]


def finish_qkv_kernel(place, *refs):
    heads, kinds = refs[:3], refs[3:6]
    weight, gain, grad, grad_gain, bias, head_parts, kind_parts = refs[6:]
    width, side = heads[0].shape[2], heads[0].shape[2] * 4
    for parts, (own, near, across) in ((head_parts, heads), (kind_parts, kinds)):
        parts[place[AT_U]] = own[0]
        parts[place[AT_U] ^ 2] = near[0]
        parts[place[AT_U] ^ 1] = across[0]
        parts[place[AT_U] ^ 3] = across[1]
    total = jnp.zeros(grad_gain.shape, F32)
    for u in range(4):
        bias[u] = kind_parts[u, :16].astype(F32)
        start = side + (u % 2) * KV_HEADS * HEAD_DIM + (u // 2) * HEAD_DIM
        for at, part in (
            (slice(u * width, (u + 1) * width), head_parts[u]),
            (slice(start, start + HEAD_DIM), kind_parts[u, 16:]),
        ):
            part = part.astype(F32)
            grad[:, at] = part * gain[...]
            total = total + jnp.sum(part * weight[:, at].astype(F32), axis=1, keepdims=True)
    grad_gain[...] = total


def finish_kernel(depth, gates, uppers, downs, gate, upper, gain, grad_gate, grad_upper, grad_down, grad_gain):
    rows, units = gate.shape[0], gate.shape[1] // depth
    total = jnp.zeros(grad_gain.shape, F32)
    for k in range(depth):
        at = slice(k * units, (k + 1) * units)
        part = get_packed(gates, (k, 0), rows).astype(F32)
        grad_gate[:, at] = part * gain[...]
        total = total + jnp.sum(part * gate[:, at].astype(F32), axis=1, keepdims=True)
        part = get_packed(uppers, (k, 0), rows).astype(F32)
        grad_upper[:, at] = part * gain[...]
        total = total + jnp.sum(part * upper[:, at].astype(F32), axis=1, keepdims=True)
        grad_down[:, at] = get_packed(downs, (k, 0), rows).astype(F32)
    grad_gain[...] = total


def like(shape, kind=BF16):
    return jax.ShapeDtypeStruct(shape, kind)


def together(*values):
    return lax.optimization_barrier(values)


def after(value, *others):
    return lax.optimization_barrier((value, others))[0]


class Grid:
    def __init__(self):
        self.blocks = lax.axis_size("blk")
        self.ulys = lax.axis_size("uly")
        self.depth = self.blocks // PAIR
        self.b = lax.axis_index("blk")
        self.u = lax.axis_index("uly")
        self.z = self.b // PAIR
        self.x = self.b % PAIR
        self.y = self.u // 2
        self.c = self.u % 2

    def to_z(self, value, step):
        pairs = [
            (z * PAIR + x, ((z + step) % self.depth) * PAIR + x)
            for z in range(self.depth)
            for x in range(PAIR)
        ]
        return lax.ppermute(value, "blk", pairs)

    def swap_x(self, value):
        return lax.ppermute(value, "blk", [(i, i ^ 1) for i in range(self.blocks)])

    def swap_y(self, value):
        return lax.ppermute(value, "uly", [(i, i ^ 2) for i in range(self.ulys)])

    def swap_both(self, value):
        return lax.ppermute(value, "uly", [(i, i ^ 3) for i in range(self.ulys)])

    def swap_core(self, value):
        return lax.ppermute(value, "uly", [(i, i ^ 1) for i in range(self.ulys)])


def paired(bit, mine, other, axis):
    low = jnp.where(bit == 0, mine, other)
    high = jnp.where(bit == 0, other, mine)
    return jnp.stack([low, high], axis=axis)


def pick(bit, array, axis):
    low = lax.index_in_dim(array, 0, axis, keepdims=False)
    high = lax.index_in_dim(array, 1, axis, keepdims=False)
    return jnp.where(bit == 0, low, high), jnp.where(bit == 0, high, low)


def order_z(grid, pieces):
    stacked = jnp.stack(pieces[::-1] + pieces[::-1][:-1])
    start = (grid.depth - 1 - grid.z) % grid.depth
    return lax.dynamic_slice_in_dim(stacked, start, grid.depth, 0)


def gather_uly(grid, value):
    both = paired(grid.y, value, grid.swap_y(value), 0)
    every = paired(grid.c, both, grid.swap_core(both), 1)
    return every.reshape((grid.ulys,) + value.shape)


def scatter_uly(grid, parts, kind=BF16):
    parts = parts.reshape((2, 2) + parts.shape[1:])
    keep, send = pick(grid.c, parts, 1)
    both = keep.astype(F32) + grid.swap_core(send.astype(kind)).astype(F32)
    keep, send = pick(grid.y, both, 0)
    return keep + grid.swap_y(send.astype(kind)).astype(F32)


def gather_blk(grid, value):
    pieces = [value] + [grid.to_z(value, d) for d in range(1, grid.depth)]
    pairs = [paired(grid.x, piece, grid.swap_x(piece), 0) for piece in pieces]
    return order_z(grid, pairs)


def exchange_z(grid, parts):
    pieces = [lax.dynamic_index_in_dim(parts, grid.z, 0, keepdims=False)]
    for d in range(1, grid.depth):
        there = (grid.z + d) % grid.depth
        pieces.append(grid.to_z(lax.dynamic_index_in_dim(parts, there, 0, keepdims=False), d))
    return pieces


def exchange_z_all(grid, parts):
    groups = [[z * PAIR + x for z in range(grid.depth)] for x in range(PAIR)]
    return lax.all_to_all(
        parts, "blk", split_axis=0, concat_axis=0, axis_index_groups=groups, tiled=True
    )


def spread_z(grid, value):
    return exchange_z_all(grid, jnp.broadcast_to(value, (grid.depth, *value.shape)))


def exchange_uly(parts):
    return lax.all_to_all(parts, "uly", split_axis=0, concat_axis=0, tiled=True)


def per_device(
    tokens,
    span_order,
    attn_gain,
    qkv_weight,
    qkv_bias,
    out_weight,
    ffn_gain,
    gate_weight,
    up_weight,
    down_weight,
    cotangent,
):
    grid = Grid()
    local_rows, seqs, model = tokens.shape
    count = local_rows * seqs
    ulys = grid.ulys
    depth = grid.depth
    blocks = grid.blocks
    cycle_rows = local_rows * ulys
    spans = cycle_rows // SPAN
    slots = blocks * spans
    group = HEADS // ulys
    factor = 1.0 / math.sqrt(HEAD_DIM)
    width = group * HEAD_DIM
    columns = width + HEAD_DIM
    shard = qkv_weight.shape[0]
    block_model = shard * ulys
    chunk = math.gcd(slots, 4) * SPAN
    side = HEADS * HEAD_DIM
    place = jnp.stack([grid.z, grid.x, grid.y, grid.c, grid.b, grid.u]).astype(jnp.int32)

    def by_seq(array):
        return jnp.transpose(array, (1, 0, 2)).reshape(count, model)

    def by_row(array):
        return jnp.transpose(array.reshape(seqs, local_rows, model), (1, 0, 2))

    def by_uly(array):
        lead = array.shape[0]
        heads = array[:, :side].reshape(lead, ulys, width)
        kinds = array[:, side:].reshape(lead, 2, KV_HEADS, HEAD_DIM)
        kinds = jnp.transpose(kinds, (0, 2, 1, 3)).reshape(lead, ulys, HEAD_DIM)
        return jnp.transpose(jnp.concatenate([heads, kinds], axis=-1), (1, 0, 2))

    rows = by_seq(tokens).astype(F32)
    unit_one, factor_one = norm_rows(rows)
    unit_own = unit_one.astype(BF16)
    unit_near = grid.swap_y(unit_own)
    gain_one = attn_gain.astype(F32)[:, None]
    scaled = (qkv_weight.astype(F32) * gain_one).astype(BF16)
    heads_share = blocks // ulys
    owned_columns = qkv_bias.shape[0]
    column_start = (grid.b * ulys + grid.u) * owned_columns
    bias_row = lax.dynamic_update_slice(
        jnp.zeros((16, owned_columns * blocks * ulys), BF16),
        jnp.pad(qkv_bias[None], ((0, 15), (0, 0))),
        (0, column_start),
    )
    by_head = by_uly(jnp.concatenate([scaled, bias_row], axis=0))
    by_head = exchange_uly(by_head)
    block_rows = jnp.concatenate(
        [by_head[:, :shard].reshape(block_model, columns), jnp.sum(by_head[:, shard:], axis=0)],
        axis=0,
    )
    qkv_mine = [block_rows] + [grid.to_z(block_rows, d) for d in range(1, depth)]
    first_far = grid.swap_x(block_rows)
    first_arrived = qkv_mine[1]
    *qkv_mine, first_far, unit_near = together(*qkv_mine, first_far, unit_near)

    gain_two = ffn_gain.astype(F32)[:, None]
    hidden_units = gate_weight.shape[1] // depth
    order = sorted(range(1, depth), key=lambda d: (min(d, depth - d), d))
    early, middle, late = order[0], order[1:-1], order[-1]
    split_in = after((gate_weight, up_weight, down_weight), first_arrived)
    split_in = (*split_in[:2], split_in[2].T)
    tile_pieces = call(
        functools.partial(split_tiles_kernel, depth),
        [place],
        [*split_in, gain_two],
        [like((3, *packed(block_model, hidden_units)))] * depth,
        scratch=[pltpu.VMEM((depth, 3, *packed(block_model, hidden_units)), BF16)],
    )
    qkv_far = [first_far] + [grid.swap_x(piece) for piece in qkv_mine[1:]]
    unit_across = grid.swap_core(jnp.stack([unit_own, unit_near]))
    out_first, early_piece = after((out_weight, tile_pieces[early]), *qkv_mine[1:])
    tile_mine = {0: tile_pieces[0], early: grid.to_z(early_piece, early)}
    out_mine = spread_z(grid, out_first)
    tile_far = {0: grid.swap_x(after(tile_pieces[0], qkv_far[1]))}
    *qkv_far, unit_across = together(*qkv_far, unit_across)
    unit_parts = (unit_own, unit_near, unit_across)

    head_rows = grid.b * cycle_rows + jnp.arange(cycle_rows, dtype=jnp.int32)
    places = positions(span_order, head_rows).reshape(seqs, ulys, local_rows)
    places = jnp.transpose(places, (1, 0, 2)).reshape(ulys, count)
    cosine, sine = rope_tables(places)
    units, qkv_part, query, kind = call(
        functools.partial(mix_kernel, depth, group),
        [place],
        [*unit_parts, cosine, sine, *qkv_mine, *qkv_far],
        [
            like((ulys, count, model)),
            like((blocks, block_model, columns)),
            like((ulys, count, width)),
            like((ulys, count, HEAD_DIM)),
        ],
        scratch=[
            pltpu.VMEM((blocks, 16, columns), BF16),
            pltpu.SemaphoreType.DMA((2 * blocks + ulys,)),
        ],
        far=(0, 1, 2, *range(5, 2 * depth + 5)),
    )
    units = units.reshape(ulys * count, model)
    qkv_part = qkv_part.reshape(model, columns)
    kinds = [kind] + [grid.to_z(kind, d) for d in range(1, depth)]
    out_mine, cot_flat = after((out_mine, by_seq(cotangent)), kind)
    out_far = grid.swap_x(out_mine)
    cot_first = cot_flat
    cot_near = grid.swap_y(cot_first)
    *held, late_pair, late_down = after(
        (*[tile_pieces[d] for d in middle], tile_pieces[late][:2], tile_pieces[late][2:]), kinds[1]
    )
    for d, piece in zip(middle, held):
        tile_mine[d] = grid.to_z(after(piece, *kinds[1:]), d)
    out_far, cot_near, tile_mine[early], tile_far[0], *kinds = together(
        out_far, cot_near, tile_mine[early], tile_far[0], *kinds
    )
    late_pair = grid.to_z(after(late_pair, kinds[-1]), late)

    a_own = jnp.stack(kinds)
    a_far = grid.swap_x(a_own)
    b_own = grid.swap_core(a_own)
    out_own, out_near = call(
        sort_rows_kernel,
        [place],
        [out_mine, out_far],
        [like((2, heads_share, shard, model))] * 2,
        scratch=[pltpu.VMEM((blocks, shard, model), BF16)],
    )
    out_near = grid.swap_y(out_near)
    a_far, b_own, out_near, *held = together(
        a_far, b_own, out_near, *[tile_mine[d] for d in middle]
    )
    tile_mine.update(zip(middle, held))

    b_far = grid.swap_core(a_far)
    out_across = grid.swap_core(jnp.stack([out_own[1], out_near[1]]))
    tile_far[early] = grid.swap_x(after(tile_mine[early], a_far))
    b_far, out_across = together(b_far, out_across)

    def over_uly(piece):
        both = jnp.concatenate([piece, grid.swap_y(piece)], axis=0)
        return jnp.concatenate([both, grid.swap_core(both)], axis=0)

    grad_rows = cot_flat.astype(F32)

    scale = factor * LOG2E
    kv_shape = (depth, ulys, seqs, local_rows, HEAD_DIM)
    kv_spec = pl.BlockSpec(
        (depth, ulys, 1, local_rows, HEAD_DIM), lambda s, *unused: (0, 0, s, 0, 0)
    )
    heads_shape = (ulys, seqs, local_rows, width)
    heads_spec = pl.BlockSpec((ulys, 1, local_rows, width), lambda s, *unused: (0, s, 0, 0))
    lse_spec = pl.BlockSpec((1, spans, 1, group * SPAN), lambda s, *unused: (s, 0, 0, 0))
    table_shape = (ulys, seqs, local_rows, HEAD_DIM)
    table_spec = pl.BlockSpec((ulys, 1, local_rows, HEAD_DIM), lambda s, *unused: (0, s, 0, 0))
    sorted_spec = pl.BlockSpec((1, 2, slots * SPAN, HEAD_DIM), lambda s, *unused: (s, 0, 0, 0))
    params = pltpu.CompilerParams(vmem_limit_bytes=VMEM_LIMIT)
    query = query.reshape(heads_shape)
    attended, lse, kv = pl.pallas_call(
        functools.partial(attend_kernel, depth, spans, chunk, group, scale),
        grid_spec=pltpu.PrefetchScalarGridSpec(
            num_scalar_prefetch=2,
            grid=(seqs,),
            in_specs=[heads_spec] + [kv_spec] * 4,
            out_specs=[heads_spec, lse_spec, sorted_spec],
        ),
        out_shape=[
            like(heads_shape),
            like((seqs, spans, 1, group * SPAN), F32),
            like((seqs, 2, slots * SPAN, HEAD_DIM)),
        ],
        compiler_params=params,
        cost_estimate=SMALL,
    )(span_order, place, query, *[part.reshape(kv_shape) for part in (a_own, a_far, b_own, b_far)])
    flat = attended.reshape(ulys, count, width)
    out_own, tile_far[early], late_pair, attended = together(
        out_own, tile_far[early], late_pair, attended
    )
    late_down = grid.to_z(after(late_down, attended), late)
    flat = attended.reshape(ulys, count, width)
    for d in middle:
        tile_far[d] = grid.swap_x(after(tile_mine[d], attended))
    (out_part,) = call(
        place_rows_kernel, [place], [out_own, out_near, out_across], [like((heads_share, ulys, shard, model))]
    )
    out_part = out_part.reshape(width, model)
    keep, send = call(
        functools.partial(project_kernel, False),
        [place],
        [flat, out_part],
        [like((2, count, model), F32), like((2, count, model))],
    )
    got = grid.swap_core(send)
    both = keep + got.astype(F32)
    got = grid.swap_y(both[1].astype(BF16))
    got, late_down, *held = together(got, late_down, *[tile_far[d] for d in middle])
    tile_mine[late] = jnp.concatenate([late_pair, late_down])
    tile_far.update(zip(middle, held))
    tile_far[late] = grid.swap_x(after(tile_mine[late], got))
    hidden = rows + both[0] + got.astype(F32)

    unit_two, factor_two = norm_rows(hidden)
    mid_own = unit_two.astype(BF16)
    mid_near = grid.swap_y(mid_own)
    mid_pieces = [mid_own, grid.to_z(mid_own, 1)]
    cot_pieces = [cot_first, grid.to_z(after(cot_first, mid_near), 1)]
    mid_near, tile_far[late] = together(mid_near, tile_far[late])
    for d in range(2, depth):
        mid_pieces.append(grid.to_z(mid_pieces[-1], 1))
        cot_pieces.append(grid.to_z(cot_pieces[-1], 1))

    def chunk_of(own, near):
        both = jnp.concatenate([own, near], axis=0)
        return jnp.concatenate([both, grid.swap_core(both)], axis=0)

    mid_chunks = [chunk_of(mid_own, mid_near)] + [over_uly(piece) for piece in mid_pieces[1:]]
    cot_chunks = [chunk_of(cot_first, cot_near)] + [over_uly(piece) for piece in cot_pieces[1:]]
    gate_used, upper_used, down_used = [
        tile.reshape(model, hidden_units)
        for tile in call(
            functools.partial(merge_tiles_kernel, depth),
            [place],
            [tile_mine[d] for d in range(depth)] + [tile_far[d] for d in range(depth)],
            [like((blocks, block_model, hidden_units))] * 3,
        )
    ]
    actives, gate_grads, upper_grads, back_chunks = [], [], [], []
    for mid, cot in zip(mid_chunks, cot_chunks):
        gate = matmul(mid, gate_used)
        upper = matmul(mid, upper_used)
        sigmoid = jax.nn.sigmoid(gate)
        active_grad = matmul(cot, down_used)
        actives.append((gate * sigmoid * upper).astype(BF16))
        gate_grad = (active_grad * upper * sigmoid * (1.0 + gate * (1.0 - sigmoid))).astype(BF16)
        upper_grad = (active_grad * gate * sigmoid).astype(BF16)
        gate_grads.append(gate_grad)
        upper_grads.append(upper_grad)
        back_chunks.append(
            contract_cols(gate_grad, gate_used) + contract_cols(upper_grad, upper_used)
        )
    def over_core(chunk):
        chunk = chunk.reshape(2, 2, count, model)
        return chunk[0].astype(F32) + grid.swap_core(chunk[1].astype(BF16)).astype(F32)

    def over_y(both):
        return both[0] + grid.swap_y(both[1].astype(BF16)).astype(F32)

    def halve(shares, rows):
        shape = (depth, PAIR, *rows, shares[0].shape[-1])
        shares = [share.astype(BF16).reshape(shape) for share in shares]
        half = like((depth, len(shares), *rows, shape[-1]))
        return call(choose_kernel, [place], shares, [half] * 2)

    def weight_grad(rows, grads):
        half = like((depth, 1, *packed(block_model, hidden_units)))
        return call(
            functools.partial(weight_grad_kernel, depth),
            [place],
            [*rows, *grads],
            [half] * 2,
            scratch=[pltpu.VMEM((model, hidden_units), F32)],
            single=depth > 4,
        )

    def fold(keep, got):
        return exchange_z_all(grid, (keep.astype(F32) + got.astype(F32)).astype(BF16))

    z_groups = [[z * PAIR + x for z in range(depth)] for x in range(PAIR)]
    boths = [over_core(chunk) for chunk in back_chunks]
    mid_parts = [over_y(both) for both in boths]
    back_pieces = [grid.to_z(mid_parts[d].astype(BF16), -d) for d in range(1, depth)]
    mid_all = tuple(mid_chunks)
    mid_now = after(mid_all, back_chunks[-1], *boths[:-1], *mid_parts[:-1])
    gate_keep, gate_send = weight_grad(mid_now, gate_grads)
    mid_now = after(mid_all, gate_send, *mid_parts, back_pieces[0])
    upper_keep, upper_send = weight_grad(mid_now, upper_grads)
    gate_got = grid.swap_x(gate_send)
    first, gate_got, upper_send, *back_pieces = together(
        mid_parts[0], gate_got, upper_send, *back_pieces
    )
    mid_grad = first + sum(piece.astype(F32) for piece in back_pieces)

    hidden_grad = grad_rows + norm_back(mid_grad, unit_two, factor_two)
    branch_own = hidden_grad.astype(BF16)
    branch_near = grid.swap_y(branch_own)
    upper_got = grid.swap_x(after(upper_send, gate_got))
    gate_owned = fold(*after((gate_keep, gate_got), branch_own))
    down_keep, down_send = weight_grad(after(tuple(cot_chunks), branch_own), actives)
    down_send, branch_near, upper_got = together(down_send, branch_near, upper_got)
    down_got = grid.swap_x(down_send)
    branch_across = grid.swap_core(jnp.stack([branch_own, branch_near]))
    branch_parts = (branch_own, branch_near, branch_across)
    (grad_heads,) = call(
        heads_grad_kernel, [place], [*branch_parts, out_part], [like((ulys, count, width))]
    )

    grad_heads, gate_owned = together(grad_heads.reshape(heads_shape), gate_owned)
    upper_owned = fold(*after((upper_keep, upper_got), gate_owned))
    both_spec = pl.BlockSpec(
        (2, depth, ulys, 1, local_rows, HEAD_DIM), lambda s, *unused: (0, 0, 0, s, 0, 0)
    )
    query_grad, keep_own, keep_far, send_both = pl.pallas_call(
        functools.partial(attend_back_kernel, depth, spans, chunk, group, scale, factor),
        grid_spec=pltpu.PrefetchScalarGridSpec(
            num_scalar_prefetch=2,
            grid=(seqs,),
            in_specs=[heads_spec, sorted_spec]
            + [heads_spec] * 2
            + [lse_spec]
            + [table_spec] * 2,
            out_specs=[heads_spec] + [kv_spec] * 2 + [both_spec],
            scratch_shapes=[pltpu.VMEM((2, slots * SPAN, HEAD_DIM), F32)],
        ),
        out_shape=[like(heads_shape)] + [like(kv_shape)] * 2 + [like((2, *kv_shape))],
        compiler_params=params,
        cost_estimate=SMALL,
    )(
        span_order,
        place,
        query,
        kv,
        grad_heads,
        attended,
        lse,
        cosine.reshape(table_shape),
        sine.reshape(table_shape),
    )
    got_far, got_own = [
        jnp.concatenate([grid.swap_core(part) for part in jnp.split(send_both[k], 2, axis=0)])
        for k in (1, 0)
    ]
    query_grad = query_grad.reshape(ulys * count, width)
    got_far, got_own, query_grad, upper_owned = together(
        got_far, got_own, query_grad, upper_owned
    )
    (out_all,) = call(
        functools.partial(down_kernel, depth),
        [place],
        [*after(tuple(actives), got_far), down_used],
        [like((ulys, depth, count, model))],
    )
    from_x = grid.swap_x((keep_far.astype(F32) + got_far.astype(F32)).astype(BF16))
    share_parts = after(branch_parts, got_far)
    (out_share,) = call(out_share_kernel, [place], [*share_parts, flat], [like((width, model))])
    out_own, out_near = call(
        pick_uly_kernel,
        [place],
        [out_share.reshape(heads_share, ulys, shard, model)],
        [like((2, heads_share, shard, model))] * 2,
    )
    head_keep, head_send = halve([contract_rows(units, query_grad)], (ulys, shard))
    from_x, head_send, out_near, out_all, down_got = together(
        from_x, head_send, out_near, out_all, down_got
    )
    out_all = lax.psum_scatter(out_all, "uly", scatter_dimension=0, tiled=False)
    kind_parts = keep_own.astype(F32) + got_own.astype(F32) + from_x.astype(F32)
    kind_parts = kind_parts.astype(BF16)
    kind_back = [grid.to_z(kind_parts[d], -d) for d in range(1, depth)]
    head_got = grid.swap_x(head_send)
    out_near = grid.swap_y(out_near)
    *kind_back, out_near, kind_parts, head_got = together(
        *kind_back, out_near, kind_parts, head_got
    )
    out_across = grid.swap_core(jnp.stack([out_own[1], out_near[1]]))
    kind_grad = kind_parts[0].astype(F32)
    for piece in kind_back:
        kind_grad = kind_grad + piece.astype(F32)
    kind_grad = kind_grad.reshape(ulys * count, HEAD_DIM)
    turned = jnp.roll(kind_grad, HEAD_DIM // 2, axis=1)
    is_key = grid.c == 0
    flat_cosine = cosine.reshape(ulys * count, HEAD_DIM)
    flat_sine = sine.reshape(ulys * count, HEAD_DIM)
    kind_grad = jnp.where(is_key, kind_grad * flat_cosine - turned * flat_sine, kind_grad)
    kind_grad = kind_grad.astype(BF16)

    bias = jnp.sum(query_grad.astype(F32), axis=0).reshape(group, HEAD_DIM)
    bias = jnp.concatenate([bias, jnp.sum(kind_grad.astype(F32), axis=0)[None]], axis=0)
    bias = jnp.pad(bias.astype(BF16), ((0, 16 - group - 1), (0, 0)))
    bias = jnp.broadcast_to(bias, (blocks, ulys, 16, HEAD_DIM))
    share = contract_rows(units, kind_grad).astype(BF16)
    share = share.reshape(blocks, ulys, shard, HEAD_DIM)
    share = jnp.concatenate([bias, share], axis=2)
    kind_keep, kind_send = halve([share], (ulys, shard + 16))
    kind_got = grid.swap_x(kind_send)
    out_all = lax.psum_scatter(
        after(out_all, kind_send), "blk", scatter_dimension=0, axis_index_groups=z_groups, tiled=False
    )
    head_pieces = fold(*after((head_keep, head_got), kind_send))
    out_across = after(out_across, kind_send)
    out_keep, out_send = call(
        group_rows_kernel,
        [place],
        [out_own, out_near, out_across],
        [like((depth, 1, shard, model))] * 2,
        scratch=[pltpu.VMEM((blocks, shard, model), BF16)],
    )
    out_got = grid.swap_x(after(out_send, kind_got))
    kind_pieces = call(
        functools.partial(fold_kernel, depth),
        [place],
        [kind_keep, kind_got],
        [like(kind_keep.shape[1:])] * depth,
    )
    kind_pieces = [kind_pieces[0]] + [grid.to_z(kind_pieces[d], d) for d in range(1, depth)]
    kind_pieces = jnp.stack(kind_pieces)
    kind_pieces, out_got = together(kind_pieces, out_got)
    kind_now = after(kind_grad, kind_pieces)
    keep, send = call(
        functools.partial(project_kernel, True),
        [place],
        [
            query_grad.reshape(ulys, count, width),
            kind_now.reshape(ulys, count, HEAD_DIM),
            qkv_part[:, :width],
            qkv_part[:, width:],
        ],
        [like((2, count, model), F32), like((2, count, model))],
    )
    both = keep + grid.swap_core(send).astype(F32)
    down_owned = fold(*after((down_keep, down_got), head_pieces))
    out_pieces = call(
        functools.partial(fold_kernel, depth),
        [place],
        [out_keep, out_got],
        [like(out_keep.shape[1:])] * depth,
    )
    out_pieces = [out_pieces[0]] + [grid.to_z(out_pieces[d], d) for d in range(1, depth)]

    def to_owners(pieces):
        own, near = call(
            split_uly_kernel, [place], [pieces], [like((2, *pieces.shape[3:]))] * 2
        )
        near = grid.swap_y(near)
        return own, near, grid.swap_core(jnp.stack([own[1], near[1]]))

    head_owned = to_owners(head_pieces)
    kind_owned = to_owners(kind_pieces)
    grad_qkv, grad_gain_one, bias = call(
        finish_qkv_kernel,
        [place],
        [*head_owned, *kind_owned, qkv_weight, gain_one],
        [
            like(qkv_weight.shape, F32),
            like((shard, 1), F32),
            like((ulys, 16, HEAD_DIM), F32),
        ],
        scratch=[
            pltpu.VMEM((ulys, shard, width), BF16),
            pltpu.VMEM((ulys, shard + 16, HEAD_DIM), BF16),
        ],
    )
    grad_gain_one = grad_gain_one[:, 0]
    kind_bias = bias[:, group].reshape(KV_HEADS, 2, HEAD_DIM)
    bias = jnp.concatenate(
        [bias[:, :group].reshape(-1), jnp.transpose(kind_bias, (1, 0, 2)).reshape(-1)]
    )
    grad_bias = lax.dynamic_slice_in_dim(bias, column_start, owned_columns, 0)
    grad_out = sum(piece[0].astype(F32) for piece in out_pieces)
    result = hidden + after(out_all, grad_qkv).astype(F32)
    output = by_row(result.astype(BF16))
    normed_grad = both[0] + grid.swap_y(both[1].astype(BF16)).astype(F32)
    grad_tokens = by_row(hidden_grad + norm_back(normed_grad, unit_one, factor_one))
    tile_shape = gate_weight.shape
    grad_gate, grad_upper, grad_down, gain_part = call(
        functools.partial(finish_kernel, depth),
        [],
        [gate_owned, upper_owned, after(down_owned, grad_qkv), gate_weight, up_weight, gain_two],
        [like(tile_shape, F32)] * 3 + [like((block_model, 1), F32)],
    )
    grad_down = grad_down.T
    grad_gain_two = scatter_uly(grid, gain_part.reshape(ulys, -1), F32)
    return (
        output,
        grad_tokens,
        grad_gain_one,
        grad_qkv,
        grad_bias,
        grad_out,
        grad_gain_two.reshape(-1),
        grad_gate,
        grad_upper,
        grad_down,
    )


def solution(mesh):
    in_specs = (
        P(("blk", "uly"), None, None),
        P(),
        P(("blk", "uly")),
        P(("blk", "uly"), None),
        P(("blk", "uly")),
        P(("blk", "uly"), None),
        P("blk"),
        P("blk", "uly"),
        P("blk", "uly"),
        P("uly", "blk"),
        P(("blk", "uly"), None, None),
    )
    out_specs = (
        P(("blk", "uly"), None, None),
        P(("blk", "uly"), None, None),
        P(("blk", "uly")),
        P(("blk", "uly"), None),
        P(("blk", "uly")),
        P(("blk", "uly"), None),
        P(("blk", "uly")),
        P("blk", "uly"),
        P("blk", "uly"),
        P("uly", "blk"),
    )
    return jax.shard_map(
        per_device, mesh=mesh, in_specs=in_specs, out_specs=out_specs, check_vma=False
    )
```

```python
import functools
import math

import jax
import jax.numpy as jnp
from jax import lax
from jax.experimental import pallas as pl
from jax.experimental.pallas import tpu as pltpu
from jax.sharding import PartitionSpec as P

HEADS = 12
KV_HEADS = 2
HEAD_DIM = 128
SPAN = 128
PAIR = 2


EPS = 1e-06
THETA = 1000000.0
FLOOR = -1e30
LOG2E = 1.4426950408889634
BF16 = jnp.bfloat16
F32 = jnp.float32
SMALL = pl.CostEstimate(flops=1, transcendentals=0, bytes_accessed=1)
VMEM_LIMIT = 48 * 1024 * 1024

def norm_rows(rows):
    factor = lax.rsqrt(jnp.mean(rows * rows, axis=-1, keepdims=True) + EPS)
    return (rows * factor, factor)


def norm_back(scaled, unit, factor):
    return factor * (scaled - unit * jnp.mean(scaled * unit, axis=-1, keepdims=True))


def matmul(left, right):
    return jnp.dot(left, right, preferred_element_type=F32)


def contract_rows(left, right):
    return lax.dot_general(left, right, (((0,), (0,)), ((), ())), preferred_element_type=F32)


def contract_cols(left, right):
    return lax.dot_general(left, right, (((1,), (1,)), ((), ())), preferred_element_type=F32)


def positions(order, rows):
    table = jnp.arange(order.shape[1], dtype=jnp.int32)
    slots = rows // SPAN
    picked = jnp.where(slots[None, :, None] == table[None, None, :], order[:, None, :], 0)
    return jnp.sum(picked, axis=-1) * SPAN + (rows % SPAN)[None, :]


def rope_tables(places):
    index = jnp.arange(HEAD_DIM // 2).astype(F32)
    freq = THETA ** (-2.0 * index / HEAD_DIM)
    angle = places.astype(F32)[..., None] * freq
    cosine, sine = jnp.cos(angle), jnp.sin(angle)
    cosine = jnp.concatenate([cosine, cosine], axis=-1)
    return (cosine, jnp.concatenate([-sine, sine], axis=-1))


def dot_nn(left, right):
    return lax.dot_general(left, right, (((1,), (0,)), ((), ())), preferred_element_type=F32)


def dot_nt(left, right):
    return lax.dot_general(left, right, (((1,), (1,)), ((), ())), preferred_element_type=F32)


def dot_tn(left, right):
    return lax.dot_general(left, right, (((0,), (0,)), ((), ())), preferred_element_type=F32)


def call(kernel, scalars, arrays, outs, **options):
    return pl.pallas_call(
        kernel,
        grid_spec=pltpu.PrefetchScalarGridSpec(
            num_scalar_prefetch=len(scalars),
            grid=(1,),
            in_specs=[
                pl.BlockSpec(memory_space=pltpu.HBM) if i in options.get("far", ()) else whole(array.shape, options.get("single", False))
                for i, array in enumerate(arrays)
            ],
            out_specs=[whole(out.shape, options.get("single", False)) for out in outs],
            scratch_shapes=options.get("scratch", ()),
        ),
        out_shape=outs,
        compiler_params=pltpu.CompilerParams(vmem_limit_bytes=VMEM_LIMIT),
        cost_estimate=SMALL,
    )(*scalars, *arrays)


def whole(shape, single=False):
    mode = pl.Buffered(buffer_count=1) if single else None
    return pl.BlockSpec(shape, lambda *unused: (0,) * len(shape), pipeline_mode=mode)


def turn(field):
    return pltpu.roll(field, HEAD_DIM // 2, 1)


AT_Z, AT_X, AT_Y, AT_C, AT_B, AT_U = range(6)


def mix_kernel(depth, group, place, own, near, across, cosine, sine, *rest):
    pieces, far = rest[:depth], rest[depth : 2 * depth]
    units, weights, query, kind, bias_rows, flags = rest[2 * depth :]
    u = place[AT_U]
    rows = weights.shape[1]
    copies = []

    def bring(source, target):
        copies.append(pltpu.make_async_copy(source, target, flags.at[len(copies)]))
        copies[-1].start()

    for d in range(depth):
        from_z = lax.rem(place[AT_Z] - d + depth, depth)
        for k in range(PAIR):
            piece = far[d] if k else pieces[d]
            from_x = place[AT_X] if k == 0 else 1 - place[AT_X]
            bring(piece.at[pl.ds(0, rows)], weights.at[from_z * PAIR + from_x])
            bring(piece.at[pl.ds(rows, 16)], bias_rows.at[PAIR * d + k])
    bring(own, units.at[u])
    bring(near, units.at[u ^ 2])
    bring(across.at[0], units.at[u ^ 1])
    bring(across.at[1], units.at[u ^ 3])
    for copy in copies:
        copy.wait()
    bias = jnp.sum(bias_rows[...].astype(F32), axis=(0, 1))[None]
    model = units.shape[2]
    all_weights = weights[...].reshape(model, weights.shape[2])
    is_key = place[AT_C] == 0
    for i in range(units.shape[0]):
        mixed = dot_nn(units[i], all_weights) + bias
        cos, sin = cosine[i], sine[i]
        for h in range(group):
            field = mixed[:, h * HEAD_DIM : (h + 1) * HEAD_DIM]
            query[i, :, h * HEAD_DIM : (h + 1) * HEAD_DIM] = (field * cos + turn(field) * sin).astype(
                BF16
            )
        field = mixed[:, group * HEAD_DIM :]
        turned = field * cos + turn(field) * sin
        kind[i] = jnp.where(is_key, turned, field).astype(BF16)


def stack_heads(block, group):
    block = block.reshape(SPAN, group * HEAD_DIM)
    return jnp.concatenate(
        [block[:, h * HEAD_DIM : (h + 1) * HEAD_DIM] for h in range(group)], axis=0
    )


def key_mask(first_key, keys, place, group):
    key = first_key + lax.broadcasted_iota(jnp.int32, (keys, group * SPAN), 0)
    row = lax.broadcasted_iota(jnp.int32, (keys, group * SPAN), 1) % SPAN
    return key <= place * SPAN + row


def attend_kernel(
    depth, spans, chunk, group, scale, order, place, query, a_own, a_far, b_own, b_far, out, lse, kv
):
    seq = pl.program_id(0)
    core, x, z = place[AT_C], place[AT_X], place[AT_Z]
    step = query.shape[0] // spans
    slots = depth * PAIR * spans

    def settle(slot, unused):
        blk, span = slot // spans, lax.rem(slot, spans)
        d = lax.rem(z - blk // PAIR + depth, depth)
        there = pl.ds(pl.multiple_of(order[seq, slot] * SPAN, SPAN), SPAN)
        here = pl.ds(span * step, step)
        for mine, other, far in ((a_own, b_own, False), (a_far, b_far, True)):

            @pl.when((lax.rem(blk, PAIR) != x) == far)
            def unused_copy():
                kv[0, core, there] = mine[d, here, 0].reshape(SPAN, HEAD_DIM)
                kv[0, 1 - core, there] = other[d, here, 0].reshape(SPAN, HEAD_DIM)

        return 0

    lax.fori_loop(0, slots, settle, 0)
    for span in range(spans):
        spot = order[seq, place[AT_B] * spans + span]
        queries = stack_heads(query[span * step : (span + 1) * step, 0], group)

        def advance(index, state, masked):
            peak, total, summed = state
            keys = pl.ds(pl.multiple_of(index * chunk, chunk), chunk)
            scores = dot_nt(kv[0, 0, keys], queries)
            if masked:
                allowed = key_mask(index * chunk, chunk, spot, group)
                scores = jnp.where(allowed, scores, FLOOR)
            new_peak = jnp.maximum(peak, jnp.max(scores, axis=0, keepdims=True))
            weights = jnp.exp2((scores - new_peak) * scale)
            fade = jnp.exp2((peak - new_peak) * scale)
            total = total * fade + jnp.sum(weights, axis=0, keepdims=True)
            summed = summed * fade + dot_tn(kv[0, 1, keys], weights.astype(BF16))
            return new_peak, total, summed

        start = (
            jnp.full((1, group * SPAN), FLOOR, F32),
            jnp.zeros((1, group * SPAN), F32),
            jnp.zeros((HEAD_DIM, group * SPAN), F32),
        )
        last = spot * SPAN // chunk
        state = lax.fori_loop(0, last, lambda i, s: advance(i, s, False), start)
        peak, total, summed = advance(last, state, True)
        lse[0, span] = peak * scale + jnp.log2(total)
        result = (summed / total).T.astype(BF16)
        for h in range(group):
            out[span * step : (span + 1) * step, 0, :, h * HEAD_DIM : (h + 1) * HEAD_DIM] = result[
                h * SPAN : (h + 1) * SPAN
            ].reshape(step, SPAN // step, HEAD_DIM)


def attend_back_kernel(
    depth,
    spans,
    chunk,
    group,
    scale,
    factor,
    order,
    place,
    query,
    kv,
    grad,
    out,
    lse,
    cosine,
    sine,
    query_grad,
    keep_own,
    keep_far,
    send_both,
    sums,
):
    seq = pl.program_id(0)
    core, x, z = place[AT_C], place[AT_X], place[AT_Z]
    step = query.shape[0] // spans
    slots = depth * PAIR * spans
    sums[...] = jnp.zeros(sums.shape, F32)
    for span in range(spans):
        spot = order[seq, place[AT_B] * spans + span]
        at = slice(span * step, (span + 1) * step)
        queries = stack_heads(query[at, 0], group)
        grads = stack_heads(grad[at, 0], group)
        results = stack_heads(out[at, 0], group)
        delta = jnp.sum(
            (grads.astype(F32) * results.astype(F32)).T, axis=0, keepdims=True
        )
        level = lse[0, span]

        def advance(index, total, masked):
            keys = pl.ds(pl.multiple_of(index * chunk, chunk), chunk)
            key, value = kv[0, 0, keys], kv[0, 1, keys]
            probs = jnp.exp2(dot_nt(key, queries) * scale - level)
            if masked:
                probs = jnp.where(key_mask(index * chunk, chunk, spot, group), probs, 0.0)
            score_grad = (probs * (dot_nt(value, grads) - delta)).astype(BF16)
            sums[1, keys] += dot_nn(probs.astype(BF16), grads)
            sums[0, keys] += dot_nn(score_grad, queries)
            return total + dot_tn(key, score_grad)

        last = spot * SPAN // chunk
        total = jnp.zeros((HEAD_DIM, group * SPAN), F32)
        total = lax.fori_loop(0, last, lambda i, s: advance(i, s, False), total)
        total = (advance(last, total, True) * factor).T
        cos = cosine[at, 0].reshape(SPAN, HEAD_DIM)
        sin = sine[at, 0].reshape(SPAN, HEAD_DIM)
        for h in range(group):
            field = total[h * SPAN : (h + 1) * SPAN]
            field = (field * cos - turn(field) * sin).astype(BF16)
            query_grad[at, 0, :, h * HEAD_DIM : (h + 1) * HEAD_DIM] = field.reshape(
                step, SPAN // step, HEAD_DIM
            )

    keep_scale = jnp.where(core == 0, factor, 1.0)
    send_scale = jnp.where(core == 0, 1.0, factor)

    def settle(slot, unused):
        blk, span = slot // spans, lax.rem(slot, spans)
        d = lax.rem(z - blk // PAIR + depth, depth)
        there = pl.ds(pl.multiple_of(order[seq, slot] * SPAN, SPAN), SPAN)
        here = pl.ds(span * step, step)
        shape = (step, SPAN // step, HEAD_DIM)
        for keep, send, far in ((keep_own, 0, False), (keep_far, 1, True)):

            @pl.when((lax.rem(blk, PAIR) != x) == far)
            def unused_copy():
                keep[d, here, 0] = (sums[core, there] * keep_scale).astype(BF16).reshape(shape)
                send_both[send, d, here, 0] = (sums[1 - core, there] * send_scale).astype(BF16).reshape(shape)

        return 0

    lax.fori_loop(0, slots, settle, 0)


def project_kernel(transposed, place, *refs):
    lefts, (weights, keep, send) = refs[:-3], refs[-3:]
    u = place[AT_U]
    dot = dot_nt if transposed else dot_nn
    rights, start = [], 0
    for left in lefts:
        size = left.shape[-1]
        at = slice(start, start + size)
        rights.append(weights[:, at] if transposed else weights[at])
        start += size
    for at, target, spot in ((1, send, 0), (3, send, 1), (0, keep, 0), (2, keep, 1)):
        total = None
        for left, right in zip(lefts, rights):
            part = dot(left[u ^ at], right)
            total = part if total is None else total + part
        target[spot] = total.astype(target.dtype)


def heads_grad_kernel(place, own, near, across, weights, out):
    u = place[AT_U]
    for at, piece in ((0, own[...]), (2, near[...]), (1, across[0]), (3, across[1])):
        out[u ^ at] = dot_nt(piece, weights[...]).astype(BF16)


def out_share_kernel(place, own, near, across, attended, out):
    u = place[AT_U]
    total = dot_tn(attended[u], own[...])
    total = total + dot_tn(attended[u ^ 2], near[...])
    total = total + dot_tn(attended[u ^ 1], across[0])
    total = total + dot_tn(attended[u ^ 3], across[1])
    out[...] = total.astype(BF16)


def pack_of(rows):
    return 2 if rows % 32 == 0 else 1


def packed(rows, units):
    pack = pack_of(rows)
    return (rows // pack, units * pack)


def put_packed(target, index, part):
    rows, units = part.shape
    size = rows // pack_of(rows)
    for j in range(pack_of(rows)):
        target[(*index, slice(None), slice(j * units, (j + 1) * units))] = part[
            j * size : (j + 1) * size
        ]


def get_packed(source, index, rows):
    pack = pack_of(rows)
    units = source.shape[-1] // pack
    return jnp.concatenate(
        [source[(*index, slice(None), slice(j * units, (j + 1) * units))] for j in range(pack)],
        axis=0,
    )


def split_tiles_kernel(depth, place, gate, upper, down, gain, *rest):
    pieces, parts = rest[:depth], rest[depth]
    units = gate.shape[1] // depth
    for i, (tile, scaled) in enumerate(((gate, True), (upper, True), (down, False))):
        for k in range(depth):
            part = tile[:, k * units : (k + 1) * units]
            if scaled:
                part = (part.astype(F32) * gain[...]).astype(BF16)
            put_packed(parts, (k, i), part)
    for d in range(depth):
        pieces[d][...] = parts[lax.rem(place[AT_Z] + d, depth)]


def merge_tiles_kernel(depth, place, *refs):
    mine, far, outs = refs[:depth], refs[depth : 2 * depth], refs[2 * depth :]
    for d in range(depth):
        from_z = lax.rem(place[AT_Z] - d + depth, depth)
        for i, out in enumerate(outs):
            rows = out.shape[1]
            out[from_z * PAIR + place[AT_X]] = get_packed(mine[d], (i,), rows)
            out[from_z * PAIR + 1 - place[AT_X]] = get_packed(far[d], (i,), rows)


def down_kernel(depth, place, *refs):
    actives, (weight, out) = refs[:depth], refs[depth:]
    count = out.shape[2]
    for d, active in enumerate(actives):
        from_z = lax.rem(place[AT_Z] - d + depth, depth)
        rows = dot_nt(active[...], weight[...])
        for i, other in enumerate((0, 2, 1, 3)):
            out[place[AT_U] ^ other, from_z] = rows[i * count : (i + 1) * count].astype(BF16)


def sort_rows_kernel(place, mine, far, own, near, rows):
    share = own.shape[1]
    for z in range(mine.shape[0]):
        rows[z * PAIR + place[AT_X]] = mine[z]
        rows[z * PAIR + 1 - place[AT_X]] = far[z]

    def part(m):
        return rows[pl.ds((place[AT_U] ^ m) * share, share)]

    own[0], own[1] = part(0), part(1)
    near[0], near[1] = part(2), part(3)


def place_rows_kernel(place, own, near, across, out):
    out[:, place[AT_U]] = own[0]
    out[:, place[AT_U] ^ 2] = near[0]
    out[:, place[AT_U] ^ 1] = across[0]
    out[:, place[AT_U] ^ 3] = across[1]


def weight_grad_kernel(depth, place, *refs):
    rows, grads, (keep, send, total) = refs[:depth], refs[depth : 2 * depth], refs[2 * depth :]
    step = total.shape[0] // 4
    for k in range(4):
        at = slice(k * step, (k + 1) * step)
        part = None
        for row, grad in zip(rows, grads):
            new = dot_tn(row[:, at], grad[...])
            part = new if part is None else part + new
        total[at] = part
    size = total.shape[0] // (depth * PAIR)
    for z in range(depth):
        for out, x in ((keep, place[AT_X]), (send, 1 - place[AT_X])):
            start = pl.multiple_of((z * PAIR + x) * size, 16)
            put_packed(out, (z, 0), total[pl.ds(start, size)].astype(BF16))


def choose_kernel(place, *refs):
    shares, (keep, send) = refs[:-2], refs[-2:]
    for i, share in enumerate(shares):
        keep[:, i] = share[:, place[AT_X]]
        send[:, i] = share[:, 1 - place[AT_X]]


def fold_kernel(depth, place, keep, got, *outs):
    for d in range(depth):
        at = lax.rem(place[AT_Z] + d, depth)
        outs[d][...] = (keep[at].astype(F32) + got[at].astype(F32)).astype(BF16)


def split_uly_kernel(place, pieces, own, near):
    total = None
    parts = []
    for m in range(4):
        total = None
        for z in range(pieces.shape[0]):
            part = pieces[z, 0, place[AT_U] ^ m].astype(F32)
            total = part if total is None else total + part
        parts.append(total.astype(BF16))
    own[0], own[1], near[0], near[1] = parts


def pick_uly_kernel(place, share, own, near):
    own[0], own[1] = share[:, place[AT_U]], share[:, place[AT_U] ^ 1]
    near[0], near[1] = share[:, place[AT_U] ^ 2], share[:, place[AT_U] ^ 3]


def group_rows_kernel(place, own, near, across, keep, send, rows):
    share = own.shape[1]
    for m, part in ((0, own[0]), (2, near[0]), (1, across[0]), (3, across[1])):
        rows[pl.ds((place[AT_U] ^ m) * share, share)] = part
    for z in range(keep.shape[0]):
        keep[z, 0] = rows[z * PAIR + place[AT_X]]
        send[z, 0] = rows[z * PAIR + 1 - place[AT_X]]


def finish_qkv_kernel(place, *refs):
    heads, kinds = refs[:3], refs[3:6]
    weight, gain, grad, grad_gain, bias, head_parts, kind_parts = refs[6:]
    width, side = heads[0].shape[2], heads[0].shape[2] * 4
    for parts, (own, near, across) in ((head_parts, heads), (kind_parts, kinds)):
        parts[place[AT_U]] = own[0]
        parts[place[AT_U] ^ 2] = near[0]
        parts[place[AT_U] ^ 1] = across[0]
        parts[place[AT_U] ^ 3] = across[1]
    total = jnp.zeros(grad_gain.shape, F32)
    for u in range(4):
        bias[u] = kind_parts[u, :16].astype(F32)
        start = side + (u % 2) * KV_HEADS * HEAD_DIM + (u // 2) * HEAD_DIM
        for at, part in (
            (slice(u * width, (u + 1) * width), head_parts[u]),
            (slice(start, start + HEAD_DIM), kind_parts[u, 16:]),
        ):
            part = part.astype(F32)
            grad[:, at] = part * gain[...]
            total = total + jnp.sum(part * weight[:, at].astype(F32), axis=1, keepdims=True)
    grad_gain[...] = total


def finish_kernel(depth, gates, uppers, downs, gate, upper, gain, grad_gate, grad_upper, grad_down, grad_gain):
    rows, units = gate.shape[0], gate.shape[1] // depth
    total = jnp.zeros(grad_gain.shape, F32)
    for k in range(depth):
        at = slice(k * units, (k + 1) * units)
        part = get_packed(gates, (k, 0), rows).astype(F32)
        grad_gate[:, at] = part * gain[...]
        total = total + jnp.sum(part * gate[:, at].astype(F32), axis=1, keepdims=True)
        part = get_packed(uppers, (k, 0), rows).astype(F32)
        grad_upper[:, at] = part * gain[...]
        total = total + jnp.sum(part * upper[:, at].astype(F32), axis=1, keepdims=True)
        grad_down[:, at] = get_packed(downs, (k, 0), rows).astype(F32)
    grad_gain[...] = total


def like(shape, kind=BF16):
    return jax.ShapeDtypeStruct(shape, kind)


def together(*values):
    return lax.optimization_barrier(values)


def after(value, *others):
    return lax.optimization_barrier((value, others))[0]


class Grid:
    def __init__(self):
        self.blocks = lax.axis_size("blk")
        self.ulys = lax.axis_size("uly")
        self.depth = self.blocks // PAIR
        self.b = lax.axis_index("blk")
        self.u = lax.axis_index("uly")
        self.z = self.b // PAIR
        self.x = self.b % PAIR
        self.y = self.u // 2
        self.c = self.u % 2

    def to_z(self, value, step):
        pairs = [
            (z * PAIR + x, ((z + step) % self.depth) * PAIR + x)
            for z in range(self.depth)
            for x in range(PAIR)
        ]
        return lax.ppermute(value, "blk", pairs)

    def swap_x(self, value):
        return lax.ppermute(value, "blk", [(i, i ^ 1) for i in range(self.blocks)])

    def swap_y(self, value):
        return lax.ppermute(value, "uly", [(i, i ^ 2) for i in range(self.ulys)])

    def swap_both(self, value):
        return lax.ppermute(value, "uly", [(i, i ^ 3) for i in range(self.ulys)])

    def swap_core(self, value):
        return lax.ppermute(value, "uly", [(i, i ^ 1) for i in range(self.ulys)])


def paired(bit, mine, other, axis):
    low = jnp.where(bit == 0, mine, other)
    high = jnp.where(bit == 0, other, mine)
    return jnp.stack([low, high], axis=axis)


def pick(bit, array, axis):
    low = lax.index_in_dim(array, 0, axis, keepdims=False)
    high = lax.index_in_dim(array, 1, axis, keepdims=False)
    return jnp.where(bit == 0, low, high), jnp.where(bit == 0, high, low)


def order_z(grid, pieces):
    stacked = jnp.stack(pieces[::-1] + pieces[::-1][:-1])
    start = (grid.depth - 1 - grid.z) % grid.depth
    return lax.dynamic_slice_in_dim(stacked, start, grid.depth, 0)


def gather_uly(grid, value):
    both = paired(grid.y, value, grid.swap_y(value), 0)
    every = paired(grid.c, both, grid.swap_core(both), 1)
    return every.reshape((grid.ulys,) + value.shape)


def scatter_uly(grid, parts, kind=BF16):
    parts = parts.reshape((2, 2) + parts.shape[1:])
    keep, send = pick(grid.c, parts, 1)
    both = keep.astype(F32) + grid.swap_core(send.astype(kind)).astype(F32)
    keep, send = pick(grid.y, both, 0)
    return keep + grid.swap_y(send.astype(kind)).astype(F32)


def gather_blk(grid, value):
    pieces = [value] + [grid.to_z(value, d) for d in range(1, grid.depth)]
    pairs = [paired(grid.x, piece, grid.swap_x(piece), 0) for piece in pieces]
    return order_z(grid, pairs)


def exchange_z(grid, parts):
    pieces = [lax.dynamic_index_in_dim(parts, grid.z, 0, keepdims=False)]
    for d in range(1, grid.depth):
        there = (grid.z + d) % grid.depth
        pieces.append(grid.to_z(lax.dynamic_index_in_dim(parts, there, 0, keepdims=False), d))
    return pieces


def exchange_z_all(grid, parts):
    groups = [[z * PAIR + x for z in range(grid.depth)] for x in range(PAIR)]
    return lax.all_to_all(
        parts, "blk", split_axis=0, concat_axis=0, axis_index_groups=groups, tiled=True
    )


def spread_z(grid, value):
    return exchange_z_all(grid, jnp.broadcast_to(value, (grid.depth, *value.shape)))


def exchange_uly(parts):
    return lax.all_to_all(parts, "uly", split_axis=0, concat_axis=0, tiled=True)


def per_device(
    tokens,
    span_order,
    attn_gain,
    qkv_weight,
    qkv_bias,
    out_weight,
    ffn_gain,
    gate_weight,
    up_weight,
    down_weight,
    cotangent,
):
    grid = Grid()
    local_rows, seqs, model = tokens.shape
    count = local_rows * seqs
    ulys = grid.ulys
    depth = grid.depth
    blocks = grid.blocks
    cycle_rows = local_rows * ulys
    spans = cycle_rows // SPAN
    slots = blocks * spans
    group = HEADS // ulys
    factor = 1.0 / math.sqrt(HEAD_DIM)
    width = group * HEAD_DIM
    columns = width + HEAD_DIM
    shard = qkv_weight.shape[0]
    block_model = shard * ulys
    chunk = math.gcd(slots, 4) * SPAN
    side = HEADS * HEAD_DIM
    place = jnp.stack([grid.z, grid.x, grid.y, grid.c, grid.b, grid.u]).astype(jnp.int32)

    def by_seq(array):
        return jnp.transpose(array, (1, 0, 2)).reshape(count, model)

    def by_row(array):
        return jnp.transpose(array.reshape(seqs, local_rows, model), (1, 0, 2))

    def by_uly(array):
        lead = array.shape[0]
        heads = array[:, :side].reshape(lead, ulys, width)
        kinds = array[:, side:].reshape(lead, 2, KV_HEADS, HEAD_DIM)
        kinds = jnp.transpose(kinds, (0, 2, 1, 3)).reshape(lead, ulys, HEAD_DIM)
        return jnp.transpose(jnp.concatenate([heads, kinds], axis=-1), (1, 0, 2))

    rows = by_seq(tokens).astype(F32)
    unit_one, factor_one = norm_rows(rows)
    unit_own = unit_one.astype(BF16)
    unit_near = grid.swap_y(unit_own)
    gain_one = attn_gain.astype(F32)[:, None]
    scaled = (qkv_weight.astype(F32) * gain_one).astype(BF16)
    heads_share = blocks // ulys
    owned_columns = qkv_bias.shape[0]
    column_start = (grid.b * ulys + grid.u) * owned_columns
    bias_row = lax.dynamic_update_slice(
        jnp.zeros((16, owned_columns * blocks * ulys), BF16),
        jnp.pad(qkv_bias[None], ((0, 15), (0, 0))),
        (0, column_start),
    )
    by_head = by_uly(jnp.concatenate([scaled, bias_row], axis=0))
    by_head = exchange_uly(by_head)
    block_rows = jnp.concatenate(
        [by_head[:, :shard].reshape(block_model, columns), jnp.sum(by_head[:, shard:], axis=0)],
        axis=0,
    )
    qkv_mine = [block_rows] + [grid.to_z(block_rows, d) for d in range(1, depth)]
    first_far = grid.swap_x(block_rows)
    first_arrived = qkv_mine[1]
    *qkv_mine, first_far, unit_near = together(*qkv_mine, first_far, unit_near)

    gain_two = ffn_gain.astype(F32)[:, None]
    hidden_units = gate_weight.shape[1] // depth
    order = sorted(range(1, depth), key=lambda d: (min(d, depth - d), d))
    early, middle, late = order[0], order[1:-1], order[-1]
    split_in = after((gate_weight, up_weight, down_weight), first_arrived)
    split_in = (*split_in[:2], split_in[2].T)
    tile_pieces = call(
        functools.partial(split_tiles_kernel, depth),
        [place],
        [*split_in, gain_two],
        [like((3, *packed(block_model, hidden_units)))] * depth,
        scratch=[pltpu.VMEM((depth, 3, *packed(block_model, hidden_units)), BF16)],
    )
    qkv_far = [first_far] + [grid.swap_x(piece) for piece in qkv_mine[1:]]
    unit_across = grid.swap_core(jnp.stack([unit_own, unit_near]))
    out_first, early_piece = after((out_weight, tile_pieces[early]), *qkv_mine[1:])
    tile_mine = {0: tile_pieces[0], early: grid.to_z(early_piece, early)}
    out_mine = spread_z(grid, out_first)
    tile_far = {0: grid.swap_x(after(tile_pieces[0], qkv_far[1]))}
    *qkv_far, unit_across = together(*qkv_far, unit_across)
    unit_parts = (unit_own, unit_near, unit_across)

    head_rows = grid.b * cycle_rows + jnp.arange(cycle_rows, dtype=jnp.int32)
    places = positions(span_order, head_rows).reshape(seqs, ulys, local_rows)
    places = jnp.transpose(places, (1, 0, 2)).reshape(ulys, count)
    cosine, sine = rope_tables(places)
    units, qkv_part, query, kind = call(
        functools.partial(mix_kernel, depth, group),
        [place],
        [*unit_parts, cosine, sine, *qkv_mine, *qkv_far],
        [
            like((ulys, count, model)),
            like((blocks, block_model, columns)),
            like((ulys, count, width)),
            like((ulys, count, HEAD_DIM)),
        ],
        scratch=[
            pltpu.VMEM((blocks, 16, columns), BF16),
            pltpu.SemaphoreType.DMA((2 * blocks + ulys,)),
        ],
        far=(0, 1, 2, *range(5, 2 * depth + 5)),
    )
    units = units.reshape(ulys * count, model)
    qkv_part = qkv_part.reshape(model, columns)
    kinds = [kind] + [grid.to_z(kind, d) for d in range(1, depth)]
    out_mine, cot_flat = after((out_mine, by_seq(cotangent)), kind)
    out_far = grid.swap_x(out_mine)
    cot_first = cot_flat
    cot_near = grid.swap_y(cot_first)
    *held, late_pair, late_down = after(
        (*[tile_pieces[d] for d in middle], tile_pieces[late][:2], tile_pieces[late][2:]), kinds[1]
    )
    for d, piece in zip(middle, held):
        tile_mine[d] = grid.to_z(after(piece, *kinds[1:]), d)
    out_far, cot_near, tile_mine[early], tile_far[0], *kinds = together(
        out_far, cot_near, tile_mine[early], tile_far[0], *kinds
    )
    late_pair = grid.to_z(after(late_pair, kinds[-1]), late)

    a_own = jnp.stack(kinds)
    a_far = grid.swap_x(a_own)
    b_own = grid.swap_core(a_own)
    out_own, out_near = call(
        sort_rows_kernel,
        [place],
        [out_mine, out_far],
        [like((2, heads_share, shard, model))] * 2,
        scratch=[pltpu.VMEM((blocks, shard, model), BF16)],
    )
    out_near = grid.swap_y(out_near)
    a_far, b_own, out_near, *held = together(
        a_far, b_own, out_near, *[tile_mine[d] for d in middle]
    )
    tile_mine.update(zip(middle, held))

    b_far = grid.swap_core(a_far)
    out_across = grid.swap_core(jnp.stack([out_own[1], out_near[1]]))
    tile_far[early] = grid.swap_x(after(tile_mine[early], a_far))
    b_far, out_across = together(b_far, out_across)

    def over_uly(piece):
        both = jnp.concatenate([piece, grid.swap_y(piece)], axis=0)
        return jnp.concatenate([both, grid.swap_core(both)], axis=0)

    grad_rows = cot_flat.astype(F32)

    scale = factor * LOG2E
    kv_shape = (depth, ulys, seqs, local_rows, HEAD_DIM)
    kv_spec = pl.BlockSpec(
        (depth, ulys, 1, local_rows, HEAD_DIM), lambda s, *unused: (0, 0, s, 0, 0)
    )
    heads_shape = (ulys, seqs, local_rows, width)
    heads_spec = pl.BlockSpec((ulys, 1, local_rows, width), lambda s, *unused: (0, s, 0, 0))
    lse_spec = pl.BlockSpec((1, spans, 1, group * SPAN), lambda s, *unused: (s, 0, 0, 0))
    table_shape = (ulys, seqs, local_rows, HEAD_DIM)
    table_spec = pl.BlockSpec((ulys, 1, local_rows, HEAD_DIM), lambda s, *unused: (0, s, 0, 0))
    sorted_spec = pl.BlockSpec((1, 2, slots * SPAN, HEAD_DIM), lambda s, *unused: (s, 0, 0, 0))
    params = pltpu.CompilerParams(vmem_limit_bytes=VMEM_LIMIT)
    query = query.reshape(heads_shape)
    attended, lse, kv = pl.pallas_call(
        functools.partial(attend_kernel, depth, spans, chunk, group, scale),
        grid_spec=pltpu.PrefetchScalarGridSpec(
            num_scalar_prefetch=2,
            grid=(seqs,),
            in_specs=[heads_spec] + [kv_spec] * 4,
            out_specs=[heads_spec, lse_spec, sorted_spec],
        ),
        out_shape=[
            like(heads_shape),
            like((seqs, spans, 1, group * SPAN), F32),
            like((seqs, 2, slots * SPAN, HEAD_DIM)),
        ],
        compiler_params=params,
        cost_estimate=SMALL,
    )(span_order, place, query, *[part.reshape(kv_shape) for part in (a_own, a_far, b_own, b_far)])
    flat = attended.reshape(ulys, count, width)
    out_own, tile_far[early], late_pair, attended = together(
        out_own, tile_far[early], late_pair, attended
    )
    late_down = grid.to_z(after(late_down, attended), late)
    flat = attended.reshape(ulys, count, width)
    for d in middle:
        tile_far[d] = grid.swap_x(after(tile_mine[d], attended))
    (out_part,) = call(
        place_rows_kernel, [place], [out_own, out_near, out_across], [like((heads_share, ulys, shard, model))]
    )
    out_part = out_part.reshape(width, model)
    keep, send = call(
        functools.partial(project_kernel, False),
        [place],
        [flat, out_part],
        [like((2, count, model), F32), like((2, count, model))],
    )
    got = grid.swap_core(send)
    both = keep + got.astype(F32)
    got = grid.swap_y(both[1].astype(BF16))
    got, late_down, *held = together(got, late_down, *[tile_far[d] for d in middle])
    tile_mine[late] = jnp.concatenate([late_pair, late_down])
    tile_far.update(zip(middle, held))
    tile_far[late] = grid.swap_x(after(tile_mine[late], got))
    hidden = rows + both[0] + got.astype(F32)

    unit_two, factor_two = norm_rows(hidden)
    mid_own = unit_two.astype(BF16)
    mid_near = grid.swap_y(mid_own)
    mid_pieces = [mid_own, grid.to_z(mid_own, 1)]
    cot_pieces = [cot_first, grid.to_z(after(cot_first, mid_near), 1)]
    mid_near, tile_far[late] = together(mid_near, tile_far[late])
    for d in range(2, depth):
        mid_pieces.append(grid.to_z(mid_pieces[-1], 1))
        cot_pieces.append(grid.to_z(cot_pieces[-1], 1))

    def chunk_of(own, near):
        both = jnp.concatenate([own, near], axis=0)
        return jnp.concatenate([both, grid.swap_core(both)], axis=0)

    mid_chunks = [chunk_of(mid_own, mid_near)] + [over_uly(piece) for piece in mid_pieces[1:]]
    cot_chunks = [chunk_of(cot_first, cot_near)] + [over_uly(piece) for piece in cot_pieces[1:]]
    gate_used, upper_used, down_used = [
        tile.reshape(model, hidden_units)
        for tile in call(
            functools.partial(merge_tiles_kernel, depth),
            [place],
            [tile_mine[d] for d in range(depth)] + [tile_far[d] for d in range(depth)],
            [like((blocks, block_model, hidden_units))] * 3,
        )
    ]
    actives, gate_grads, upper_grads, back_chunks = [], [], [], []
    for mid, cot in zip(mid_chunks, cot_chunks):
        gate = matmul(mid, gate_used)
        upper = matmul(mid, upper_used)
        sigmoid = jax.nn.sigmoid(gate)
        active_grad = matmul(cot, down_used)
        actives.append((gate * sigmoid * upper).astype(BF16))
        gate_grad = (active_grad * upper * sigmoid * (1.0 + gate * (1.0 - sigmoid))).astype(BF16)
        upper_grad = (active_grad * gate * sigmoid).astype(BF16)
        gate_grads.append(gate_grad)
        upper_grads.append(upper_grad)
        back_chunks.append(
            contract_cols(gate_grad, gate_used) + contract_cols(upper_grad, upper_used)
        )
    def over_core(chunk):
        chunk = chunk.reshape(2, 2, count, model)
        return chunk[0].astype(F32) + grid.swap_core(chunk[1].astype(BF16)).astype(F32)

    def over_y(both):
        return both[0] + grid.swap_y(both[1].astype(BF16)).astype(F32)

    def halve(shares, rows):
        shape = (depth, PAIR, *rows, shares[0].shape[-1])
        shares = [share.astype(BF16).reshape(shape) for share in shares]
        half = like((depth, len(shares), *rows, shape[-1]))
        return call(choose_kernel, [place], shares, [half] * 2)

    def weight_grad(rows, grads):
        half = like((depth, 1, *packed(block_model, hidden_units)))
        return call(
            functools.partial(weight_grad_kernel, depth),
            [place],
            [*rows, *grads],
            [half] * 2,
            scratch=[pltpu.VMEM((model, hidden_units), F32)],
            single=depth > 4,
        )

    def fold(keep, got):
        return exchange_z_all(grid, (keep.astype(F32) + got.astype(F32)).astype(BF16))

    z_groups = [[z * PAIR + x for z in range(depth)] for x in range(PAIR)]
    boths = [over_core(chunk) for chunk in back_chunks]
    mid_parts = [over_y(both) for both in boths]
    back_pieces = [grid.to_z(mid_parts[d].astype(BF16), -d) for d in range(1, depth)]
    mid_all = tuple(mid_chunks)
    mid_now = after(mid_all, back_chunks[-1], *boths[:-1], *mid_parts[:-1])
    gate_keep, gate_send = weight_grad(mid_now, gate_grads)
    mid_now = after(mid_all, gate_send, *mid_parts, back_pieces[0])
    upper_keep, upper_send = weight_grad(mid_now, upper_grads)
    gate_got = grid.swap_x(gate_send)
    first, upper_send, *back_pieces = together(mid_parts[0], upper_send, *back_pieces)
    mid_grad = first + sum(piece.astype(F32) for piece in back_pieces)

    hidden_grad = grad_rows + norm_back(mid_grad, unit_two, factor_two)
    branch_own = hidden_grad.astype(BF16)
    branch_near = grid.swap_y(branch_own)
    upper_got = grid.swap_x(after(upper_send, gate_got))
    gate_owned = fold(*after((gate_keep, gate_got), branch_own))
    down_keep, down_send = weight_grad(after(tuple(cot_chunks), branch_own), actives)
    down_send, branch_near, upper_got = together(down_send, branch_near, upper_got)
    down_got = grid.swap_x(down_send)
    branch_across = grid.swap_core(jnp.stack([branch_own, branch_near]))
    branch_parts = (branch_own, branch_near, branch_across)
    (grad_heads,) = call(
        heads_grad_kernel, [place], [*branch_parts, out_part], [like((ulys, count, width))]
    )

    grad_heads, gate_owned = together(grad_heads.reshape(heads_shape), gate_owned)
    upper_owned = fold(*after((upper_keep, upper_got), gate_owned))
    both_spec = pl.BlockSpec(
        (2, depth, ulys, 1, local_rows, HEAD_DIM), lambda s, *unused: (0, 0, 0, s, 0, 0)
    )
    query_grad, keep_own, keep_far, send_both = pl.pallas_call(
        functools.partial(attend_back_kernel, depth, spans, chunk, group, scale, factor),
        grid_spec=pltpu.PrefetchScalarGridSpec(
            num_scalar_prefetch=2,
            grid=(seqs,),
            in_specs=[heads_spec, sorted_spec]
            + [heads_spec] * 2
            + [lse_spec]
            + [table_spec] * 2,
            out_specs=[heads_spec] + [kv_spec] * 2 + [both_spec],
            scratch_shapes=[pltpu.VMEM((2, slots * SPAN, HEAD_DIM), F32)],
        ),
        out_shape=[like(heads_shape)] + [like(kv_shape)] * 2 + [like((2, *kv_shape))],
        compiler_params=params,
        cost_estimate=SMALL,
    )(
        span_order,
        place,
        query,
        kv,
        grad_heads,
        attended,
        lse,
        cosine.reshape(table_shape),
        sine.reshape(table_shape),
    )
    got_far, got_own = [
        jnp.concatenate([grid.swap_core(part) for part in jnp.split(send_both[k], 2, axis=0)])
        for k in (1, 0)
    ]
    query_grad = query_grad.reshape(ulys * count, width)
    got_far, got_own, query_grad, upper_owned = together(
        got_far, got_own, query_grad, upper_owned
    )
    (out_all,) = call(
        functools.partial(down_kernel, depth),
        [place],
        [*after(tuple(actives), got_far), down_used],
        [like((ulys, depth, count, model))],
    )
    from_x = grid.swap_x((keep_far.astype(F32) + got_far.astype(F32)).astype(BF16))
    share_parts = after(branch_parts, got_far)
    (out_share,) = call(out_share_kernel, [place], [*share_parts, flat], [like((width, model))])
    out_own, out_near = call(
        pick_uly_kernel,
        [place],
        [out_share.reshape(heads_share, ulys, shard, model)],
        [like((2, heads_share, shard, model))] * 2,
    )
    head_keep, head_send = halve([contract_rows(units, query_grad)], (ulys, shard))
    from_x, head_send, out_near, out_all, down_got = together(
        from_x, head_send, out_near, out_all, down_got
    )
    out_all = lax.psum_scatter(out_all, "uly", scatter_dimension=0, tiled=False)
    kind_parts = keep_own.astype(F32) + got_own.astype(F32) + from_x.astype(F32)
    kind_parts = kind_parts.astype(BF16)
    kind_back = [grid.to_z(kind_parts[d], -d) for d in range(1, depth)]
    head_got = grid.swap_x(head_send)
    out_near = grid.swap_y(out_near)
    *kind_back, out_near, kind_parts, head_got = together(
        *kind_back, out_near, kind_parts, head_got
    )
    out_across = grid.swap_core(jnp.stack([out_own[1], out_near[1]]))
    kind_grad = kind_parts[0].astype(F32)
    for piece in kind_back:
        kind_grad = kind_grad + piece.astype(F32)
    kind_grad = kind_grad.reshape(ulys * count, HEAD_DIM)
    turned = jnp.roll(kind_grad, HEAD_DIM // 2, axis=1)
    is_key = grid.c == 0
    flat_cosine = cosine.reshape(ulys * count, HEAD_DIM)
    flat_sine = sine.reshape(ulys * count, HEAD_DIM)
    kind_grad = jnp.where(is_key, kind_grad * flat_cosine - turned * flat_sine, kind_grad)
    kind_grad = kind_grad.astype(BF16)

    bias = jnp.sum(query_grad.astype(F32), axis=0).reshape(group, HEAD_DIM)
    bias = jnp.concatenate([bias, jnp.sum(kind_grad.astype(F32), axis=0)[None]], axis=0)
    bias = jnp.pad(bias.astype(BF16), ((0, 16 - group - 1), (0, 0)))
    bias = jnp.broadcast_to(bias, (blocks, ulys, 16, HEAD_DIM))
    share = contract_rows(units, kind_grad).astype(BF16)
    share = share.reshape(blocks, ulys, shard, HEAD_DIM)
    share = jnp.concatenate([bias, share], axis=2)
    kind_keep, kind_send = halve([share], (ulys, shard + 16))
    kind_got = grid.swap_x(kind_send)
    out_all = lax.psum_scatter(
        after(out_all, kind_send), "blk", scatter_dimension=0, axis_index_groups=z_groups, tiled=False
    )
    head_pieces = fold(*after((head_keep, head_got), kind_send))
    out_across = after(out_across, kind_send)
    out_keep, out_send = call(
        group_rows_kernel,
        [place],
        [out_own, out_near, out_across],
        [like((depth, 1, shard, model))] * 2,
        scratch=[pltpu.VMEM((blocks, shard, model), BF16)],
    )
    out_got = grid.swap_x(after(out_send, kind_got))
    kind_pieces = call(
        functools.partial(fold_kernel, depth),
        [place],
        [kind_keep, kind_got],
        [like(kind_keep.shape[1:])] * depth,
    )
    kind_pieces = [kind_pieces[0]] + [grid.to_z(kind_pieces[d], d) for d in range(1, depth)]
    kind_pieces = jnp.stack(kind_pieces)
    kind_pieces, out_got = together(kind_pieces, out_got)
    kind_now = after(kind_grad, kind_pieces)
    keep, send = call(
        functools.partial(project_kernel, True),
        [place],
        [
            query_grad.reshape(ulys, count, width),
            kind_now.reshape(ulys, count, HEAD_DIM),
            qkv_part,
        ],
        [like((2, count, model), F32), like((2, count, model))],
    )
    both = keep + grid.swap_core(send).astype(F32)
    down_owned = fold(*after((down_keep, down_got), head_pieces))
    out_pieces = call(
        functools.partial(fold_kernel, depth),
        [place],
        [out_keep, out_got],
        [like(out_keep.shape[1:])] * depth,
    )
    out_pieces = [out_pieces[0]] + [grid.to_z(out_pieces[d], d) for d in range(1, depth)]

    def to_owners(pieces):
        own, near = call(
            split_uly_kernel, [place], [pieces], [like((2, *pieces.shape[3:]))] * 2
        )
        near = grid.swap_y(near)
        return own, near, grid.swap_core(jnp.stack([own[1], near[1]]))

    head_owned = to_owners(head_pieces)
    kind_owned = to_owners(kind_pieces)
    grad_qkv, grad_gain_one, bias = call(
        finish_qkv_kernel,
        [place],
        [*head_owned, *kind_owned, qkv_weight, gain_one],
        [
            like(qkv_weight.shape, F32),
            like((shard, 1), F32),
            like((ulys, 16, HEAD_DIM), F32),
        ],
        scratch=[
            pltpu.VMEM((ulys, shard, width), BF16),
            pltpu.VMEM((ulys, shard + 16, HEAD_DIM), BF16),
        ],
    )
    grad_gain_one = grad_gain_one[:, 0]
    kind_bias = bias[:, group].reshape(KV_HEADS, 2, HEAD_DIM)
    bias = jnp.concatenate(
        [bias[:, :group].reshape(-1), jnp.transpose(kind_bias, (1, 0, 2)).reshape(-1)]
    )
    grad_bias = lax.dynamic_slice_in_dim(bias, column_start, owned_columns, 0)
    grad_out = sum(piece[0].astype(F32) for piece in out_pieces)
    result = hidden + after(out_all, grad_qkv).astype(F32)
    output = by_row(result.astype(BF16))
    normed_grad = both[0] + grid.swap_y(both[1].astype(BF16)).astype(F32)
    grad_tokens = by_row(hidden_grad + norm_back(normed_grad, unit_one, factor_one))
    tile_shape = gate_weight.shape
    grad_gate, grad_upper, grad_down, gain_part = call(
        functools.partial(finish_kernel, depth),
        [],
        [gate_owned, upper_owned, after(down_owned, grad_qkv), gate_weight, up_weight, gain_two],
        [like(tile_shape, F32)] * 3 + [like((block_model, 1), F32)],
    )
    grad_down = grad_down.T
    grad_gain_two = scatter_uly(grid, gain_part.reshape(ulys, -1), F32)
    return (
        output,
        grad_tokens,
        grad_gain_one,
        grad_qkv,
        grad_bias,
        grad_out,
        grad_gain_two.reshape(-1),
        grad_gate,
        grad_upper,
        grad_down,
    )


def solution(mesh):
    in_specs = (
        P(("blk", "uly"), None, None),
        P(),
        P(("blk", "uly")),
        P(("blk", "uly"), None),
        P(("blk", "uly")),
        P(("blk", "uly"), None),
        P("blk"),
        P("blk", "uly"),
        P("blk", "uly"),
        P("uly", "blk"),
        P(("blk", "uly"), None, None),
    )
    out_specs = (
        P(("blk", "uly"), None, None),
        P(("blk", "uly"), None, None),
        P(("blk", "uly")),
        P(("blk", "uly"), None),
        P(("blk", "uly")),
        P(("blk", "uly"), None),
        P(("blk", "uly")),
        P("blk", "uly"),
        P("blk", "uly"),
        P("uly", "blk"),
    )
    return jax.shard_map(
        per_device, mesh=mesh, in_specs=in_specs, out_specs=out_specs, check_vma=False
    )
```
